128 devices in a mesh: row: 16 (over y_hi, x, core), col: 8 (over y_lo, z).
Axes of the slice: x: 4, y: 4 (y_hi: 2, y_lo: 2; y = y_hi * 2 + y_lo), z: 4, core: 2. Of those that a mesh axis runs over, the one named last changes fastest.
Arguments:
- mode_block: float32 [131072, 256], P(('row', 'col')), may hold values from -80 to 80
- k_blocks: float32 [1024, 3, 128, 128], P(('row', 'col')), may hold values from -1 to 9
- block_cols: int32 [1024, 3], P(('row', 'col')), may hold values from 0 to 1023, as said below
- panel_node: int32 [16384], replicated, may hold values from 0 to 131071, as said below
- added_mass: bfloat16 [16384, 16384], P('row', 'col'), may hold values from -0.0625 to 0.0625
- low_edge: int32 [256], replicated, may hold values from 4 to 8
- high_edge: int32 [256], replicated, may hold values from 40 to 56
Outputs:
- filtered: float32 [131072, 256], P(('row', 'col'))
The draws below stay inside these ranges and needn't reach their ends.
Inputs may be any that keep to these rules, and one draw needn't show every extreme that they name: `panel_node`: distinct shell rows. Cut the panels into 128 aligned blocks of 128; in each block at most 2 panels lie on the 1024 rows of one shell device (rows d * 1024 to (d + 1) * 1024 - 1), exactly 2 for some device, and the panels of a block on one device are consecutive. `block_cols`: row i holds i first, then two different block rows among i - 2 to i + 2 other than i.
All inputs are finite; a program needn't handle non-finite values.
Results may differ from the reference program's by a relative error of at most 0.0015.
Values may be sent and summed in bfloat16 or wider, within the bound.
No kernel may reach another device: no remote copies, remote signals or barrier semaphores. Data moves between devices by JAX's collectives and lax.ppermute only.
A program may use at most 64 MiB of HBM per device.

```python
import jax
import jax.numpy as jnp
from jax import lax

NB = 256
BLK = 128
KB = 3
DEGREE = 3
OUTER = 2
ROWS_DEV = 1024
PB = 128
NS = 131072
NP = 16384
DEVICES = 128


def wet_layout(key):
    hull_key, swap_key, spot_key, perm_key = jax.random.split(key, 4)
    spread = (PB + DEVICES - 1) // DEVICES
    capacity = 2 * spread
    heavy_count = max(1, PB // (4 * spread))
    boundary = heavy_count * capacity
    within = jnp.arange(PB)
    position = jnp.where(within < boundary, within // capacity, heavy_count + (within - boundary) // spread)
    offset = jnp.where(within < boundary, within % capacity, (within - boundary) % spread)
    hull_order = jax.random.permutation(hull_key, DEVICES)
    device_order = jnp.tile(hull_order[None, :], (DEVICES, 1))
    heavy_spot = jax.random.randint(swap_key, (DEVICES,), 0, heavy_count)
    second = jax.random.randint(spot_key, (DEVICES,), 0, DEVICES)
    blocks = jnp.arange(DEVICES)
    heavy_value = device_order[blocks, heavy_spot]
    second_value = device_order[blocks, second]
    device_order = device_order.at[blocks, heavy_spot].set(second_value)
    device_order = device_order.at[blocks, second].set(heavy_value)
    source = device_order[:, position]
    counts = jnp.sum((source[:, :, None] == jnp.arange(DEVICES)[None, None, :]).astype(jnp.int32), axis=1)
    before = jnp.cumsum(counts, axis=0) - counts
    base_rank = jnp.take_along_axis(before, source, axis=1)
    rank_on_device = base_rank + offset[None, :]
    row_perms = jax.vmap(lambda sub_key: jax.random.permutation(sub_key, ROWS_DEV))(jax.random.split(perm_key, DEVICES))
    row_pick = row_perms[source, rank_on_device]
    return (source * ROWS_DEV + row_pick).reshape(-1).astype(jnp.int32)


def draw_panel_node(key, part):
    return wet_layout(jax.random.fold_in(key, 7))


def draw_block_cols(key, part):
    block_total = NS // BLK
    index_rows = jnp.arange(block_total)
    offsets = jnp.array([-2, -1, 1, 2], dtype=jnp.int32)
    candidate = index_rows[:, None] + offsets[None, :]
    valid = (candidate >= 0) & (candidate < block_total)
    scores = jax.random.randint(key, (block_total, 4), 0, 1000) * 4 + jnp.arange(4)[None, :]
    scores = jnp.where(valid, scores, 100000)
    top_values, picked = lax.top_k(-scores, 2)
    chosen = jnp.take_along_axis(candidate, picked, axis=1)
    return jnp.concatenate([index_rows[:, None], chosen], axis=1).astype(jnp.int32)


def draw_k_blocks(key, part):
    noise_key, diag_key = jax.random.split(key, 2)
    block_shape = (NS // BLK, KB, BLK, BLK)
    values = jnp.clip(jax.random.normal(noise_key, block_shape, jnp.float32), -6.0, 6.0)
    values = values * (KB * BLK) ** (-0.5)
    diagonal = jnp.exp(jax.random.uniform(diag_key, (NS // BLK, BLK), jnp.float32, jnp.log(2.0), jnp.log(8.0)))
    identity = jnp.eye(BLK, dtype=jnp.float32)
    return values.at[:, 0].add(diagonal[:, :, None] * identity[None, :, :])


def draw_mode_block(key, part):
    base_key, row_key, col_key = jax.random.split(key, 3)
    base = jnp.clip(jax.random.normal(base_key, (NS, NB), jnp.float32), -6.0, 6.0)
    ramp = jnp.exp(jnp.log(3.0) * jnp.arange(NS).astype(jnp.float32) / NS)[:, None]
    row_scale = jnp.exp(jax.random.uniform(row_key, (NS, 1), jnp.float32, 0.0, jnp.log(10.0))) * ramp
    col_scale = jnp.exp(jax.random.uniform(col_key, (1, NB), jnp.float32, 0.0, jnp.log(10.0)))
    return base * row_scale * col_scale / 30.0


def place_ends(values, key, smallest, largest):
    spot = [jax.random.randint(jax.random.fold_in(key, axis), (), 0, length) for axis, length in enumerate(values.shape)]
    longest = values.shape.index(max(values.shape))
    neighbour = spot[:longest] + [(spot[longest] + 1) % values.shape[longest]] + spot[longest + 1:]
    return values.at[tuple(spot)].set(smallest).at[tuple(neighbour)].set(largest)


def strengthened(result, stream_key, source, target, blocks, factor):
    def block_of(axis_at):
        return (jnp.arange(result.shape[axis_at]) // (result.shape[axis_at] // blocks)).reshape((-1,) + (1,) * (result.ndim - 1 - axis_at))

    one_side = jax.random.permutation(stream_key, blocks)[block_of(target)]
    far = (block_of(target) + blocks // 2) % blocks
    return jnp.where((block_of(source) == one_side) | (block_of(source) == far), factor * result, result)


def level_of(own_key, shape, pieces, least, largest):
    factor_of, own = 1.0, jax.random.fold_in(own_key, 6)
    for dim, blocks in pieces:
        draws = jnp.exp(jax.random.uniform(jax.random.fold_in(own, dim), (blocks,), jnp.float32, least / len(pieces), largest / len(pieces)))
        factor_of = factor_of * jnp.repeat(draws, shape[dim] // blocks).reshape([-1 if axis == dim else 1 for axis in range(len(shape))])
    return factor_of


def bell_draw_with(stream_key, shape, deviation, most, pieces, heavy, kind=jnp.bfloat16):
    values = deviation * jax.random.normal(stream_key, shape, jnp.float32)
    if pieces:
        values = values * level_of(stream_key, shape, pieces, -0.22, 0.18)
    return jnp.clip(strengthened(values, jax.random.fold_in(stream_key, 3), *heavy), -most, most).astype(kind)


def setup_inputs(seed: int = 0) -> dict:
    seeds = jax.random.split(jax.random.key(seed), 8)
    return {
        "mode_block": draw_mode_block(jax.random.fold_in(seeds[7], 71), 0),
        "k_blocks": draw_k_blocks(jax.random.fold_in(seeds[7], 71), 0),
        "block_cols": draw_block_cols(jax.random.fold_in(seeds[7], 71), 0),
        "panel_node": draw_panel_node(jax.random.fold_in(seeds[7], 71), 0),
        "added_mass": bell_draw_with(seeds[4], (NP, NP), NP ** -0.5, 0.0625, ((0, 16), (1, 8)), (1, 0, 16, 2.0)),
        "low_edge": place_ends(jax.random.randint(seeds[5], (NB,), 4, 9), jax.random.fold_in(seeds[5], 1), 4, 8).astype(jnp.int32),
        "high_edge": place_ends(jax.random.randint(seeds[6], (NB,), 40, 57), jax.random.fold_in(seeds[6], 1), 40, 56).astype(jnp.int32),
    }


def stiffness(vectors, k_blocks, block_cols):
    row_total = k_blocks.shape[0]
    block_size = k_blocks.shape[2]
    blocked = vectors.reshape(row_total, block_size, vectors.shape[1])

    def one_row(paired):
        values, columns = paired
        chosen = blocked[columns]
        return jnp.einsum('kij,kjn->in', values, chosen, precision=lax.Precision.HIGHEST)
    return lax.map(one_row, (k_blocks, block_cols)).reshape(vectors.shape)

def operate(vectors, k_blocks, block_cols, panel_node, added_mass):
    wetted = vectors[panel_node].astype(jnp.bfloat16)
    pressure = jnp.dot(added_mass, wetted, preferred_element_type=jnp.float32)
    loads = jnp.zeros_like(vectors).at[panel_node].set(pressure)
    return stiffness(vectors, k_blocks, block_cols) + loads

def reference(mode_block, k_blocks, block_cols, panel_node, added_mass, low_edge, high_edge):
    lower = low_edge.astype(jnp.float32) * 0.25
    upper = high_edge.astype(jnp.float32) * 0.25
    centre = 0.5 * (upper + lower)
    radius = 0.5 * (upper - lower)
    current = mode_block
    for outer_no in range(OUTER):
        previous = current
        image = operate(current, k_blocks, block_cols, panel_node, added_mass)
        current = (image - centre * current) / radius
        for degree_no in range(DEGREE - 1):
            image = operate(current, k_blocks, block_cols, panel_node, added_mass)
            following = 2.0 * (image - centre * current) / radius - previous
            previous = current
            current = following
        squares = lax.optimization_barrier(jnp.sum(current * current, axis=0))
        current = current / jnp.sqrt(squares / NS + 1e-06)
    return current
```

```python
import functools

import jax
import jax.numpy as jnp
from jax import lax
from jax.experimental import pallas as pl
from jax.experimental.pallas import tpu as pltpu
from jax.sharding import PartitionSpec as P

DEGREE = 3
OUTER = 2
F32 = jnp.float32
BF16 = jnp.bfloat16
HIGHEST = lax.Precision.HIGHEST


def stiff_kernel(cols, k_hi, k_lo, low, here, high, prev, scale, shift, out, p_hi, p_lo):
    halo = low.shape[0]
    rows = here.shape[0]
    size = k_hi.shape[1]

    def split(value, at):
        hi = value.astype(BF16)
        p_hi[at, :] = hi
        p_lo[at, :] = (value - hi.astype(F32)).astype(BF16)

    split(low[...], pl.ds(0, halo))
    split(here[...], pl.ds(halo, rows))
    split(high[...], pl.ds(halo + rows, halo))
    for i in range(rows // size):
        acc = jnp.zeros((size, here.shape[1]), F32)
        for k in range(k_hi.shape[2] // size):
            at = pl.ds(pl.multiple_of(cols[i, k] * size, size), size)
            kh = k_hi[i, :, k * size : (k + 1) * size]
            kl = k_lo[i, :, k * size : (k + 1) * size]
            vh = p_hi[at, :]
            vl = p_lo[at, :]
            acc += jnp.dot(kh, vh, preferred_element_type=F32)
            acc += jnp.dot(kh, vl, preferred_element_type=F32)
            acc += jnp.dot(kl, vh, preferred_element_type=F32)
        mine = pl.ds(i * size, size)
        out[mine, :] = scale[...] * acc + shift[...] * here[mine, :] - prev[mine, :]


def stiff(cols, k_hi, k_lo, low, here, high, prev, scale, shift):
    rows, width = here.shape
    halo = low.shape[0]
    vmem = pl.BlockSpec(memory_space=pltpu.VMEM)
    return pl.pallas_call(
        stiff_kernel,
        out_shape=jax.ShapeDtypeStruct((rows, width), F32),
        in_specs=[pl.BlockSpec(memory_space=pltpu.SMEM)] + [vmem] * 8,
        out_specs=vmem,
        scratch_shapes=[pltpu.VMEM((rows + 2 * halo, width), BF16)] * 2,
        compiler_params=pltpu.CompilerParams(vmem_limit_bytes=24 * 2**20),
        cost_estimate=pl.CostEstimate(
            flops=18 * rows * 384 * width, bytes_accessed=6 * 2**20, transcendentals=0
        ),
        name="stiff",
    )(cols, k_hi, k_lo, low, here, high, prev, scale, shift)


def body(mode_block, k_blocks, block_cols, panel_node, added_mass, low_edge, high_edge):
    n_row = lax.axis_size("row")
    n_col = lax.axis_size("col")
    devices = n_row * n_col
    my_row = lax.axis_index("row")
    my_col = lax.axis_index("col")
    linear = my_row * n_col + my_col
    core = my_row % 2
    rows_dev, width = mode_block.shape
    size = k_blocks.shape[2]
    blocks_dev = rows_dev // size
    per_block = panel_node.shape[0] // devices
    slots = 2 * devices
    both = ("row", "col")

    panel_rows = panel_node.reshape(devices, per_block)
    source = panel_rows // rows_dev
    before = jnp.concatenate([jnp.full((devices, 1), -1, source.dtype), source[:, :-1]], axis=1)
    rank = (source == before).astype(jnp.int32)
    owned = source == linear
    local = panel_rows - linear * rows_dev
    first = jnp.max(jnp.where(owned & (rank == 0), local, -1), axis=1)
    second = jnp.max(jnp.where(owned & (rank == 1), local, -1), axis=1)
    by_block = jnp.stack([first, second], axis=1)
    by_target = by_block.reshape(n_col, n_row, 2).transpose(1, 0, 2)
    shell_rows = jnp.arange(rows_dev, dtype=jnp.int32)
    pick = (by_target.reshape(slots, 1) == shell_rows[None, :]).astype(BF16)
    place = (shell_rows[:, None] == by_block.reshape(1, slots)).astype(BF16)
    flat = 2 * source + rank
    slot_ids = jnp.arange(slots, dtype=jnp.int32)
    in_flat = lax.dynamic_index_in_dim(flat, my_col * n_row + my_row, 0, keepdims=False)
    out_flat = lax.dynamic_index_in_dim(flat, linear, 0, keepdims=False)
    gather_in = (in_flat[:, None] == slot_ids[None, :]).astype(BF16)
    spread_out = (slot_ids[:, None] == out_flat[None, :]).astype(BF16)

    mass = added_mass.reshape(added_mass.shape[0], n_row // 2, 2, per_block)
    mass_same = lax.dynamic_index_in_dim(mass, core, 2, keepdims=False).reshape(added_mass.shape[0], -1)
    mass_other = lax.dynamic_index_in_dim(mass, 1 - core, 2, keepdims=False).reshape(added_mass.shape[0], -1)

    cols = block_cols - (linear * blocks_dev - 2)
    k_rows = k_blocks.transpose(0, 2, 1, 3).reshape(blocks_dev, size, -1)
    k_top = lax.reduce_precision(k_rows, 8, 7)
    k_hi = k_top.astype(BF16)
    k_lo = (k_rows - k_top).astype(BF16)

    same_core = [[i for i in range(n_row) if i % 2 == c] for c in range(2)]
    swap_core = [(i, i ^ 1) for i in range(n_row)]
    forward = [(i, i + 1) for i in range(devices - 1)]
    backward = [(i + 1, i) for i in range(devices - 1)]
    to_in = [(b, (b % n_row) * n_col + b // n_row) for b in range(devices)]

    def choose(matrix, value):
        return jnp.dot(matrix.astype(F32), value, precision=HIGHEST)

    def exchange(message):
        return lax.all_to_all(message, both, split_axis=0, concat_axis=0, tiled=True)

    def pressure_of(wetted):
        n_same = n_row // 2
        sent = jnp.broadcast_to(wetted[None], (n_same,) + wetted.shape)
        same = lax.all_to_all(
            sent, "row", split_axis=0, concat_axis=0, tiled=True, axis_index_groups=same_core
        ).reshape(n_same * per_block, width)
        other = lax.ppermute(same, "row", swap_core)
        partial = jnp.dot(mass_same, same, preferred_element_type=F32)
        partial = partial + jnp.dot(mass_other, other, preferred_element_type=F32)
        parts = lax.all_to_all(
            partial.reshape(n_col, per_block, width), "col", split_axis=0, concat_axis=0, tiled=True
        )
        return jnp.sum(parts, axis=0)

    def dry_part(current, previous, scale, shift):
        low = lax.ppermute(current[rows_dev - 2 * size :], both, forward)
        high = lax.ppermute(current[: 2 * size], both, backward)
        return stiff(cols, k_hi, k_lo, low, current, high, previous, scale, shift)

    lower = low_edge.astype(F32) * 0.25
    upper = high_edge.astype(F32) * 0.25
    centre = (0.5 * (upper + lower))[None, :]
    radius = (0.5 * (upper - lower))[None, :]
    total_rows = rows_dev * devices

    current = mode_block
    previous = jnp.zeros_like(current)
    first_send = choose(pick, current).astype(BF16).reshape(devices, 2, width)
    wetted = jnp.dot(
        gather_in, exchange(first_send).reshape(slots, width), preferred_element_type=F32
    ).astype(BF16)
    for outer_no in range(OUTER):
        for degree_no in range(DEGREE):
            step = 1.0 if degree_no == 0 else 2.0
            last = outer_no == OUTER - 1 and degree_no == DEGREE - 1
            rescale = outer_no > 0 and degree_no == 0
            gain = step / radius
            zero = jnp.zeros_like(current)
            dry = dry_part(current, zero if degree_no == 0 else previous, gain, -centre * gain)
            load = gain * pressure_of(wetted)
            load_in = None if last else lax.ppermute(load, both, to_in)
            load_slots = choose(spread_out, load).reshape(devices, 2, width)
            rows = [load_slots]
            if not last:
                rows.append(choose(pick, dry).reshape(devices, 2, width))
            if rescale:
                squares = jnp.sum(current * current, axis=0)
                rows.append(jnp.broadcast_to(squares[None, None, :], (devices, 1, width)))
            got = exchange(jnp.concatenate(rows, axis=1))
            if rescale:
                squares = jnp.sum(got[:, 4, :], axis=0, keepdims=True)
                factor = 1.0 / jnp.sqrt(squares / total_rows + 1e-06)
            else:
                factor = None
            if not last:
                wet = choose(gather_in, got[:, 2:4].reshape(slots, width)) + load_in
                if rescale:
                    wet = wet * factor
                wetted = wet.astype(BF16)
            following = dry + choose(place, got[:, 0:2].reshape(slots, width))
            if rescale:
                following = following * factor
                current = current * factor
            previous = current
            current = following
    squares = jnp.sum(current * current, axis=0)
    squares = exchange(jnp.broadcast_to(squares[None, None, :], (devices, 1, width)))
    squares = jnp.sum(squares, axis=0)
    return current / jnp.sqrt(squares / total_rows + 1e-06)


def solution(mesh):
    placed = (
        P(("row", "col"), None),
        P(("row", "col"), None, None, None),
        P(("row", "col"), None),
        P(),
        P("row", "col"),
        P(),
        P(),
    )
    return jax.shard_map(
        body, mesh=mesh, in_specs=placed, out_specs=P(("row", "col"), None), check_vma=False
    )
```

```python
import jax
import jax.numpy as jnp
from jax import lax
from jax.experimental import pallas as pl
from jax.experimental.pallas import tpu as pltpu
from jax.sharding import PartitionSpec as P

SF = 40
DF = 1
DEGREE = 3
OUTER = 2
F32 = jnp.float32
BF16 = jnp.bfloat16
LANES = 128
VMEM = pl.BlockSpec(memory_space=pltpu.VMEM)
ANY = pl.BlockSpec(memory_space=pl.ANY)
SMEM = pl.BlockSpec(memory_space=pltpu.SMEM)


def two_parts(value):
    hi = value.astype(BF16)
    return hi, (value - hi.astype(F32)).astype(BF16)


def choose(matrix, value):
    hi, lo = two_parts(value)
    picked = jnp.dot(matrix, hi, preferred_element_type=F32)
    return picked + jnp.dot(matrix, lo, preferred_element_type=F32)


def call(kernel, name, out_shape, in_specs, flops, moved, scratch=(), limit=8):
    return pl.pallas_call(
        kernel,
        out_shape=out_shape,
        in_specs=in_specs,
        out_specs=jax.tree.map(lambda _: VMEM, out_shape),
        scratch_shapes=list(scratch),
        compiler_params=pltpu.CompilerParams(vmem_limit_bytes=limit * 2**20),
        cost_estimate=pl.CostEstimate(flops=flops, bytes_accessed=moved, transcendentals=0),
        name=name,
    )


def stiff_kernel(cols, k, low, here, high, prev, scale, shift, *rest):
    if len(rest) == 5:
        pick, out, wet, p_hi, p_lo = rest
    else:
        (out, p_hi, p_lo), pick, wet = rest, None, None
    halo = low.shape[0]
    rows = here.shape[0]
    size = k.shape[2]

    def put(value, start, count):
        hi, lo = two_parts(value)
        p_hi[start : start + count, :] = hi
        p_lo[start : start + count, :] = lo

    put(low[...], 0, halo)
    put(here[...], halo, rows)
    put(high[...], halo + rows, halo)
    for i in range(rows // size):
        acc = jnp.zeros((size, here.shape[1]), F32)
        for j in range(k.shape[1]):
            at = pl.ds(pl.multiple_of(cols[i, j] * size, size), size)
            kh, kl = two_parts(k[i, j])
            vh = p_hi[at, :]
            vl = p_lo[at, :]
            acc += jnp.dot(kh, vh, preferred_element_type=F32)
            acc += jnp.dot(kh, vl, preferred_element_type=F32)
            acc += jnp.dot(kl, vh, preferred_element_type=F32)
        mine = pl.ds(i * size, size)
        out[mine, :] = scale[...] * acc + shift[...] * here[mine, :] - prev[mine, :]
    if wet is not None:
        wet[...] = choose(pick[...], out[...])


def pack_kernel(parts, gain, spread, *rest):
    if len(rest) == 3:
        wet, load, message = rest
    else:
        (message,), wet, load = rest, None, None
    total = parts[0]
    for i in range(1, parts.shape[0]):
        total = total + parts[i]
    total = total * gain[...]
    if load is not None:
        load[...] = total
    sent = choose(spread[...], total)
    devices = sent.shape[0] // 2
    rows = message.shape[0] // devices
    for s in range(2):
        for h in range(2):
            piece = pl.ds(h * LANES, LANES)
            message[pl.ds(4 * h + s, devices, stride=rows), :] = sent[
                s * devices : (s + 1) * devices, h * LANES : (h + 1) * LANES
            ]
            if wet is not None:
                message[pl.ds(4 * h + 2 + s, devices, stride=rows), :] = wet[
                    pl.ds(s * devices, devices), piece
                ]


def slot_rows(got, devices, first):
    rows = got.shape[0] // devices

    def one(s):
        halves = [got[pl.ds(4 * h + first + s, devices, stride=rows), :] for h in range(2)]
        return jnp.concatenate(halves, axis=1)

    return jnp.concatenate([one(0), one(1)], axis=0)


def meet_kernel(got, dry, place, factor, *rest):
    if len(rest) == 6:
        load, gather, sent, out, head, tail = rest
    else:
        (out,), load, gather, sent = rest, None, None, None
    devices = place.shape[1] // 2
    if sent is not None:
        value = choose(gather[...], slot_rows(got, devices, 2)) + load[...]
        value = (value * factor[...]).astype(BF16)
        for i in range(sent.shape[0]):
            sent[i] = value
    value = (dry[...] + choose(place[...], slot_rows(got, devices, 0))) * factor[...]
    out[...] = value
    if sent is not None:
        head[...] = value[: head.shape[0]]
        tail[...] = value[value.shape[0] - tail.shape[0] :]


def dot_kernel(core, mass, same, other, out, panels):
    count, depth, _ = same.shape

    @pl.when(pl.program_id(0) == 0)
    def _():
        for j in range(count):
            at = pl.multiple_of((2 * j + core[0]) * depth, depth)
            panels[pl.ds(at, depth), :] = same[j]
            at = pl.multiple_of((2 * j + 1 - core[0]) * depth, depth)
            panels[pl.ds(at, depth), :] = other[j]

    out[...] = jnp.dot(mass[...], panels[...], preferred_element_type=F32)


def mass_dot(core, mass, same, other, *earlier):
    rows, depth = mass.shape
    width = same.shape[2]
    chunk = rows // 4
    whole = pl.BlockSpec(same.shape, lambda i: (0, 0, 0))
    return pl.pallas_call(
        dot_kernel,
        grid=(rows // chunk,),
        out_shape=jax.ShapeDtypeStruct((rows, width), F32),
        in_specs=[SMEM, pl.BlockSpec((chunk, depth), lambda i: (i, 0)), whole, whole],
        out_specs=pl.BlockSpec((chunk, width), lambda i: (i, 0)),
        scratch_shapes=[pltpu.VMEM((depth, width), BF16)],
        compiler_params=pltpu.CompilerParams(vmem_limit_bytes=10 * 2**20),
        cost_estimate=pl.CostEstimate(
            flops=DF * 2 * rows * depth * width, bytes_accessed=7 * 2**20, transcendentals=0
        ),
        name="mass_dot",
    )(core, mass, same, other, *earlier)


def body(mode_block, k_blocks, block_cols, panel_node, added_mass, low_edge, high_edge):
    n_row = lax.axis_size("row")
    n_col = lax.axis_size("col")
    devices = n_row * n_col
    my_row = lax.axis_index("row")
    my_col = lax.axis_index("col")
    linear = my_row * n_col + my_col
    core = (my_row % 2).astype(jnp.int32).reshape(1)
    rows_dev, width = mode_block.shape
    size = k_blocks.shape[2]
    blocks_dev = rows_dev // size
    per_block = panel_node.shape[0] // devices
    slots = 2 * devices
    both = ("row", "col")

    panel_rows = panel_node.reshape(devices, per_block)
    source = panel_rows // rows_dev
    before = jnp.concatenate([jnp.full((devices, 1), -1, source.dtype), source[:, :-1]], axis=1)
    rank = (source == before).astype(jnp.int32)
    owned = source == linear
    local = panel_rows - linear * rows_dev
    first = jnp.max(jnp.where(owned & (rank == 0), local, -1), axis=1)
    second = jnp.max(jnp.where(owned & (rank == 1), local, -1), axis=1)
    by_block = jnp.stack([first, second], axis=0)
    by_target = by_block.reshape(2, n_col, n_row).transpose(0, 2, 1)
    shell_rows = jnp.arange(rows_dev, dtype=jnp.int32)
    pick = (by_target.reshape(slots, 1) == shell_rows[None, :]).astype(BF16)
    place = (shell_rows[:, None] == by_block.reshape(1, slots)).astype(BF16)
    flat = rank * devices + source
    slot_ids = jnp.arange(slots, dtype=jnp.int32)
    in_flat = lax.dynamic_index_in_dim(flat, my_col * n_row + my_row, 0, keepdims=False)
    out_flat = lax.dynamic_index_in_dim(flat, linear, 0, keepdims=False)
    gather_in = (in_flat[:, None] == slot_ids[None, :]).astype(BF16)
    spread_out = (slot_ids[:, None] == out_flat[None, :]).astype(BF16)

    cols = block_cols - (linear * blocks_dev - 2)
    halo = 2 * size
    n_same = n_row // 2
    same_core = [[i for i in range(n_row) if i % 2 == c] for c in range(2)]
    swap_core = [(i, i ^ 1) for i in range(n_row)]
    forward = [(i, i + 1) for i in range(devices - 1)]
    backward = [(i + 1, i) for i in range(devices - 1)]
    to_in = [(b, (b % n_row) * n_col + b // n_row) for b in range(devices)]

    block_f32 = jax.ShapeDtypeStruct((rows_dev, width), F32)
    wet_f32 = jax.ShapeDtypeStruct((slots, width), F32)
    load_f32 = jax.ShapeDtypeStruct((per_block, width), F32)
    edge_f32 = jax.ShapeDtypeStruct((halo, width), F32)
    message_f32 = jax.ShapeDtypeStruct((8 * devices, LANES), F32)
    padded = pltpu.VMEM((rows_dev + 2 * halo, width), BF16)

    def stiff(low, current, high, previous, scale, shift, with_wet):
        shapes = [block_f32, wet_f32] if with_wet else [block_f32]
        args = (cols, k_blocks, low, current, high, previous, scale, shift)
        args = args + ((pick,) if with_wet else ())
        made = call(
            stiff_kernel, "stiff", shapes, [SMEM] + [VMEM] * (len(args) - 1),
            SF * 10**9, 8 * 2**20, [padded, padded], 12,
        )(*args)
        return made if with_wet else (made[0], None)

    def pack(parts, gain, wet):
        shapes = [message_f32] if wet is None else [load_f32, message_f32]
        args = (parts, gain, spread_out) + (() if wet is None else (wet,))
        made = call(pack_kernel, "pack", shapes, [VMEM] * len(args), 10**8, 3 * 2**20)(*args)
        return (None, made[0]) if wet is None else made

    def exchange(message):
        return lax.all_to_all(message, both, split_axis=0, concat_axis=0, tiled=True)

    def gathered(sent):
        same = lax.all_to_all(
            sent, "row", split_axis=0, concat_axis=0, tiled=True, axis_index_groups=same_core
        )
        return same, lax.ppermute(same, "row", swap_core)

    lower = low_edge.astype(F32) * 0.25
    upper = high_edge.astype(F32) * 0.25
    centre = (0.5 * (upper + lower))[None, :]
    radius = (0.5 * (upper - lower))[None, :]
    total_rows = rows_dev * devices
    ones = jnp.ones((1, width), F32)

    current = mode_block
    previous = jnp.zeros_like(current)
    head, tail = current[:halo], current[rows_dev - halo :]
    start_rows = jnp.dot(pick, current.astype(BF16), preferred_element_type=F32)
    start_rows = start_rows.astype(BF16).reshape(2, devices, width).transpose(1, 0, 2)
    start_rows = exchange(start_rows).transpose(1, 0, 2).reshape(slots, width)
    wetted = jnp.dot(gather_in, start_rows, preferred_element_type=F32).astype(BF16)
    sent = jnp.broadcast_to(wetted[None], (n_same,) + wetted.shape)
    for outer_no in range(OUTER):
        for degree_no in range(DEGREE):
            last = outer_no == OUTER - 1 and degree_no == DEGREE - 1
            rescale = outer_no > 0 and degree_no == 0
            gain = (1.0 if degree_no == 0 else 2.0) / radius
            before = jnp.zeros_like(current) if degree_no == 0 else previous
            low = lax.ppermute(tail, both, forward)
            high = lax.ppermute(head, both, backward)
            same, other = gathered(sent)
            partial = mass_dot(core, added_mass, same, other)
            dry, wet = stiff(low, current, high, before, gain, -centre * gain, not last)
            parts = lax.all_to_all(
                partial.reshape(n_col, per_block, width), "col", split_axis=0, concat_axis=0, tiled=True
            )
            load, message = pack(parts, gain, wet)
            message = message.reshape(devices, 8, LANES)
            if rescale:
                squares = jnp.sum(current * current, axis=0).reshape(1, 2, LANES)
                squares = jnp.broadcast_to(
                    jnp.concatenate([squares, jnp.zeros((1, 6, LANES), F32)], axis=1), message.shape
                )
                got = exchange(jnp.concatenate([message, squares], axis=1))
                squares = jnp.sum(got[:, 8:10], axis=0).reshape(1, width)
                factor = 1.0 / jnp.sqrt(squares / total_rows + 1e-06)
            else:
                got = exchange(message)
                factor = ones
            got = got.reshape(-1, LANES)
            if last:
                following = call(meet_kernel, "meet", block_f32, [VMEM] * 4, 3 * 10**8, 3 * 2**20)(
                    got, dry, place, factor
                )
            else:
                load_in = lax.ppermute(load, both, to_in)
                sent, following, head, tail = call(
                    meet_kernel, "meet",
                    [jax.ShapeDtypeStruct((n_same, per_block, width), BF16), block_f32, edge_f32, edge_f32],
                    [VMEM] * 6, 4 * 10**8, 4 * 2**20,
                )(got, dry, place, factor, load_in, gather_in)
            if rescale:
                current = current * factor
            previous = current
            current = following
    squares = jnp.sum(current * current, axis=0)
    squares = exchange(jnp.broadcast_to(squares[None, None, :], (devices, 1, width)))
    squares = jnp.sum(squares, axis=0)
    return current / jnp.sqrt(squares / total_rows + 1e-06)


def solution(mesh):
    placed = (
        P(("row", "col"), None),
        P(("row", "col"), None, None, None),
        P(("row", "col"), None),
        P(),
        P("row", "col"),
        P(),
        P(),
    )
    return jax.shard_map(
        body, mesh=mesh, in_specs=placed, out_specs=P(("row", "col"), None), check_vma=False
    )
```

```python
import functools

import jax
import jax.numpy as jnp
from jax import lax
from jax.experimental import pallas as pl
from jax.experimental.pallas import tpu as pltpu
from jax.sharding import PartitionSpec as P

DEGREE = 3
OUTER = 2
F32 = jnp.float32
BF16 = jnp.bfloat16
LANES = 128
PAD = 16
STEPS = 32000.0
VMEM = pl.BlockSpec(memory_space=pltpu.VMEM)
HBM = pl.BlockSpec(memory_space=pltpu.HBM)
SMEM = pl.BlockSpec(memory_space=pltpu.SMEM)


def two_parts(value):
    hi = value.astype(BF16)
    return hi, (value - hi.astype(F32)).astype(BF16)


def choose(matrix, value):
    hi, lo = two_parts(value)
    picked = jnp.dot(matrix, hi, preferred_element_type=F32)
    return picked + jnp.dot(matrix, lo, preferred_element_type=F32)


def call(kernel, name, out_shape, in_specs, out_specs, flops, moved, scratch=(), limit=8):
    return pl.pallas_call(
        kernel,
        out_shape=out_shape,
        in_specs=in_specs,
        out_specs=out_specs,
        scratch_shapes=list(scratch),
        compiler_params=pltpu.CompilerParams(vmem_limit_bytes=limit * 2**20),
        cost_estimate=pl.CostEstimate(flops=flops, bytes_accessed=moved, transcendentals=0),
        name=name,
    )


def encode(value, out):
    rows = value.shape[0]
    top = jnp.maximum(jnp.max(jnp.abs(value), axis=0, keepdims=True), 1e-30)
    power = jnp.clip(jnp.ceil(jnp.log2(top)), -100.0, 126.0)
    steps = jnp.round(value * (STEPS * jnp.exp2(-power)))
    out[0:rows, :] = steps.astype(jnp.int32).astype(jnp.int16)
    tail = jnp.broadcast_to(power, (PAD, value.shape[1]))
    out[rows : rows + PAD, :] = tail.astype(jnp.int32).astype(jnp.int16)


def decode(coded):
    rows = coded.shape[0] - PAD
    power = coded[rows : rows + PAD, :].astype(jnp.int32).astype(F32)[0:1]
    return coded[0:rows, :].astype(jnp.int32).astype(F32) * (jnp.exp2(power) * (1.0 / STEPS))


def edge_kernel(head, tail, head_out, tail_out):
    encode(head[...], head_out)
    encode(tail[...], tail_out)


def stiff_kernel(with_prev, with_wet, *refs):
    refs = list(refs)
    cols, k_hbm, low, here_hbm, high, scale, shift = refs[:7]
    del refs[:7]
    prev_hbm, weight = (refs.pop(0), refs.pop(0)) if with_prev else (None, None)
    pick = refs.pop(0) if with_wet else None
    out_hbm = refs.pop(0)
    wet = refs.pop(0) if with_wet else None
    k, here, prev, out, p_hi, p_lo, k_sem, here_sem, prev_sem, out_sem = refs
    rows = here.shape[0]
    size = k.shape[2]
    halo = low.shape[0] - PAD
    count = rows // size
    here_copy = pltpu.make_async_copy(here_hbm, here, here_sem)
    here_copy.start()
    k_copies = [pltpu.make_async_copy(k_hbm.at[i], k.at[i], k_sem.at[i]) for i in range(count)]
    for copy in k_copies:
        copy.start()
    if with_prev:
        prev_copy = pltpu.make_async_copy(prev_hbm, prev, prev_sem)
        prev_copy.start()

    def put(value, start):
        hi, lo = two_parts(value)
        p_hi[start : start + value.shape[0], :] = hi
        p_lo[start : start + value.shape[0], :] = lo

    put(decode(low), 0)
    put(decode(high), halo + rows)
    here_copy.wait()
    put(here[...], halo)
    out_copies = []
    for i in range(count):
        k_copies[i].wait()
        if with_prev and i == 0:
            prev_copy.wait()
        acc = jnp.zeros((size, here.shape[1]), F32)
        for j in range(k.shape[1]):
            at = pl.ds(pl.multiple_of(cols[i, j] * size, size), size)
            kh, kl = two_parts(k[i, j])
            vh = p_hi[at, :]
            vl = p_lo[at, :]
            acc += jnp.dot(kh, vh, preferred_element_type=F32)
            acc += jnp.dot(kh, vl, preferred_element_type=F32)
            acc += jnp.dot(kl, vh, preferred_element_type=F32)
        mine = pl.ds(i * size, size)
        value = scale[...] * acc + shift[...] * here[mine, :]
        if with_prev:
            value = value - weight[...] * prev[mine, :]
        out[mine, :] = value
        copy = pltpu.make_async_copy(out.at[mine], out_hbm.at[mine], out_sem.at[i])
        copy.start()
        out_copies.append(copy)
    if with_wet:
        wet[...] = choose(pick[...], out[...])
    for copy in out_copies:
        copy.wait()


def pack_kernel(rescale, last, *refs):
    refs = list(refs)
    parts, gain, spread = refs[:3]
    del refs[:3]
    wet = None if last else refs.pop(0)
    square = refs.pop(0) if rescale else None
    load = None if last else refs.pop(0)
    message = refs.pop(0)
    total = decode(parts.at[0])
    for i in range(1, parts.shape[0]):
        total = total + decode(parts.at[i])
    total = total * gain[...]
    if not last:
        encode(total, load)
    sent = choose(spread[...], total)
    devices = sent.shape[0] // 2
    rows = message.shape[0] // devices
    for h in range(2):
        piece = slice(h * LANES, (h + 1) * LANES)
        for s in range(2):
            mine = slice(s * devices, (s + 1) * devices)
            message[pl.ds(4 * h + s, devices, stride=rows), :] = sent[mine, piece]
            if not last:
                message[pl.ds(4 * h + 2 + s, devices, stride=rows), :] = wet[mine, piece]
        if rescale:
            message[pl.ds(8 + h, devices, stride=rows), :] = jnp.broadcast_to(
                square[0:1, piece], (devices, LANES)
            )


def slot_rows(got, devices, first):
    rows = got.shape[0] // devices

    def one(s):
        halves = [got[pl.ds(4 * h + first + s, devices, stride=rows), :] for h in range(2)]
        return jnp.concatenate(halves, axis=1)

    return jnp.concatenate([one(0), one(1)], axis=0)


def meet_kernel(rescale, last, total_rows, *refs):
    refs = list(refs)
    got, dry_hbm, place = refs[:3]
    del refs[:3]
    load, gather = (None, None) if last else (refs.pop(0), refs.pop(0))
    sent = None if last else refs.pop(0)
    out = refs.pop(0)
    head, tail = (None, None) if last else (refs.pop(0), refs.pop(0))
    square = refs.pop(0)
    factor_out = refs.pop(0) if rescale else None
    dry, sem = refs
    copy = pltpu.make_async_copy(dry_hbm, dry, sem)
    copy.start()
    devices = place.shape[1] // 2
    factor = None
    if rescale:
        rows = got.shape[0] // devices
        halves = [
            jnp.sum(got[pl.ds(8 + h, devices, stride=rows), :], axis=0, keepdims=True) for h in range(2)
        ]
        factor = 1.0 / jnp.sqrt(jnp.concatenate(halves, axis=1) / total_rows + 1e-06)
        factor_out[...] = factor
    if not last:
        value = choose(gather[...], slot_rows(got, devices, 2)) + decode(load)
        if rescale:
            value = value * factor
        value = value.astype(BF16)
        for i in range(sent.shape[0]):
            sent[i] = value
    placed = choose(place[...], slot_rows(got, devices, 0))
    copy.wait()
    value = dry[...] + placed
    if rescale:
        value = value * factor
    out[...] = value
    if not last:
        rows = head.shape[0] - PAD
        encode(value[:rows], head)
        encode(value[value.shape[0] - rows :], tail)
    square[...] = jnp.broadcast_to(jnp.sum(value * value, axis=0, keepdims=True), square.shape)


def dot_kernel(core, mass_hbm, same, other, out, mass, panels, sems):
    count, depth, _ = same.shape
    chunks = sems.shape[0]
    chunk = mass.shape[0] // chunks
    block = out.shape[1] - PAD
    copies = []
    for i in range(chunks):
        rows = pl.ds(i * chunk, chunk)
        copies.append(pltpu.make_async_copy(mass_hbm.at[rows], mass.at[rows], sems.at[i]))
        copies[i].start()
    for j in range(count):
        at = pl.multiple_of((2 * j + core[0]) * depth, depth)
        panels[pl.ds(at, depth), :] = same[j]
        at = pl.multiple_of((2 * j + 1 - core[0]) * depth, depth)
        panels[pl.ds(at, depth), :] = other[j]
    for i in range(chunks):
        copies[i].wait()
        value = jnp.dot(
            mass[i * chunk : (i + 1) * chunk, :], panels[...], preferred_element_type=F32
        )
        for j in range(chunk // block):
            encode(value[j * block : (j + 1) * block], out.at[i * (chunk // block) + j])


def body(mode_block, k_blocks, block_cols, panel_node, added_mass, low_edge, high_edge):
    n_row = lax.axis_size("row")
    n_col = lax.axis_size("col")
    devices = n_row * n_col
    my_row = lax.axis_index("row")
    my_col = lax.axis_index("col")
    linear = my_row * n_col + my_col
    core = (my_row % 2).astype(jnp.int32).reshape(1)
    rows_dev, width = mode_block.shape
    size = k_blocks.shape[2]
    blocks_dev = rows_dev // size
    per_block = panel_node.shape[0] // devices
    slots = 2 * devices
    both = ("row", "col")

    panel_rows = panel_node.reshape(devices, per_block)
    source = panel_rows // rows_dev
    before = jnp.concatenate([jnp.full((devices, 1), -1, source.dtype), source[:, :-1]], axis=1)
    rank = (source == before).astype(jnp.int32)
    owned = source == linear
    local = panel_rows - linear * rows_dev
    first = jnp.max(jnp.where(owned & (rank == 0), local, -1), axis=1)
    second = jnp.max(jnp.where(owned & (rank == 1), local, -1), axis=1)
    by_block = jnp.stack([first, second], axis=0)
    by_target = by_block.reshape(2, n_col, n_row).transpose(0, 2, 1)
    shell_rows = jnp.arange(rows_dev, dtype=jnp.int32)
    pick = (by_target.reshape(slots, 1) == shell_rows[None, :]).astype(BF16)
    place = (shell_rows[:, None] == by_block.reshape(1, slots)).astype(BF16)
    flat = rank * devices + source
    slot_ids = jnp.arange(slots, dtype=jnp.int32)
    in_flat = lax.dynamic_index_in_dim(flat, my_col * n_row + my_row, 0, keepdims=False)
    out_flat = lax.dynamic_index_in_dim(flat, linear, 0, keepdims=False)
    gather_in = (in_flat[:, None] == slot_ids[None, :]).astype(BF16)
    spread_out = (slot_ids[:, None] == out_flat[None, :]).astype(BF16)

    cols = block_cols - (linear * blocks_dev - 2)
    halo = 2 * size
    n_same = n_row // 2
    same_core = [[i for i in range(n_row) if i % 2 == c] for c in range(2)]
    swap_core = [(i, i ^ 1) for i in range(n_row)]
    forward = [(i, i + 1) for i in range(devices - 1)]
    backward = [(i + 1, i) for i in range(devices - 1)]
    to_in = [(b, (b % n_row) * n_col + b // n_row) for b in range(devices)]

    block_f32 = jax.ShapeDtypeStruct((rows_dev, width), F32)
    wet_f32 = jax.ShapeDtypeStruct((slots, width), F32)
    row_f32 = jax.ShapeDtypeStruct((1, width), F32)
    eight_f32 = jax.ShapeDtypeStruct((8, width), F32)
    load_i16 = jax.ShapeDtypeStruct((per_block + PAD, width), jnp.int16)
    parts_i16 = jax.ShapeDtypeStruct((n_col, per_block + PAD, width), jnp.int16)
    edge_i16 = jax.ShapeDtypeStruct((halo + PAD, width), jnp.int16)
    sent_bf16 = jax.ShapeDtypeStruct((n_same, per_block, width), BF16)
    block_vmem = pltpu.VMEM((rows_dev, width), F32)
    padded = pltpu.VMEM((rows_dev + 2 * halo, width), BF16)
    dma = pltpu.SemaphoreType.DMA

    def stiff(low, current, high, previous, weight, scale, shift, with_wet):
        with_prev = previous is not None
        args = [cols, k_blocks, low, current, high, scale, shift]
        specs = [SMEM, HBM, VMEM, HBM, VMEM, VMEM, VMEM]
        if with_prev:
            args, specs = args + [previous, weight], specs + [HBM, VMEM]
        if with_wet:
            args, specs = args + [pick], specs + [VMEM]
        made = call(
            functools.partial(stiff_kernel, with_prev, with_wet), "stiff",
            [block_f32] + [wet_f32] * with_wet, specs, [HBM] + [VMEM] * with_wet,
            80 * 10**9, 8 * 2**20,
            [
                pltpu.VMEM(k_blocks.shape, F32), block_vmem, block_vmem, block_vmem, padded, padded,
                dma((blocks_dev,)), dma, dma, dma((blocks_dev,)),
            ],
            14,
        )(*args)
        return (made[0], made[1] if with_wet else None)

    def mass_dot(same, other):
        return call(
            dot_kernel, "mass_dot", parts_i16, [SMEM, HBM, VMEM, VMEM], VMEM,
            2 * added_mass.size * width, 6 * 2**20,
            [pltpu.VMEM(added_mass.shape, BF16), pltpu.VMEM((added_mass.shape[1], width), BF16), dma((4,))],
            14,
        )(core, added_mass, same, other)

    def pack(parts, gain, wet, square):
        rows = 8 if square is None else 16
        message = jax.ShapeDtypeStruct((rows * devices, LANES), F32)
        shapes = [message] if wet is None else [load_i16, message]
        args = [parts, gain, spread_out] + [v for v in (wet, square) if v is not None]
        made = call(
            functools.partial(pack_kernel, square is not None, wet is None), "pack",
            shapes, [VMEM] * len(args), [VMEM] * len(shapes), 10**8, 3 * 2**20,
        )(*args)
        return (None, made[0]) if wet is None else made

    def meet(got, dry, load, rescale):
        last = load is None
        args = [got, dry, place] + ([] if last else [load, gather_in])
        specs = [VMEM, HBM] + [VMEM] * (len(args) - 2)
        shapes = [block_f32] if last else [sent_bf16, block_f32, edge_i16, edge_i16]
        shapes = shapes + [eight_f32] + [row_f32] * rescale
        made = list(call(
            functools.partial(meet_kernel, rescale, last, rows_dev * devices), "meet",
            shapes, specs, [VMEM] * len(shapes), 4 * 10**8, 4 * 2**20, [block_vmem, dma],
        )(*args))
        factor = made.pop() if rescale else None
        square = made.pop()
        if last:
            return None, made[0], None, None, square, factor
        return (*made, square, factor)

    def exchange(message):
        return lax.all_to_all(message, both, split_axis=0, concat_axis=0, tiled=True)

    def gathered(sent):
        same = lax.all_to_all(
            sent, "row", split_axis=0, concat_axis=0, tiled=True, axis_index_groups=same_core
        )
        return same, lax.ppermute(same, "row", swap_core)

    lower = low_edge.astype(F32) * 0.25
    upper = high_edge.astype(F32) * 0.25
    centre = (0.5 * (upper + lower))[None, :]
    radius = (0.5 * (upper - lower))[None, :]
    total_rows = rows_dev * devices

    current = mode_block
    start_rows = jnp.dot(pick, current.astype(BF16), preferred_element_type=F32)
    start_rows = start_rows.astype(BF16).reshape(2, devices, width).transpose(1, 0, 2)
    start_rows = exchange(start_rows).transpose(1, 0, 2).reshape(slots, width)
    wetted = jnp.dot(gather_in, start_rows, preferred_element_type=F32).astype(BF16)
    sent = jnp.broadcast_to(wetted[None], (n_same,) + wetted.shape)
    head, tail = call(
        edge_kernel, "edges", [edge_i16, edge_i16], [VMEM] * 2, [VMEM] * 2, 10**6, 2**20
    )(current[:halo], current[rows_dev - halo :])
    ones = jnp.ones((1, width), F32)
    previous, weight, square = None, ones, None
    for outer_no in range(OUTER):
        for degree_no in range(DEGREE):
            last = outer_no == OUTER - 1 and degree_no == DEGREE - 1
            rescale = outer_no > 0 and degree_no == 0
            gain = (1.0 if degree_no == 0 else 2.0) / radius
            before = None if degree_no == 0 else previous
            low = lax.ppermute(tail, both, forward)
            high = lax.ppermute(head, both, backward)
            same, other = gathered(sent)
            partial = mass_dot(same, other)
            dry, wet = stiff(low, current, high, before, weight, gain, -centre * gain, not last)
            parts = lax.all_to_all(partial, "col", split_axis=0, concat_axis=0, tiled=True)
            load, message = pack(parts, gain, wet, square if rescale else None)
            got = exchange(message.reshape(devices, -1, LANES)).reshape(-1, LANES)
            load_in = None if last else lax.ppermute(load, both, to_in)
            previous = current
            sent, current, head, tail, square, factor = meet(got, dry, load_in, rescale)
            weight = factor if rescale else ones
    squares = exchange(jnp.broadcast_to(square[None, :1, :], (devices, 1, width)))
    squares = jnp.sum(squares, axis=0)
    return current / jnp.sqrt(squares / total_rows + 1e-06)


def solution(mesh):
    placed = (
        P(("row", "col"), None),
        P(("row", "col"), None, None, None),
        P(("row", "col"), None),
        P(),
        P("row", "col"),
        P(),
        P(),
    )
    return jax.shard_map(
        body, mesh=mesh, in_specs=placed, out_specs=P(("row", "col"), None), check_vma=False
    )
```

```python
import functools

import jax
import jax.numpy as jnp
from jax import lax
from jax.experimental import pallas as pl
from jax.experimental.pallas import tpu as pltpu
from jax.sharding import PartitionSpec as P

DEGREE = 3
OUTER = 2
F32 = jnp.float32
BF16 = jnp.bfloat16
LANES = 128
PAD = 16
STEPS = 32000.0
VMEM = pl.BlockSpec(memory_space=pltpu.VMEM)
HBM = pl.BlockSpec(memory_space=pltpu.HBM)
SMEM = pl.BlockSpec(memory_space=pltpu.SMEM)


def two_parts(value):
    hi = value.astype(BF16)
    return hi, (value - hi.astype(F32)).astype(BF16)


def choose(matrix, value):
    hi, lo = two_parts(value)
    picked = jnp.dot(matrix, hi, preferred_element_type=F32)
    return picked + jnp.dot(matrix, lo, preferred_element_type=F32)


def call(kernel, name, out_shape, in_specs, out_specs, flops, moved, scratch=(), limit=8):
    return pl.pallas_call(
        kernel,
        out_shape=out_shape,
        in_specs=in_specs,
        out_specs=out_specs,
        scratch_shapes=list(scratch),
        compiler_params=pltpu.CompilerParams(vmem_limit_bytes=limit * 2**20),
        cost_estimate=pl.CostEstimate(flops=flops, bytes_accessed=moved, transcendentals=0),
        name=name,
    )


def encode(value, out):
    rows = value.shape[0]
    top = jnp.maximum(jnp.max(jnp.abs(value), axis=0, keepdims=True), 1e-30)
    power = jnp.clip(jnp.ceil(jnp.log2(top)), -100.0, 126.0)
    steps = jnp.round(value * (STEPS * jnp.exp2(-power)))
    out[0:rows, :] = steps.astype(jnp.int32).astype(jnp.int16)
    tail = jnp.broadcast_to(power, (PAD, value.shape[1]))
    out[rows : rows + PAD, :] = tail.astype(jnp.int32).astype(jnp.int16)


def decode(coded):
    rows = coded.shape[0] - PAD
    power = coded[rows : rows + PAD, :].astype(jnp.int32).astype(F32)[0:1]
    return coded[0:rows, :].astype(jnp.int32).astype(F32) * (jnp.exp2(power) * (1.0 / STEPS))


def edge_kernel(head, tail, head_out, tail_out):
    encode(head[...], head_out)
    encode(tail[...], tail_out)


def stiff_kernel(with_prev, with_wet, *refs):
    refs = list(refs)
    cols, k_hbm, low, here_hbm, high, scale, shift = refs[:7]
    del refs[:7]
    prev_hbm, weight = (refs.pop(0), refs.pop(0)) if with_prev else (None, None)
    pick = refs.pop(0) if with_wet else None
    out_hbm = refs.pop(0)
    wet = refs.pop(0) if with_wet else None
    k, here, prev, out, p_hi, p_lo, k_sem, here_sem, prev_sem, out_sem = refs
    rows = here.shape[0]
    size = k.shape[2]
    halo = low.shape[0] - PAD
    count = rows // size
    here_copy = pltpu.make_async_copy(here_hbm, here, here_sem)
    here_copy.start()
    k_copies = [pltpu.make_async_copy(k_hbm.at[i], k.at[i], k_sem.at[i]) for i in range(count)]
    for copy in k_copies:
        copy.start()
    if with_prev:
        prev_copy = pltpu.make_async_copy(prev_hbm, prev, prev_sem)
        prev_copy.start()

    def put(value, start):
        hi, lo = two_parts(value)
        p_hi[start : start + value.shape[0], :] = hi
        p_lo[start : start + value.shape[0], :] = lo

    put(decode(low), 0)
    put(decode(high), halo + rows)
    here_copy.wait()
    put(here[...], halo)
    out_copies = []
    for i in range(count):
        k_copies[i].wait()
        if with_prev and i == 0:
            prev_copy.wait()
        acc = jnp.zeros((size, here.shape[1]), F32)
        for j in range(k.shape[1]):
            at = pl.ds(pl.multiple_of(cols[i, j] * size, size), size)
            kh, kl = two_parts(k[i, j])
            vh = p_hi[at, :]
            vl = p_lo[at, :]
            acc += jnp.dot(kh, vh, preferred_element_type=F32)
            acc += jnp.dot(kh, vl, preferred_element_type=F32)
            acc += jnp.dot(kl, vh, preferred_element_type=F32)
        mine = pl.ds(i * size, size)
        value = scale[...] * acc + shift[...] * here[mine, :]
        if with_prev:
            value = value - weight[...] * prev[mine, :]
        out[mine, :] = value
        copy = pltpu.make_async_copy(out.at[mine], out_hbm.at[mine], out_sem.at[i])
        copy.start()
        out_copies.append(copy)
    if with_wet:
        wet[...] = choose(pick[...], out[...])
    for copy in out_copies:
        copy.wait()


def pack_kernel(rescale, last, *refs):
    refs = list(refs)
    parts, gain, spread = refs[:3]
    del refs[:3]
    wet = None if last else refs.pop(0)
    square = refs.pop(0) if rescale else None
    load = None if last else refs.pop(0)
    message = refs.pop(0)
    total = decode(parts.at[0])
    for i in range(1, parts.shape[0]):
        total = total + decode(parts.at[i])
    total = total * gain[...]
    if not last:
        encode(total, load)
    sent = choose(spread[...], total)
    devices = sent.shape[0] // 2
    rows = message.shape[0] // devices
    for h in range(2):
        piece = slice(h * LANES, (h + 1) * LANES)
        for s in range(2):
            mine = slice(s * devices, (s + 1) * devices)
            message[pl.ds(4 * h + s, devices, stride=rows), :] = sent[mine, piece]
            if not last:
                message[pl.ds(4 * h + 2 + s, devices, stride=rows), :] = wet[mine, piece]
        if rescale:
            message[pl.ds(8 + h, devices, stride=rows), :] = jnp.broadcast_to(
                square[0:1, piece], (devices, LANES)
            )


def slot_rows(got, devices, first):
    rows = got.shape[0] // devices

    def one(s):
        halves = [got[pl.ds(4 * h + first + s, devices, stride=rows), :] for h in range(2)]
        return jnp.concatenate(halves, axis=1)

    return jnp.concatenate([one(0), one(1)], axis=0)


def meet_kernel(rescale, last, total_rows, *refs):
    refs = list(refs)
    got, dry_hbm, place = refs[:3]
    del refs[:3]
    load, gather = (None, None) if last else (refs.pop(0), refs.pop(0))
    sent = None if last else refs.pop(0)
    out = refs.pop(0)
    head, tail = (None, None) if last else (refs.pop(0), refs.pop(0))
    square = refs.pop(0)
    factor_out = refs.pop(0) if rescale else None
    dry, sem = refs
    copy = pltpu.make_async_copy(dry_hbm, dry, sem)
    copy.start()
    devices = place.shape[1] // 2
    factor = None
    if rescale:
        rows = got.shape[0] // devices
        halves = [
            jnp.sum(got[pl.ds(8 + h, devices, stride=rows), :], axis=0, keepdims=True) for h in range(2)
        ]
        factor = 1.0 / jnp.sqrt(jnp.concatenate(halves, axis=1) / total_rows + 1e-06)
        factor_out[...] = factor
    if not last:
        value = choose(gather[...], slot_rows(got, devices, 2)) + decode(load)
        if rescale:
            value = value * factor
        value = value.astype(BF16)
        for i in range(sent.shape[0]):
            sent[i] = value
    placed = choose(place[...], slot_rows(got, devices, 0))
    copy.wait()
    value = dry[...] + placed
    if rescale:
        value = value * factor
    out[...] = value
    if not last:
        rows = head.shape[0] - PAD
        encode(value[:rows], head)
        encode(value[value.shape[0] - rows :], tail)
    square[...] = jnp.broadcast_to(jnp.sum(value * value, axis=0, keepdims=True), square.shape)


def dot_kernel(core, mass_hbm, same, other, out, mass, panels, sems):
    count, depth, _ = same.shape
    chunks = sems.shape[0]
    chunk = mass.shape[0] // chunks
    block = out.shape[1] - PAD
    copies = []
    for i in range(chunks):
        rows = pl.ds(i * chunk, chunk)
        copies.append(pltpu.make_async_copy(mass_hbm.at[rows], mass.at[rows], sems.at[i]))
        copies[i].start()
    for j in range(count):
        at = pl.multiple_of((2 * j + core[0]) * depth, depth)
        panels[pl.ds(at, depth), :] = same[j]
        at = pl.multiple_of((2 * j + 1 - core[0]) * depth, depth)
        panels[pl.ds(at, depth), :] = other[j]
    for i in range(chunks):
        copies[i].wait()
        value = jnp.dot(
            mass[i * chunk : (i + 1) * chunk, :], panels[...], preferred_element_type=F32
        )
        for j in range(chunk // block):
            encode(value[j * block : (j + 1) * block], out.at[i * (chunk // block) + j])


def body(mode_block, k_blocks, block_cols, panel_node, added_mass, low_edge, high_edge):
    n_row = lax.axis_size("row")
    n_col = lax.axis_size("col")
    devices = n_row * n_col
    my_row = lax.axis_index("row")
    my_col = lax.axis_index("col")
    linear = my_row * n_col + my_col
    core = (my_row % 2).astype(jnp.int32).reshape(1)
    rows_dev, width = mode_block.shape
    size = k_blocks.shape[2]
    blocks_dev = rows_dev // size
    per_block = panel_node.shape[0] // devices
    slots = 2 * devices
    both = ("row", "col")

    panel_rows = panel_node.reshape(devices, per_block)
    source = panel_rows // rows_dev
    before = jnp.concatenate([jnp.full((devices, 1), -1, source.dtype), source[:, :-1]], axis=1)
    rank = (source == before).astype(jnp.int32)
    owned = source == linear
    local = panel_rows - linear * rows_dev
    first = jnp.max(jnp.where(owned & (rank == 0), local, -1), axis=1)
    second = jnp.max(jnp.where(owned & (rank == 1), local, -1), axis=1)
    by_block = jnp.stack([first, second], axis=0)
    by_target = by_block.reshape(2, n_col, n_row).transpose(0, 2, 1)
    shell_rows = jnp.arange(rows_dev, dtype=jnp.int32)
    pick = (by_target.reshape(slots, 1) == shell_rows[None, :]).astype(BF16)
    place = (shell_rows[:, None] == by_block.reshape(1, slots)).astype(BF16)
    flat = rank * devices + source
    slot_ids = jnp.arange(slots, dtype=jnp.int32)
    in_flat = lax.dynamic_index_in_dim(flat, my_col * n_row + my_row, 0, keepdims=False)
    out_flat = lax.dynamic_index_in_dim(flat, linear, 0, keepdims=False)
    gather_in = (in_flat[:, None] == slot_ids[None, :]).astype(BF16)
    spread_out = (slot_ids[:, None] == out_flat[None, :]).astype(BF16)

    cols = block_cols - (linear * blocks_dev - 2)
    halo = 2 * size
    n_same = n_row // 2
    same_core = [[i for i in range(n_row) if i % 2 == c] for c in range(2)]
    swap_core = [(i, i ^ 1) for i in range(n_row)]
    forward = [(i, i + 1) for i in range(devices - 1)]
    backward = [(i + 1, i) for i in range(devices - 1)]
    to_in = [(b, (b % n_row) * n_col + b // n_row) for b in range(devices)]

    block_f32 = jax.ShapeDtypeStruct((rows_dev, width), F32)
    wet_f32 = jax.ShapeDtypeStruct((slots, width), F32)
    row_f32 = jax.ShapeDtypeStruct((1, width), F32)
    eight_f32 = jax.ShapeDtypeStruct((8, width), F32)
    load_i16 = jax.ShapeDtypeStruct((per_block + PAD, width), jnp.int16)
    parts_i16 = jax.ShapeDtypeStruct((n_col, per_block + PAD, width), jnp.int16)
    edge_i16 = jax.ShapeDtypeStruct((halo + PAD, width), jnp.int16)
    sent_bf16 = jax.ShapeDtypeStruct((n_same, per_block, width), BF16)
    block_vmem = pltpu.VMEM((rows_dev, width), F32)
    padded = pltpu.VMEM((rows_dev + 2 * halo, width), BF16)
    dma = pltpu.SemaphoreType.DMA

    def stiff(low, current, high, previous, weight, scale, shift, with_wet):
        with_prev = previous is not None
        args = [cols, k_blocks, low, current, high, scale, shift]
        specs = [SMEM, HBM, VMEM, HBM, VMEM, VMEM, VMEM]
        if with_prev:
            args, specs = args + [previous, weight], specs + [HBM, VMEM]
        if with_wet:
            args, specs = args + [pick], specs + [VMEM]
        made = call(
            functools.partial(stiff_kernel, with_prev, with_wet), "stiff",
            [block_f32] + [wet_f32] * with_wet, specs, [HBM] + [VMEM] * with_wet,
            80 * 10**9, 8 * 2**20,
            [
                pltpu.VMEM(k_blocks.shape, F32), block_vmem, block_vmem, block_vmem, padded, padded,
                dma((blocks_dev,)), dma, dma, dma((blocks_dev,)),
            ],
            52,
        )(*args)
        return (made[0], made[1] if with_wet else None)

    def mass_dot(same, other):
        return call(
            dot_kernel, "mass_dot", parts_i16, [SMEM, HBM, VMEM, VMEM], VMEM,
            2 * added_mass.size * width, 6 * 2**20,
            [pltpu.VMEM(added_mass.shape, BF16), pltpu.VMEM((added_mass.shape[1], width), BF16), dma((4,))],
            52,
        )(core, added_mass, same, other)

    def pack(parts, gain, wet, square):
        rows = 8 if square is None else 16
        message = jax.ShapeDtypeStruct((rows * devices, LANES), F32)
        shapes = [message] if wet is None else [load_i16, message]
        args = [parts, gain, spread_out] + [v for v in (wet, square) if v is not None]
        made = call(
            functools.partial(pack_kernel, square is not None, wet is None), "pack",
            shapes, [VMEM] * len(args), [VMEM] * len(shapes), 10**8, 3 * 2**20,
        )(*args)
        return (None, made[0]) if wet is None else made

    def meet(got, dry, load, rescale):
        last = load is None
        args = [got, dry, place] + ([] if last else [load, gather_in])
        specs = [VMEM, HBM] + [VMEM] * (len(args) - 2)
        shapes = [block_f32] if last else [sent_bf16, block_f32, edge_i16, edge_i16]
        shapes = shapes + [eight_f32] + [row_f32] * rescale
        made = list(call(
            functools.partial(meet_kernel, rescale, last, rows_dev * devices), "meet",
            shapes, specs, [VMEM] * len(shapes), 4 * 10**8, 4 * 2**20, [block_vmem, dma], 52,
        )(*args))
        factor = made.pop() if rescale else None
        square = made.pop()
        if last:
            return None, made[0], None, None, square, factor
        return (*made, square, factor)

    def exchange(message):
        return lax.all_to_all(message, both, split_axis=0, concat_axis=0, tiled=True)

    def gathered(sent):
        same = lax.all_to_all(
            sent, "row", split_axis=0, concat_axis=0, tiled=True, axis_index_groups=same_core
        )
        return same, lax.ppermute(same, "row", swap_core)

    lower = low_edge.astype(F32) * 0.25
    upper = high_edge.astype(F32) * 0.25
    centre = (0.5 * (upper + lower))[None, :]
    radius = (0.5 * (upper - lower))[None, :]
    total_rows = rows_dev * devices

    current = mode_block
    start_rows = jnp.dot(pick, current.astype(BF16), preferred_element_type=F32)
    start_rows = start_rows.astype(BF16).reshape(2, devices, width).transpose(1, 0, 2)
    start_rows = exchange(start_rows).transpose(1, 0, 2).reshape(slots, width)
    wetted = jnp.dot(gather_in, start_rows, preferred_element_type=F32).astype(BF16)
    sent = jnp.broadcast_to(wetted[None], (n_same,) + wetted.shape)
    head, tail = call(
        edge_kernel, "edges", [edge_i16, edge_i16], [VMEM] * 2, [VMEM] * 2, 10**6, 2**20
    )(current[:halo], current[rows_dev - halo :])
    ones = jnp.ones((1, width), F32)
    previous, weight, square = None, ones, None
    for outer_no in range(OUTER):
        for degree_no in range(DEGREE):
            last = outer_no == OUTER - 1 and degree_no == DEGREE - 1
            rescale = outer_no > 0 and degree_no == 0
            gain = (1.0 if degree_no == 0 else 2.0) / radius
            before = None if degree_no == 0 else previous
            low = lax.ppermute(tail, both, forward)
            high = lax.ppermute(head, both, backward)
            same, other = gathered(sent)
            partial = mass_dot(same, other)
            dry, wet = stiff(low, current, high, before, weight, gain, -centre * gain, not last)
            parts = lax.all_to_all(partial, "col", split_axis=0, concat_axis=0, tiled=True)
            load, message = pack(parts, gain, wet, square if rescale else None)
            got = exchange(message.reshape(devices, -1, LANES)).reshape(-1, LANES)
            load_in = None if last else lax.ppermute(load, both, to_in)
            previous = current
            sent, current, head, tail, square, factor = meet(got, dry, load_in, rescale)
            weight = factor if rescale else ones
    squares = exchange(jnp.broadcast_to(square[None, :1, :], (devices, 1, width)))
    squares = jnp.sum(squares, axis=0)
    return current / jnp.sqrt(squares / total_rows + 1e-06)


def solution(mesh):
    placed = (
        P(("row", "col"), None),
        P(("row", "col"), None, None, None),
        P(("row", "col"), None),
        P(),
        P("row", "col"),
        P(),
        P(),
    )
    return jax.shard_map(
        body, mesh=mesh, in_specs=placed, out_specs=P(("row", "col"), None), check_vma=False
    )
```

```python
import functools

import jax
import jax.numpy as jnp
from jax import lax
from jax.experimental import pallas as pl
from jax.experimental.pallas import tpu as pltpu
from jax.sharding import PartitionSpec as P

DEGREE = 3
OUTER = 2
F32 = jnp.float32
BF16 = jnp.bfloat16
LANES = 128
PAD = 16
STEPS = 32000.0
VMEM = pl.BlockSpec(memory_space=pltpu.VMEM)
HBM = pl.BlockSpec(memory_space=pltpu.HBM)
ANY = pl.BlockSpec(memory_space=pl.ANY)
SMEM = pl.BlockSpec(memory_space=pltpu.SMEM)


def two_parts(value):
    hi = value.astype(BF16)
    return hi, (value - hi.astype(F32)).astype(BF16)


def choose(matrix, value):
    hi, lo = two_parts(value)
    picked = jnp.dot(matrix, hi, preferred_element_type=F32)
    return picked + jnp.dot(matrix, lo, preferred_element_type=F32)


def call(kernel, name, out_shape, in_specs, out_specs, flops, moved, scratch=(), limit=8):
    return pl.pallas_call(
        kernel,
        out_shape=out_shape,
        in_specs=in_specs,
        out_specs=out_specs,
        scratch_shapes=list(scratch),
        compiler_params=pltpu.CompilerParams(vmem_limit_bytes=limit * 2**20),
        cost_estimate=pl.CostEstimate(flops=flops, bytes_accessed=moved, transcendentals=0),
        name=name,
    )


def encode(value, out):
    rows = value.shape[0]
    top = jnp.maximum(jnp.max(jnp.abs(value), axis=0, keepdims=True), 1e-30)
    power = jnp.clip(jnp.ceil(jnp.log2(top)), -100.0, 126.0)
    steps = jnp.floor(value * (STEPS * jnp.exp2(-power)) + 0.5)
    out[0:rows, :] = steps.astype(jnp.int32).astype(jnp.int16)
    tail = jnp.broadcast_to(power, (PAD, value.shape[1]))
    out[rows : rows + PAD, :] = tail.astype(jnp.int32).astype(jnp.int16)


def decode(coded):
    rows = coded.shape[0] - PAD
    power = coded[rows : rows + PAD, :].astype(jnp.int32).astype(F32)[0:1]
    return coded[0:rows, :].astype(jnp.int32).astype(F32) * (jnp.exp2(power) * (1.0 / STEPS))


def edge_kernel(head, tail, head_out, tail_out):
    encode(head[...], head_out)
    encode(tail[...], tail_out)


def stiff_kernel(with_prev, with_wet, *refs):
    refs = list(refs)
    cols, k_hbm, low, here_hbm, high, scale, shift = refs[:7]
    del refs[:7]
    prev_hbm, weight = (refs.pop(0), refs.pop(0)) if with_prev else (None, None)
    pick = refs.pop(0) if with_wet else None
    out_hbm = refs.pop(0)
    wet = refs.pop(0) if with_wet else None
    k, here, prev, out, p_hi, p_lo, k_sem, here_sem, prev_sem, out_sem = refs
    rows = here.shape[0]
    size = k.shape[2]
    halo = low.shape[0] - PAD
    count = rows // size
    here_copy = pltpu.make_async_copy(here_hbm, here, here_sem)
    here_copy.start()
    row_copies = []
    for i in range(count):
        mine = pl.ds(i * size, size)
        row_copies.append([pltpu.make_async_copy(k_hbm.at[i], k.at[i], k_sem.at[i])])
        if with_prev:
            row_copies[i].append(
                pltpu.make_async_copy(prev_hbm.at[mine], prev.at[mine], prev_sem.at[i])
            )
        for copy in row_copies[i]:
            copy.start()

    def put(value, start):
        hi, lo = two_parts(value)
        p_hi[start : start + value.shape[0], :] = hi
        p_lo[start : start + value.shape[0], :] = lo

    put(decode(low), 0)
    put(decode(high), halo + rows)
    here_copy.wait()
    put(here[...], halo)
    out_copies = []
    for i in range(count):
        for copy in row_copies[i]:
            copy.wait()
        acc = jnp.zeros((size, here.shape[1]), F32)
        for j in range(k.shape[1]):
            at = pl.ds(pl.multiple_of(cols[i, j] * size, size), size)
            kh, kl = two_parts(k[i, j])
            vh = p_hi[at, :]
            vl = p_lo[at, :]
            acc += jnp.dot(kh, vh, preferred_element_type=F32)
            acc += jnp.dot(kh, vl, preferred_element_type=F32)
            acc += jnp.dot(kl, vh, preferred_element_type=F32)
        mine = pl.ds(i * size, size)
        value = scale[...] * acc + shift[...] * here[mine, :]
        if with_prev:
            value = value - weight[...] * prev[mine, :]
        out[mine, :] = value
        copy = pltpu.make_async_copy(out.at[mine], out_hbm.at[mine], out_sem.at[i])
        copy.start()
        out_copies.append(copy)
    if with_wet:
        wet[...] = choose(pick[...], out[...])
    for copy in out_copies:
        copy.wait()


def pack_kernel(rescale, last, *refs):
    refs = list(refs)
    parts, gain, spread = refs[:3]
    del refs[:3]
    wet = None if last else refs.pop(0)
    square = refs.pop(0) if rescale else None
    load = None if last else refs.pop(0)
    message = refs.pop(0)
    total = decode(parts.at[0])
    for i in range(1, parts.shape[0]):
        total = total + decode(parts.at[i])
    total = total * gain[...]
    if not last:
        encode(total, load)
    sent = choose(spread[...], total)
    devices = sent.shape[0] // 2
    rows = message.shape[0] // devices
    for h in range(2):
        piece = slice(h * LANES, (h + 1) * LANES)
        for s in range(2):
            mine = slice(s * devices, (s + 1) * devices)
            message[pl.ds(4 * h + s, devices, stride=rows), :] = sent[mine, piece]
            if not last:
                message[pl.ds(4 * h + 2 + s, devices, stride=rows), :] = wet[mine, piece]
        if rescale:
            message[pl.ds(8 + h, devices, stride=rows), :] = jnp.broadcast_to(
                square[0:1, piece], (devices, LANES)
            )


def slot_rows(got, devices, first):
    rows = got.shape[0] // devices

    def one(s):
        halves = [got[pl.ds(4 * h + first + s, devices, stride=rows), :] for h in range(2)]
        return jnp.concatenate(halves, axis=1)

    return jnp.concatenate([one(0), one(1)], axis=0)


def factor_of(got, devices, total_rows):
    rows = got.shape[0] // devices
    halves = [
        jnp.sum(got[pl.ds(8 + h, devices, stride=rows), :], axis=0, keepdims=True) for h in range(2)
    ]
    return 1.0 / jnp.sqrt(jnp.concatenate(halves, axis=1) / total_rows + 1e-06)


def wet_kernel(rescale, total_rows, got, load, gather, sent):
    devices = gather.shape[1] // 2
    value = choose(gather[...], slot_rows(got, devices, 2)) + decode(load)
    if rescale:
        value = value * factor_of(got, devices, total_rows)
    value = value.astype(BF16)
    for i in range(sent.shape[0]):
        sent[i] = value


def shell_kernel(rescale, last, with_square, total_rows, *refs):
    refs = list(refs)
    got, dry_hbm, place = refs[:3]
    del refs[:3]
    out = refs.pop(0)
    head, tail = (None, None) if last else (refs.pop(0), refs.pop(0))
    square = refs.pop(0) if with_square else None
    factor_out = refs.pop(0) if rescale else None
    dry, sem = refs
    copy = pltpu.make_async_copy(dry_hbm, dry, sem)
    copy.start()
    devices = place.shape[1] // 2
    placed = choose(place[...], slot_rows(got, devices, 0))
    if rescale:
        factor = factor_of(got, devices, total_rows)
        factor_out[...] = factor
    copy.wait()
    value = dry[...] + placed
    if rescale:
        value = value * factor
    out[...] = value
    if not last:
        rows = head.shape[0] - PAD
        encode(value[:rows], head)
        encode(value[value.shape[0] - rows :], tail)
    if with_square:
        square[...] = jnp.broadcast_to(jnp.sum(value * value, axis=0, keepdims=True), square.shape)


def tie_kernel(value, other, out):
    pass


def dot_kernel(core, mass_hbm, same, other, out, mass, panels, sems):
    count, depth, _ = same.shape
    chunks = sems.shape[0]
    chunk = mass.shape[0] // chunks
    block = out.shape[1] - PAD
    copies = []
    for i in range(chunks):
        rows = pl.ds(i * chunk, chunk)
        copies.append(pltpu.make_async_copy(mass_hbm.at[rows], mass.at[rows], sems.at[i]))
        copies[i].start()
    for j in range(count):
        at = pl.multiple_of((2 * j + core[0]) * depth, depth)
        panels[pl.ds(at, depth), :] = same[j]
        at = pl.multiple_of((2 * j + 1 - core[0]) * depth, depth)
        panels[pl.ds(at, depth), :] = other[j]
    for i in range(chunks):
        copies[i].wait()
        value = jnp.dot(
            mass[i * chunk : (i + 1) * chunk, :], panels[...], preferred_element_type=F32
        )
        for j in range(chunk // block):
            encode(value[j * block : (j + 1) * block], out.at[i * (chunk // block) + j])


def body(mode_block, k_blocks, block_cols, panel_node, added_mass, low_edge, high_edge):
    n_row = lax.axis_size("row")
    n_col = lax.axis_size("col")
    devices = n_row * n_col
    my_row = lax.axis_index("row")
    my_col = lax.axis_index("col")
    linear = my_row * n_col + my_col
    core = (my_row % 2).astype(jnp.int32).reshape(1)
    rows_dev, width = mode_block.shape
    size = k_blocks.shape[2]
    blocks_dev = rows_dev // size
    per_block = panel_node.shape[0] // devices
    slots = 2 * devices
    both = ("row", "col")

    panel_rows = panel_node.reshape(devices, per_block)
    source = panel_rows // rows_dev
    before = jnp.concatenate([jnp.full((devices, 1), -1, source.dtype), source[:, :-1]], axis=1)
    rank = (source == before).astype(jnp.int32)
    owned = source == linear
    local = panel_rows - linear * rows_dev
    first = jnp.max(jnp.where(owned & (rank == 0), local, -1), axis=1)
    second = jnp.max(jnp.where(owned & (rank == 1), local, -1), axis=1)
    by_block = jnp.stack([first, second], axis=0)
    by_target = by_block.reshape(2, n_col, n_row).transpose(0, 2, 1)
    shell_rows = jnp.arange(rows_dev, dtype=jnp.int32)
    pick = (by_target.reshape(slots, 1) == shell_rows[None, :]).astype(BF16)
    place = (shell_rows[:, None] == by_block.reshape(1, slots)).astype(BF16)
    flat = rank * devices + source
    slot_ids = jnp.arange(slots, dtype=jnp.int32)
    in_flat = lax.dynamic_index_in_dim(flat, my_col * n_row + my_row, 0, keepdims=False)
    out_flat = lax.dynamic_index_in_dim(flat, linear, 0, keepdims=False)
    gather_in = (in_flat[:, None] == slot_ids[None, :]).astype(BF16)
    spread_out = (slot_ids[:, None] == out_flat[None, :]).astype(BF16)

    cols = block_cols - (linear * blocks_dev - 2)
    halo = 2 * size
    n_same = n_row // 2
    same_core = [[i for i in range(n_row) if i % 2 == c] for c in range(2)]
    swap_core = [(i, i ^ 1) for i in range(n_row)]
    forward = [(i, i + 1) for i in range(devices - 1)]
    backward = [(i + 1, i) for i in range(devices - 1)]
    to_in = [(b, (b % n_row) * n_col + b // n_row) for b in range(devices)]

    block_f32 = jax.ShapeDtypeStruct((rows_dev, width), F32)
    wet_f32 = jax.ShapeDtypeStruct((slots, width), F32)
    row_f32 = jax.ShapeDtypeStruct((1, width), F32)
    eight_f32 = jax.ShapeDtypeStruct((8, width), F32)
    load_i16 = jax.ShapeDtypeStruct((per_block + PAD, width), jnp.int16)
    parts_i16 = jax.ShapeDtypeStruct((n_col, per_block + PAD, width), jnp.int16)
    edge_i16 = jax.ShapeDtypeStruct((halo + PAD, width), jnp.int16)
    sent_bf16 = jax.ShapeDtypeStruct((n_same, per_block, width), BF16)
    block_vmem = pltpu.VMEM((rows_dev, width), F32)
    padded = pltpu.VMEM((rows_dev + 2 * halo, width), BF16)
    dma = pltpu.SemaphoreType.DMA

    def stiff(low, current, high, previous, weight, scale, shift, with_wet):
        with_prev = previous is not None
        args = [cols, k_blocks, low, current, high, scale, shift]
        specs = [SMEM, HBM, VMEM, HBM, VMEM, VMEM, VMEM]
        if with_prev:
            args, specs = args + [previous, weight], specs + [HBM, VMEM]
        if with_wet:
            args, specs = args + [pick], specs + [VMEM]
        made = call(
            functools.partial(stiff_kernel, with_prev, with_wet), "stiff",
            [block_f32] + [wet_f32] * with_wet, specs, [HBM] + [VMEM] * with_wet,
            80 * 10**9, 8 * 2**20,
            [
                pltpu.VMEM(k_blocks.shape, F32), block_vmem, block_vmem, block_vmem, padded, padded,
                dma((blocks_dev,)), dma, dma((blocks_dev,)), dma((blocks_dev,)),
            ],
            52,
        )(*args)
        return (made[0], made[1] if with_wet else None)

    def mass_dot(same, other):
        return call(
            dot_kernel, "mass_dot", parts_i16, [SMEM, HBM, VMEM, VMEM], VMEM,
            2 * added_mass.size * width, 6 * 2**20,
            [pltpu.VMEM(added_mass.shape, BF16), pltpu.VMEM((added_mass.shape[1], width), BF16), dma((4,))],
            52,
        )(core, added_mass, same, other)

    def pack(parts, gain, wet, square):
        rows = 8 if square is None else 16
        message = jax.ShapeDtypeStruct((rows * devices, LANES), F32)
        shapes = [message] if wet is None else [load_i16, message]
        args = [parts, gain, spread_out] + [v for v in (wet, square) if v is not None]
        made = call(
            functools.partial(pack_kernel, square is not None, wet is None), "pack",
            shapes, [VMEM] * len(args), [VMEM] * len(shapes), 10**8, 3 * 2**20,
        )(*args)
        return (None, made[0]) if wet is None else made

    def wet_rows(got, load, rescale):
        return call(
            functools.partial(wet_kernel, rescale, rows_dev * devices), "wet_rows", sent_bf16,
            [VMEM] * 3, VMEM, 10**8, 10**6,
        )(got, load, gather_in)

    def shell(got, dry, rescale, last, with_square):
        shapes = [block_f32] if last else [block_f32, edge_i16, edge_i16]
        shapes = shapes + [eight_f32] * with_square + [row_f32] * rescale
        made = list(call(
            functools.partial(shell_kernel, rescale, last, with_square, rows_dev * devices), "shell",
            shapes, [VMEM, HBM, VMEM], [VMEM] * len(shapes), 20 * 10**9, 4 * 2**20, [block_vmem, dma], 52,
        )(got, dry, place))
        current = made.pop(0)
        head, tail = (None, None) if last else (made.pop(0), made.pop(0))
        square = made.pop(0) if with_square else None
        return current, head, tail, square, made.pop(0) if rescale else None

    def tie(value, other):
        return pl.pallas_call(
            tie_kernel,
            out_shape=jax.ShapeDtypeStruct(value.shape, value.dtype),
            in_specs=[ANY, ANY],
            out_specs=ANY,
            input_output_aliases={0: 0},
            compiler_params=pltpu.CompilerParams(vmem_limit_bytes=4 * 2**20),
            cost_estimate=pl.CostEstimate(flops=0, bytes_accessed=0, transcendentals=0),
            name="tie",
        )(value, other)

    def exchange(message):
        return lax.all_to_all(message, both, split_axis=0, concat_axis=0, tiled=True)

    def gathered(sent, low):
        same = lax.all_to_all(
            sent, "row", split_axis=0, concat_axis=0, tiled=True, axis_index_groups=same_core
        )
        same = tie(same, low)
        return same, lax.ppermute(same, "row", swap_core)

    lower = low_edge.astype(F32) * 0.25
    upper = high_edge.astype(F32) * 0.25
    centre = (0.5 * (upper + lower))[None, :]
    radius = (0.5 * (upper - lower))[None, :]
    total_rows = rows_dev * devices

    current = mode_block
    start_rows = jnp.dot(pick, current.astype(BF16), preferred_element_type=F32)
    start_rows = start_rows.astype(BF16).reshape(2, devices, width).transpose(1, 0, 2)
    start_rows = exchange(start_rows).transpose(1, 0, 2).reshape(slots, width)
    wetted = jnp.dot(gather_in, start_rows, preferred_element_type=F32).astype(BF16)
    sent = jnp.broadcast_to(wetted[None], (n_same,) + wetted.shape)
    head, tail = call(
        edge_kernel, "edges", [edge_i16, edge_i16], [VMEM] * 2, [VMEM] * 2, 10**6, 2**20
    )(current[:halo], current[rows_dev - halo :])
    ones = jnp.ones((1, width), F32)
    previous, weight, square = None, ones, None
    for outer_no in range(OUTER):
        for degree_no in range(DEGREE):
            last = outer_no == OUTER - 1 and degree_no == DEGREE - 1
            rescale = outer_no > 0 and degree_no == 0
            gain = (1.0 if degree_no == 0 else 2.0) / radius
            before = None if degree_no == 0 else previous
            low = lax.ppermute(tail, both, forward)
            high = lax.ppermute(head, both, backward)
            same, other = gathered(sent, low)
            partial = mass_dot(same, other)
            dry, wet = stiff(low, current, high, before, weight, gain, -centre * gain, not last)
            parts = lax.all_to_all(partial, "col", split_axis=0, concat_axis=0, tiled=True)
            load, message = pack(parts, gain, wet, square if rescale else None)
            got = exchange(message.reshape(devices, -1, LANES)).reshape(-1, LANES)
            previous = current
            if not last:
                sent = wet_rows(got, lax.ppermute(load, both, to_in), rescale)
            current, head, tail, square, factor = shell(got, dry, rescale, last, degree_no == DEGREE - 1)
            weight = factor if rescale else ones
    squares = exchange(jnp.broadcast_to(square[None, :1, :], (devices, 1, width)))
    squares = jnp.sum(squares, axis=0)
    return current / jnp.sqrt(squares / total_rows + 1e-06)


def solution(mesh):
    placed = (
        P(("row", "col"), None),
        P(("row", "col"), None, None, None),
        P(("row", "col"), None),
        P(),
        P("row", "col"),
        P(),
        P(),
    )
    return jax.shard_map(
        body, mesh=mesh, in_specs=placed, out_specs=P(("row", "col"), None), check_vma=False
    )
```

```python
import functools

import jax
import jax.numpy as jnp
from jax import lax
from jax.experimental import pallas as pl
from jax.experimental.pallas import tpu as pltpu
from jax.sharding import PartitionSpec as P

DEGREE = 3
OUTER = 2
F32 = jnp.float32
BF16 = jnp.bfloat16
LANES = 128
PAD = 16
STEPS = 32000.0
VMEM = pl.BlockSpec(memory_space=pltpu.VMEM)
HBM = pl.BlockSpec(memory_space=pltpu.HBM)
ANY = pl.BlockSpec(memory_space=pl.ANY)
SMEM = pl.BlockSpec(memory_space=pltpu.SMEM)


def two_parts(value):
    hi = value.astype(BF16)
    return hi, (value - hi.astype(F32)).astype(BF16)


def choose(matrix, value):
    hi, lo = two_parts(value)
    picked = jnp.dot(matrix, hi, preferred_element_type=F32)
    return picked + jnp.dot(matrix, lo, preferred_element_type=F32)


def call(kernel, name, out_shape, in_specs, out_specs, flops, moved, scratch=(), limit=8):
    return pl.pallas_call(
        kernel,
        out_shape=out_shape,
        in_specs=in_specs,
        out_specs=out_specs,
        scratch_shapes=list(scratch),
        compiler_params=pltpu.CompilerParams(vmem_limit_bytes=limit * 2**20),
        cost_estimate=pl.CostEstimate(flops=flops, bytes_accessed=moved, transcendentals=0),
        name=name,
    )


def encode(value, out):
    rows = value.shape[0]
    top = jnp.maximum(jnp.max(jnp.abs(value), axis=0, keepdims=True), 1e-30)
    power = jnp.clip(jnp.ceil(jnp.log2(top)), -100.0, 126.0)
    steps = jnp.floor(value * (STEPS * jnp.exp2(-power)) + 0.5)
    out[0:rows, :] = steps.astype(jnp.int32).astype(jnp.int16)
    tail = jnp.broadcast_to(power, (PAD, value.shape[1]))
    out[rows : rows + PAD, :] = tail.astype(jnp.int32).astype(jnp.int16)


def decode(coded):
    rows = coded.shape[0] - PAD
    power = coded[rows : rows + PAD, :].astype(jnp.int32).astype(F32)[0:1]
    return coded[0:rows, :].astype(jnp.int32).astype(F32) * (jnp.exp2(power) * (1.0 / STEPS))


def edge_kernel(head, tail, head_out, tail_out):
    encode(head[...], head_out)
    encode(tail[...], tail_out)


def stiff_kernel(with_prev, with_wet, *refs):
    refs = list(refs)
    cols, k_hbm, low, here_hbm, high, scale, shift = refs[:7]
    del refs[:7]
    prev_hbm, weight = (refs.pop(0), refs.pop(0)) if with_prev else (None, None)
    pick = refs.pop(0) if with_wet else None
    out_hbm = refs.pop(0)
    wet = refs.pop(0) if with_wet else None
    k, here, prev, out, p_hi, p_lo, k_sem, here_sem, prev_sem, out_sem = refs
    rows = here.shape[0]
    size = k.shape[2]
    halo = low.shape[0] - PAD
    count = rows // size
    here_copy = pltpu.make_async_copy(here_hbm, here, here_sem)
    here_copy.start()
    row_copies = []
    for i in range(count):
        mine = pl.ds(i * size, size)
        row_copies.append([pltpu.make_async_copy(k_hbm.at[i], k.at[i], k_sem.at[i])])
        if with_prev:
            row_copies[i].append(
                pltpu.make_async_copy(prev_hbm.at[mine], prev.at[mine], prev_sem.at[i])
            )
        for copy in row_copies[i]:
            copy.start()

    def put(value, start):
        hi, lo = two_parts(value)
        p_hi[start : start + value.shape[0], :] = hi
        p_lo[start : start + value.shape[0], :] = lo

    put(decode(low), 0)
    put(decode(high), halo + rows)
    here_copy.wait()
    put(here[...], halo)
    out_copies = []
    for i in range(count):
        for copy in row_copies[i]:
            copy.wait()
        at = [pl.ds(pl.multiple_of(cols[i, j] * size, size), size) for j in range(k.shape[1])]
        k_parts = [two_parts(k[i, j]) for j in range(k.shape[1])]
        k_hi = jnp.concatenate([part[0] for part in k_parts], axis=1)
        k_lo = jnp.concatenate([part[1] for part in k_parts], axis=1)
        v_hi = jnp.concatenate([p_hi[rows_at, :] for rows_at in at], axis=0)
        v_lo = jnp.concatenate([p_lo[rows_at, :] for rows_at in at], axis=0)
        pair = jnp.dot(jnp.concatenate([k_hi, k_lo], axis=0), v_hi, preferred_element_type=F32)
        acc = pair[:size] + pair[size:] + jnp.dot(k_hi, v_lo, preferred_element_type=F32)
        mine = pl.ds(i * size, size)
        value = scale[...] * acc + shift[...] * here[mine, :]
        if with_prev:
            value = value - weight[...] * prev[mine, :]
        out[mine, :] = value
        copy = pltpu.make_async_copy(out.at[mine], out_hbm.at[mine], out_sem.at[i])
        copy.start()
        out_copies.append(copy)
    if with_wet:
        wet[...] = choose(pick[...], out[...])
    for copy in out_copies:
        copy.wait()


def pack_kernel(rescale, last, *refs):
    refs = list(refs)
    parts, gain, spread = refs[:3]
    del refs[:3]
    wet = None if last else refs.pop(0)
    square = refs.pop(0) if rescale else None
    load = None if last else refs.pop(0)
    message = refs.pop(0)
    total = decode(parts.at[0])
    for i in range(1, parts.shape[0]):
        total = total + decode(parts.at[i])
    total = total * gain[...]
    if not last:
        encode(total, load)
    sent = choose(spread[...], total)
    devices = sent.shape[0] // 2
    rows = message.shape[0] // devices
    for h in range(2):
        piece = slice(h * LANES, (h + 1) * LANES)
        for s in range(2):
            mine = slice(s * devices, (s + 1) * devices)
            message[pl.ds(4 * h + s, devices, stride=rows), :] = sent[mine, piece]
            if not last:
                message[pl.ds(4 * h + 2 + s, devices, stride=rows), :] = wet[mine, piece]
        if rescale:
            message[pl.ds(8 + h, devices, stride=rows), :] = jnp.broadcast_to(
                square[0:1, piece], (devices, LANES)
            )


def slot_rows(got, devices, first):
    rows = got.shape[0] // devices

    def one(s):
        halves = [got[pl.ds(4 * h + first + s, devices, stride=rows), :] for h in range(2)]
        return jnp.concatenate(halves, axis=1)

    return jnp.concatenate([one(0), one(1)], axis=0)


def factor_of(got, devices, total_rows):
    rows = got.shape[0] // devices
    halves = [
        jnp.sum(got[pl.ds(8 + h, devices, stride=rows), :], axis=0, keepdims=True) for h in range(2)
    ]
    return 1.0 / jnp.sqrt(jnp.concatenate(halves, axis=1) / total_rows + 1e-06)


def wet_kernel(rescale, total_rows, got, load, gather, sent):
    devices = gather.shape[1] // 2
    value = choose(gather[...], slot_rows(got, devices, 2)) + decode(load)
    if rescale:
        value = value * factor_of(got, devices, total_rows)
    value = value.astype(BF16)
    for i in range(sent.shape[0]):
        sent[i] = value


def shell_kernel(rescale, last, with_square, total_rows, *refs):
    refs = list(refs)
    got, dry_hbm, place = refs[:3]
    del refs[:3]
    out = refs.pop(0)
    head, tail = (None, None) if last else (refs.pop(0), refs.pop(0))
    square = refs.pop(0) if with_square else None
    factor_out = refs.pop(0) if rescale else None
    dry, sem = refs
    copy = pltpu.make_async_copy(dry_hbm, dry, sem)
    copy.start()
    devices = place.shape[1] // 2
    placed = choose(place[...], slot_rows(got, devices, 0))
    if rescale:
        factor = factor_of(got, devices, total_rows)
        factor_out[...] = factor
    copy.wait()
    value = dry[...] + placed
    if rescale:
        value = value * factor
    out[...] = value
    if not last:
        rows = head.shape[0] - PAD
        encode(value[:rows], head)
        encode(value[value.shape[0] - rows :], tail)
    if with_square:
        square[...] = jnp.broadcast_to(jnp.sum(value * value, axis=0, keepdims=True), square.shape)


def tie_kernel(value, other, out):
    pass


def fetch_kernel(earlier, mass_hbm, out, sems):
    chunk = mass_hbm.shape[0] // sems.shape[0]
    copies = []
    for i in range(sems.shape[0]):
        rows = pl.ds(i * chunk, chunk)
        copies.append(pltpu.make_async_copy(mass_hbm.at[rows], out.at[rows], sems.at[i]))
        copies[i].start()
    for copy in copies:
        copy.wait()


def dot_kernel(core, mass, same, other, out, panels):
    count, depth, _ = same.shape
    block = out.shape[1] - PAD
    chunk = 2 * block
    for j in range(count):
        at = pl.multiple_of((2 * j + core[0]) * depth, depth)
        panels[pl.ds(at, depth), :] = same[j]
        at = pl.multiple_of((2 * j + 1 - core[0]) * depth, depth)
        panels[pl.ds(at, depth), :] = other[j]
    for i in range(out.shape[0] // 2):
        value = jnp.dot(
            mass[i * chunk : (i + 1) * chunk, :], panels[...], preferred_element_type=F32
        )
        for j in range(2):
            encode(value[j * block : (j + 1) * block], out.at[2 * i + j])


def body(mode_block, k_blocks, block_cols, panel_node, added_mass, low_edge, high_edge):
    n_row = lax.axis_size("row")
    n_col = lax.axis_size("col")
    devices = n_row * n_col
    my_row = lax.axis_index("row")
    my_col = lax.axis_index("col")
    linear = my_row * n_col + my_col
    core = (my_row % 2).astype(jnp.int32).reshape(1)
    rows_dev, width = mode_block.shape
    size = k_blocks.shape[2]
    blocks_dev = rows_dev // size
    per_block = panel_node.shape[0] // devices
    slots = 2 * devices
    both = ("row", "col")

    panel_rows = panel_node.reshape(devices, per_block)
    source = panel_rows // rows_dev
    before = jnp.concatenate([jnp.full((devices, 1), -1, source.dtype), source[:, :-1]], axis=1)
    rank = (source == before).astype(jnp.int32)
    owned = source == linear
    local = panel_rows - linear * rows_dev
    first = jnp.max(jnp.where(owned & (rank == 0), local, -1), axis=1)
    second = jnp.max(jnp.where(owned & (rank == 1), local, -1), axis=1)
    by_block = jnp.stack([first, second], axis=0)
    by_target = by_block.reshape(2, n_col, n_row).transpose(0, 2, 1)
    shell_rows = jnp.arange(rows_dev, dtype=jnp.int32)
    pick = (by_target.reshape(slots, 1) == shell_rows[None, :]).astype(BF16)
    place = (shell_rows[:, None] == by_block.reshape(1, slots)).astype(BF16)
    flat = rank * devices + source
    slot_ids = jnp.arange(slots, dtype=jnp.int32)
    in_flat = lax.dynamic_index_in_dim(flat, my_col * n_row + my_row, 0, keepdims=False)
    out_flat = lax.dynamic_index_in_dim(flat, linear, 0, keepdims=False)
    gather_in = (in_flat[:, None] == slot_ids[None, :]).astype(BF16)
    spread_out = (slot_ids[:, None] == out_flat[None, :]).astype(BF16)

    cols = block_cols - (linear * blocks_dev - 2)
    halo = 2 * size
    n_same = n_row // 2
    same_core = [[i for i in range(n_row) if i % 2 == c] for c in range(2)]
    swap_core = [(i, i ^ 1) for i in range(n_row)]
    forward = [(i, i + 1) for i in range(devices - 1)]
    backward = [(i + 1, i) for i in range(devices - 1)]
    to_in = [(b, (b % n_row) * n_col + b // n_row) for b in range(devices)]

    block_f32 = jax.ShapeDtypeStruct((rows_dev, width), F32)
    wet_f32 = jax.ShapeDtypeStruct((slots, width), F32)
    row_f32 = jax.ShapeDtypeStruct((1, width), F32)
    eight_f32 = jax.ShapeDtypeStruct((8, width), F32)
    load_i16 = jax.ShapeDtypeStruct((per_block + PAD, width), jnp.int16)
    parts_i16 = jax.ShapeDtypeStruct((n_col, per_block + PAD, width), jnp.int16)
    edge_i16 = jax.ShapeDtypeStruct((halo + PAD, width), jnp.int16)
    sent_bf16 = jax.ShapeDtypeStruct((n_same, per_block, width), BF16)
    block_vmem = pltpu.VMEM((rows_dev, width), F32)
    padded = pltpu.VMEM((rows_dev + 2 * halo, width), BF16)
    dma = pltpu.SemaphoreType.DMA

    def stiff(low, current, high, previous, weight, scale, shift, with_wet):
        with_prev = previous is not None
        args = [cols, k_blocks, low, current, high, scale, shift]
        specs = [SMEM, HBM, VMEM, HBM, VMEM, VMEM, VMEM]
        if with_prev:
            args, specs = args + [previous, weight], specs + [HBM, VMEM]
        if with_wet:
            args, specs = args + [pick], specs + [VMEM]
        made = call(
            functools.partial(stiff_kernel, with_prev, with_wet), "stiff",
            [block_f32] + [wet_f32] * with_wet, specs, [HBM] + [VMEM] * with_wet,
            80 * 10**9, 8 * 2**20,
            [
                pltpu.VMEM(k_blocks.shape, F32), block_vmem, block_vmem, block_vmem, padded, padded,
                dma((blocks_dev,)), dma, dma((blocks_dev,)), dma((blocks_dev,)),
            ],
            52,
        )(*args)
        return (made[0], made[1] if with_wet else None)

    def fetch(earlier):
        return call(
            fetch_kernel, "fetch", pltpu.VMEM(added_mass.shape, BF16), [ANY, HBM], VMEM,
            10 * 10**9, 4 * 2**20, [dma((4,))], 48,
        )(earlier, added_mass)

    def mass_dot(mass, same, other):
        return call(
            dot_kernel, "mass_dot", parts_i16, [SMEM, VMEM, VMEM, VMEM], VMEM,
            2 * added_mass.size * width, 6 * 2**20,
            [pltpu.VMEM((added_mass.shape[1], width), BF16)], 48,
        )(core, mass, same, other)

    def pack(parts, gain, wet, square):
        rows = 8 if square is None else 16
        message = jax.ShapeDtypeStruct((rows * devices, LANES), F32)
        shapes = [message] if wet is None else [load_i16, message]
        args = [parts, gain, spread_out] + [v for v in (wet, square) if v is not None]
        made = call(
            functools.partial(pack_kernel, square is not None, wet is None), "pack",
            shapes, [VMEM] * len(args), [VMEM] * len(shapes), 10**8, 3 * 2**20,
        )(*args)
        return (None, made[0]) if wet is None else made

    def wet_rows(got, load, rescale):
        return call(
            functools.partial(wet_kernel, rescale, rows_dev * devices), "wet_rows", sent_bf16,
            [VMEM] * 3, VMEM, 10**8, 10**6,
        )(got, load, gather_in)

    def shell(got, dry, rescale, last, with_square):
        shapes = [block_f32] if last else [block_f32, edge_i16, edge_i16]
        shapes = shapes + [eight_f32] * with_square + [row_f32] * rescale
        made = list(call(
            functools.partial(shell_kernel, rescale, last, with_square, rows_dev * devices), "shell",
            shapes, [VMEM, HBM, VMEM], [VMEM] * len(shapes), 20 * 10**9, 4 * 2**20, [block_vmem, dma], 52,
        )(got, dry, place))
        current = made.pop(0)
        head, tail = (None, None) if last else (made.pop(0), made.pop(0))
        square = made.pop(0) if with_square else None
        return current, head, tail, square, made.pop(0) if rescale else None

    def tie(value, other):
        return pl.pallas_call(
            tie_kernel,
            out_shape=jax.ShapeDtypeStruct(value.shape, value.dtype),
            in_specs=[ANY, ANY],
            out_specs=ANY,
            input_output_aliases={0: 0},
            compiler_params=pltpu.CompilerParams(vmem_limit_bytes=4 * 2**20),
            cost_estimate=pl.CostEstimate(flops=0, bytes_accessed=0, transcendentals=0),
            name="tie",
        )(value, other)

    def exchange(message):
        return lax.all_to_all(message, both, split_axis=0, concat_axis=0, tiled=True)

    def gathered(sent, low):
        same = lax.all_to_all(
            sent, "row", split_axis=0, concat_axis=0, tiled=True, axis_index_groups=same_core
        )
        same = tie(same, low)
        return same, lax.ppermute(same, "row", swap_core)

    lower = low_edge.astype(F32) * 0.25
    upper = high_edge.astype(F32) * 0.25
    centre = (0.5 * (upper + lower))[None, :]
    radius = (0.5 * (upper - lower))[None, :]
    total_rows = rows_dev * devices

    current = mode_block
    start_rows = jnp.dot(pick, current.astype(BF16), preferred_element_type=F32)
    start_rows = start_rows.astype(BF16).reshape(2, devices, width).transpose(1, 0, 2)
    start_rows = exchange(start_rows).transpose(1, 0, 2).reshape(slots, width)
    wetted = jnp.dot(gather_in, start_rows, preferred_element_type=F32).astype(BF16)
    sent = jnp.broadcast_to(wetted[None], (n_same,) + wetted.shape)
    head, tail = call(
        edge_kernel, "edges", [edge_i16, edge_i16], [VMEM] * 2, [VMEM] * 2, 10**6, 2**20
    )(current[:halo], current[rows_dev - halo :])
    ones = jnp.ones((1, width), F32)
    previous, weight, square = None, ones, None
    got = start_rows
    for outer_no in range(OUTER):
        for degree_no in range(DEGREE):
            last = outer_no == OUTER - 1 and degree_no == DEGREE - 1
            rescale = outer_no > 0 and degree_no == 0
            gain = (1.0 if degree_no == 0 else 2.0) / radius
            before = None if degree_no == 0 else previous
            low = lax.ppermute(tail, both, forward)
            high = lax.ppermute(head, both, backward)
            mass = fetch(got)
            same, other = gathered(sent, low)
            partial = mass_dot(mass, same, other)
            dry, wet = stiff(low, current, high, before, weight, gain, -centre * gain, not last)
            parts = lax.all_to_all(partial, "col", split_axis=0, concat_axis=0, tiled=True)
            load, message = pack(parts, gain, wet, square if rescale else None)
            got = exchange(message.reshape(devices, -1, LANES)).reshape(-1, LANES)
            previous = current
            if not last:
                sent = wet_rows(got, lax.ppermute(load, both, to_in), rescale)
            current, head, tail, square, factor = shell(got, dry, rescale, last, degree_no == DEGREE - 1)
            weight = factor if rescale else ones
    squares = exchange(jnp.broadcast_to(square[None, :1, :], (devices, 1, width)))
    squares = jnp.sum(squares, axis=0)
    return current / jnp.sqrt(squares / total_rows + 1e-06)


def solution(mesh):
    placed = (
        P(("row", "col"), None),
        P(("row", "col"), None, None, None),
        P(("row", "col"), None),
        P(),
        P("row", "col"),
        P(),
        P(),
    )
    return jax.shard_map(
        body, mesh=mesh, in_specs=placed, out_specs=P(("row", "col"), None), check_vma=False
    )
```

```python
import functools

import jax
import jax.numpy as jnp
from jax import lax
from jax.experimental import pallas as pl
from jax.experimental.pallas import tpu as pltpu
from jax.sharding import PartitionSpec as P

DEGREE = 3
OUTER = 2
F32 = jnp.float32
BF16 = jnp.bfloat16
LANES = 128
PAD = 16
STEPS = 32000.0
VMEM = pl.BlockSpec(memory_space=pltpu.VMEM)
HBM = pl.BlockSpec(memory_space=pltpu.HBM)
ANY = pl.BlockSpec(memory_space=pl.ANY)
SMEM = pl.BlockSpec(memory_space=pltpu.SMEM)


def two_parts(value):
    hi = value.astype(BF16)
    return hi, (value - hi.astype(F32)).astype(BF16)


def choose(matrix, value):
    hi, lo = two_parts(value)
    picked = jnp.dot(matrix, hi, preferred_element_type=F32)
    return picked + jnp.dot(matrix, lo, preferred_element_type=F32)


def call(kernel, name, out_shape, in_specs, out_specs, flops, moved, scratch=(), limit=8):
    return pl.pallas_call(
        kernel,
        out_shape=out_shape,
        in_specs=in_specs,
        out_specs=out_specs,
        scratch_shapes=list(scratch),
        compiler_params=pltpu.CompilerParams(vmem_limit_bytes=limit * 2**20),
        cost_estimate=pl.CostEstimate(flops=flops, bytes_accessed=moved, transcendentals=0),
        name=name,
    )


def encode(value, out):
    rows = value.shape[0]
    top = jnp.maximum(jnp.max(jnp.abs(value), axis=0, keepdims=True), 1e-30)
    power = jnp.clip(jnp.ceil(jnp.log2(top)), -100.0, 126.0)
    steps = jnp.floor(value * (STEPS * jnp.exp2(-power)) + 0.5)
    out[0:rows, :] = steps.astype(jnp.int32).astype(jnp.int16)
    tail = jnp.broadcast_to(power, (PAD, value.shape[1]))
    out[rows : rows + PAD, :] = tail.astype(jnp.int32).astype(jnp.int16)


def decode(coded):
    rows = coded.shape[0] - PAD
    power = coded[rows : rows + PAD, :].astype(jnp.int32).astype(F32)[0:1]
    return coded[0:rows, :].astype(jnp.int32).astype(F32) * (jnp.exp2(power) * (1.0 / STEPS))


def edge_kernel(head, tail, head_out, tail_out):
    encode(head[...], head_out)
    encode(tail[...], tail_out)


def stiff_kernel(with_prev, with_wet, *refs):
    refs = list(refs)
    cols, k_hbm, low, here_hbm, high, scale, shift = refs[:7]
    del refs[:7]
    prev_hbm, weight = (refs.pop(0), refs.pop(0)) if with_prev else (None, None)
    pick = refs.pop(0) if with_wet else None
    out_hbm = refs.pop(0)
    wet = refs.pop(0) if with_wet else None
    k, here, prev, out, p_hi, p_lo, k_sem, here_sem, prev_sem, out_sem = refs
    rows = here.shape[0]
    size = k.shape[2]
    halo = low.shape[0] - PAD
    count = rows // size
    here_copy = pltpu.make_async_copy(here_hbm, here, here_sem)
    here_copy.start()
    row_copies = []
    for i in range(count):
        mine = pl.ds(i * size, size)
        row_copies.append([pltpu.make_async_copy(k_hbm.at[i], k.at[i], k_sem.at[i])])
        if with_prev:
            row_copies[i].append(
                pltpu.make_async_copy(prev_hbm.at[mine], prev.at[mine], prev_sem.at[i])
            )
        for copy in row_copies[i]:
            copy.start()

    def put(value, start):
        hi, lo = two_parts(value)
        p_hi[start : start + value.shape[0], :] = hi
        p_lo[start : start + value.shape[0], :] = lo

    put(decode(low), 0)
    put(decode(high), halo + rows)
    here_copy.wait()
    put(here[...], halo)
    out_copies = []
    for i in range(count):
        for copy in row_copies[i]:
            copy.wait()
        at = [pl.ds(pl.multiple_of(cols[i, j] * size, size), size) for j in range(k.shape[1])]
        k_parts = [two_parts(k[i, j]) for j in range(k.shape[1])]
        k_hi = jnp.concatenate([part[0] for part in k_parts], axis=1)
        k_lo = jnp.concatenate([part[1] for part in k_parts], axis=1)
        v_hi = jnp.concatenate([p_hi[rows_at, :] for rows_at in at], axis=0)
        v_lo = jnp.concatenate([p_lo[rows_at, :] for rows_at in at], axis=0)
        pair = jnp.dot(jnp.concatenate([k_hi, k_lo], axis=0), v_hi, preferred_element_type=F32)
        acc = pair[:size] + pair[size:] + jnp.dot(k_hi, v_lo, preferred_element_type=F32)
        mine = pl.ds(i * size, size)
        value = scale[...] * acc + shift[...] * here[mine, :]
        if with_prev:
            value = value - weight[...] * prev[mine, :]
        out[mine, :] = value
        copy = pltpu.make_async_copy(out.at[mine], out_hbm.at[mine], out_sem.at[i])
        copy.start()
        out_copies.append(copy)
    if with_wet:
        wet[...] = choose(pick[...], out[...])
    for copy in out_copies:
        copy.wait()


def pack_kernel(rescale, last, *refs):
    refs = list(refs)
    parts, gain, spread, wet = refs[:4]
    del refs[:4]
    square = refs.pop(0) if rescale else None
    load = None if last else refs.pop(0)
    message = refs.pop(0)
    total = decode(parts.at[0])
    for i in range(1, parts.shape[0]):
        total = total + decode(parts.at[i])
    total = total * gain[...]
    if not last:
        encode(total, load)
    sent = choose(spread[...], total)
    devices = sent.shape[0] // 2
    rows = message.shape[0] // devices
    for h in range(2):
        piece = slice(h * LANES, (h + 1) * LANES)
        for s in range(2):
            mine = slice(s * devices, (s + 1) * devices)
            message[pl.ds((2 if last else 4) * h + s, devices, stride=rows), :] = sent[mine, piece]
            if not last:
                message[pl.ds(4 * h + 2 + s, devices, stride=rows), :] = wet[mine, piece]
        if rescale:
            message[pl.ds(8 + h, devices, stride=rows), :] = jnp.broadcast_to(
                square[0:1, piece], (devices, LANES)
            )


def slot_rows(got, devices, first):
    rows = got.shape[0] // devices
    half = min(rows // 2, 4)

    def one(s):
        halves = [got[pl.ds(half * h + first + s, devices, stride=rows), :] for h in range(2)]
        return jnp.concatenate(halves, axis=1)

    return jnp.concatenate([one(0), one(1)], axis=0)


def factor_of(got, devices, total_rows):
    rows = got.shape[0] // devices
    halves = [
        jnp.sum(got[pl.ds(8 + h, devices, stride=rows), :], axis=0, keepdims=True) for h in range(2)
    ]
    return 1.0 / jnp.sqrt(jnp.concatenate(halves, axis=1) / total_rows + 1e-06)


def wet_kernel(rescale, total_rows, got, load, gather, sent):
    devices = gather.shape[1] // 2
    value = choose(gather[...], slot_rows(got, devices, 2)) + decode(load)
    if rescale:
        value = value * factor_of(got, devices, total_rows)
    value = value.astype(BF16)
    for i in range(sent.shape[0]):
        sent[i] = value


def shell_kernel(rescale, last, with_square, total_rows, *refs):
    refs = list(refs)
    got, dry_hbm, place = refs[:3]
    del refs[:3]
    out_hbm = refs.pop(0)
    head, tail = (None, None) if last else (refs.pop(0), refs.pop(0))
    square = refs.pop(0) if with_square else None
    factor_out = refs.pop(0) if rescale else None
    dry, out, in_sem, out_sem = refs
    count = in_sem.shape[0]
    chunk = dry.shape[0] // count
    order = [0, count - 1, *range(1, count - 1)]
    ins, outs = {}, {}
    for i in order:
        mine = pl.ds(i * chunk, chunk)
        ins[i] = pltpu.make_async_copy(dry_hbm.at[mine], dry.at[mine], in_sem.at[i])
        ins[i].start()
        outs[i] = pltpu.make_async_copy(out.at[mine], out_hbm.at[mine], out_sem.at[i])
    devices = place.shape[1] // 2
    hi, lo = two_parts(slot_rows(got, devices, 0))
    if rescale:
        factor = factor_of(got, devices, total_rows)
        factor_out[...] = factor
    squares = None
    for i in order:
        mine = pl.ds(i * chunk, chunk)
        matrix = place[mine, :]
        value = jnp.dot(matrix, hi, preferred_element_type=F32)
        value = value + jnp.dot(matrix, lo, preferred_element_type=F32)
        ins[i].wait()
        value = dry[mine, :] + value
        if rescale:
            value = value * factor
        out[mine, :] = value
        outs[i].start()
        if not last and i == 0:
            encode(value, head)
        if not last and i == count - 1:
            encode(value, tail)
        if with_square:
            more = jnp.sum(value * value, axis=0, keepdims=True)
            squares = more if squares is None else squares + more
    if with_square:
        square[...] = jnp.broadcast_to(squares, square.shape)
    for i in order:
        outs[i].wait()


def tie_kernel(value, other, out):
    pass


def fetch_kernel(earlier, mass_hbm, out, sems):
    chunk = mass_hbm.shape[0] // sems.shape[0]
    copies = []
    for i in range(sems.shape[0]):
        rows = pl.ds(i * chunk, chunk)
        copies.append(pltpu.make_async_copy(mass_hbm.at[rows], out.at[rows], sems.at[i]))
        copies[i].start()
    for copy in copies:
        copy.wait()


def dot_kernel(core, mass, same, other, out, panels):
    count, depth, _ = same.shape
    block = out.shape[1] - PAD
    chunk = 2 * block
    for j in range(count):
        at = pl.multiple_of((2 * j + core[0]) * depth, depth)
        panels[pl.ds(at, depth), :] = same[j]
        at = pl.multiple_of((2 * j + 1 - core[0]) * depth, depth)
        panels[pl.ds(at, depth), :] = other[j]
    for i in range(out.shape[0] // 2):
        value = jnp.dot(
            mass[i * chunk : (i + 1) * chunk, :], panels[...], preferred_element_type=F32
        )
        for j in range(2):
            encode(value[j * block : (j + 1) * block], out.at[2 * i + j])


def body(mode_block, k_blocks, block_cols, panel_node, added_mass, low_edge, high_edge):
    n_row = lax.axis_size("row")
    n_col = lax.axis_size("col")
    devices = n_row * n_col
    my_row = lax.axis_index("row")
    my_col = lax.axis_index("col")
    linear = my_row * n_col + my_col
    core = (my_row % 2).astype(jnp.int32).reshape(1)
    rows_dev, width = mode_block.shape
    size = k_blocks.shape[2]
    blocks_dev = rows_dev // size
    per_block = panel_node.shape[0] // devices
    slots = 2 * devices
    both = ("row", "col")

    panel_rows = panel_node.reshape(devices, per_block)
    source = panel_rows // rows_dev
    before = jnp.concatenate([jnp.full((devices, 1), -1, source.dtype), source[:, :-1]], axis=1)
    rank = (source == before).astype(jnp.int32)
    owned = source == linear
    local = panel_rows - linear * rows_dev
    first = jnp.max(jnp.where(owned & (rank == 0), local, -1), axis=1)
    second = jnp.max(jnp.where(owned & (rank == 1), local, -1), axis=1)
    by_block = jnp.stack([first, second], axis=0)
    by_target = by_block.reshape(2, n_col, n_row).transpose(0, 2, 1)
    shell_rows = jnp.arange(rows_dev, dtype=jnp.int32)
    pick = (by_target.reshape(slots, 1) == shell_rows[None, :]).astype(BF16)
    place = (shell_rows[:, None] == by_block.reshape(1, slots)).astype(BF16)
    flat = rank * devices + source
    slot_ids = jnp.arange(slots, dtype=jnp.int32)
    in_flat = lax.dynamic_index_in_dim(flat, my_col * n_row + my_row, 0, keepdims=False)
    out_flat = lax.dynamic_index_in_dim(flat, linear, 0, keepdims=False)
    gather_in = (in_flat[:, None] == slot_ids[None, :]).astype(BF16)
    spread_out = (slot_ids[:, None] == out_flat[None, :]).astype(BF16)

    cols = block_cols - (linear * blocks_dev - 2)
    halo = 2 * size
    n_same = n_row // 2
    same_core = [[i for i in range(n_row) if i % 2 == c] for c in range(2)]
    swap_core = [(i, i ^ 1) for i in range(n_row)]
    forward = [(i, i + 1) for i in range(devices - 1)]
    backward = [(i + 1, i) for i in range(devices - 1)]
    to_in = [(b, (b % n_row) * n_col + b // n_row) for b in range(devices)]

    block_f32 = jax.ShapeDtypeStruct((rows_dev, width), F32)
    wet_f32 = jax.ShapeDtypeStruct((slots, width), F32)
    row_f32 = jax.ShapeDtypeStruct((1, width), F32)
    eight_f32 = jax.ShapeDtypeStruct((8, width), F32)
    load_i16 = jax.ShapeDtypeStruct((per_block + PAD, width), jnp.int16)
    parts_i16 = jax.ShapeDtypeStruct((n_col, per_block + PAD, width), jnp.int16)
    edge_i16 = jax.ShapeDtypeStruct((halo + PAD, width), jnp.int16)
    sent_bf16 = jax.ShapeDtypeStruct((n_same, per_block, width), BF16)
    block_vmem = pltpu.VMEM((rows_dev, width), F32)
    padded = pltpu.VMEM((rows_dev + 2 * halo, width), BF16)
    dma = pltpu.SemaphoreType.DMA

    def stiff(low, current, high, previous, weight, scale, shift, with_wet):
        with_prev = previous is not None
        args = [cols, k_blocks, low, current, high, scale, shift]
        specs = [SMEM, HBM, VMEM, HBM, VMEM, VMEM, VMEM]
        if with_prev:
            args, specs = args + [previous, weight], specs + [HBM, VMEM]
        if with_wet:
            args, specs = args + [pick], specs + [VMEM]
        made = call(
            functools.partial(stiff_kernel, with_prev, with_wet), "stiff",
            [block_f32] + [wet_f32] * with_wet, specs, [HBM] + [VMEM] * with_wet,
            80 * 10**9, 8 * 2**20,
            [
                pltpu.VMEM(k_blocks.shape, F32), block_vmem, block_vmem, block_vmem, padded, padded,
                dma((blocks_dev,)), dma, dma((blocks_dev,)), dma((blocks_dev,)),
            ],
            52,
        )(*args)
        return (made[0], made[1] if with_wet else None)

    def fetch(earlier):
        return call(
            fetch_kernel, "fetch", pltpu.VMEM(added_mass.shape, BF16), [ANY, HBM], VMEM,
            10 * 10**9, 4 * 2**20, [dma((4,))], 48,
        )(earlier, added_mass)

    def mass_dot(mass, same, other):
        return call(
            dot_kernel, "mass_dot", parts_i16, [SMEM, VMEM, VMEM, VMEM], VMEM,
            2 * added_mass.size * width, 6 * 2**20,
            [pltpu.VMEM((added_mass.shape[1], width), BF16)], 48,
        )(core, mass, same, other)

    def pack(parts, gain, wet, square, last):
        rows = 4 if last else 8 if square is None else 16
        message = jax.ShapeDtypeStruct((rows * devices, LANES), F32)
        shapes = [message] if last else [load_i16, message]
        args = [parts, gain, spread_out, wet] + ([] if square is None else [square])
        specs = [VMEM] * 3 + [ANY if last else VMEM] + [VMEM] * (len(args) - 4)
        made = call(
            functools.partial(pack_kernel, square is not None, last), "pack",
            shapes, specs, [VMEM] * len(shapes), 10**8, 3 * 2**20, (), 52 if last else 8,
        )(*args)
        return (None, made[0]) if last else made

    def wet_rows(got, load, rescale):
        return call(
            functools.partial(wet_kernel, rescale, rows_dev * devices), "wet_rows", sent_bf16,
            [VMEM] * 3, VMEM, 10**8, 10**6,
        )(got, load, gather_in)

    def shell(got, dry, rescale, last, with_square):
        shapes = [block_f32] if last else [block_f32, edge_i16, edge_i16]
        shapes = shapes + [eight_f32] * with_square + [row_f32] * rescale
        made = list(call(
            functools.partial(shell_kernel, rescale, last, with_square, rows_dev * devices), "shell",
            shapes, [VMEM, HBM, VMEM], [HBM] + [VMEM] * (len(shapes) - 1), 20 * 10**9, 4 * 2**20,
            [block_vmem, block_vmem, dma((rows_dev // halo,)), dma((rows_dev // halo,))], 52,
        )(got, dry, place))
        current = made.pop(0)
        head, tail = (None, None) if last else (made.pop(0), made.pop(0))
        square = made.pop(0) if with_square else None
        return current, head, tail, square, made.pop(0) if rescale else None

    def tie(value, other):
        return pl.pallas_call(
            tie_kernel,
            out_shape=jax.ShapeDtypeStruct(value.shape, value.dtype),
            in_specs=[ANY, ANY],
            out_specs=ANY,
            input_output_aliases={0: 0},
            compiler_params=pltpu.CompilerParams(vmem_limit_bytes=4 * 2**20),
            cost_estimate=pl.CostEstimate(flops=0, bytes_accessed=0, transcendentals=0),
            name="tie",
        )(value, other)

    def exchange(message):
        return lax.all_to_all(message, both, split_axis=0, concat_axis=0, tiled=True)

    def gathered(sent, low):
        same = lax.all_to_all(
            sent, "row", split_axis=0, concat_axis=0, tiled=True, axis_index_groups=same_core
        )
        same = tie(same, low)
        return same, lax.ppermute(same, "row", swap_core)

    lower = low_edge.astype(F32) * 0.25
    upper = high_edge.astype(F32) * 0.25
    centre = (0.5 * (upper + lower))[None, :]
    radius = (0.5 * (upper - lower))[None, :]
    total_rows = rows_dev * devices

    current = mode_block
    start_rows = jnp.dot(pick, current.astype(BF16), preferred_element_type=F32)
    start_rows = start_rows.astype(BF16).reshape(2, devices, width).transpose(1, 0, 2)
    start_rows = exchange(start_rows).transpose(1, 0, 2).reshape(slots, width)
    wetted = jnp.dot(gather_in, start_rows, preferred_element_type=F32).astype(BF16)
    sent = jnp.broadcast_to(wetted[None], (n_same,) + wetted.shape)
    head, tail = call(
        edge_kernel, "edges", [edge_i16, edge_i16], [VMEM] * 2, [VMEM] * 2, 10**6, 2**20
    )(current[:halo], current[rows_dev - halo :])
    ones = jnp.ones((1, width), F32)
    previous, weight, square = None, ones, None
    got = start_rows
    for outer_no in range(OUTER):
        for degree_no in range(DEGREE):
            last = outer_no == OUTER - 1 and degree_no == DEGREE - 1
            rescale = outer_no > 0 and degree_no == 0
            gain = (1.0 if degree_no == 0 else 2.0) / radius
            before = None if degree_no == 0 else previous
            low = lax.ppermute(tail, both, forward)
            high = lax.ppermute(head, both, backward)
            mass = fetch(got)
            same, other = gathered(sent, low)
            partial = mass_dot(mass, same, other)
            dry, wet = stiff(low, current, high, before, weight, gain, -centre * gain, not last)
            parts = lax.all_to_all(partial, "col", split_axis=0, concat_axis=0, tiled=True)
            load, message = pack(parts, gain, dry if last else wet, square if rescale else None, last)
            got = exchange(message.reshape(devices, -1, LANES)).reshape(-1, LANES)
            previous = current
            if not last:
                sent = wet_rows(got, lax.ppermute(load, both, to_in), rescale)
            current, head, tail, square, factor = shell(got, dry, rescale, last, degree_no == DEGREE - 1)
            weight = factor if rescale else ones
    squares = exchange(jnp.broadcast_to(square[None, :1, :], (devices, 1, width)))
    squares = jnp.sum(squares, axis=0)
    return current / jnp.sqrt(squares / total_rows + 1e-06)


def solution(mesh):
    placed = (
        P(("row", "col"), None),
        P(("row", "col"), None, None, None),
        P(("row", "col"), None),
        P(),
        P("row", "col"),
        P(),
        P(),
    )
    return jax.shard_map(
        body, mesh=mesh, in_specs=placed, out_specs=P(("row", "col"), None), check_vma=False
    )
```

```python
import functools

import jax
import jax.numpy as jnp
from jax import lax
from jax.experimental import pallas as pl
from jax.experimental.pallas import tpu as pltpu
from jax.sharding import PartitionSpec as P

DEGREE = 3
OUTER = 2
F32 = jnp.float32
BF16 = jnp.bfloat16
LANES = 128
PAD = 16
STEPS = 32000.0
SMALL = 2.0**-20
VMEM = pl.BlockSpec(memory_space=pltpu.VMEM)
HBM = pl.BlockSpec(memory_space=pltpu.HBM)
ANY = pl.BlockSpec(memory_space=pl.ANY)
SMEM = pl.BlockSpec(memory_space=pltpu.SMEM)


def two_parts(value):
    hi = value.astype(BF16)
    return hi, (value - hi.astype(F32)).astype(BF16)


def choose(matrix, value):
    hi, lo = two_parts(value)
    picked = jnp.dot(matrix, hi, preferred_element_type=F32)
    return picked + jnp.dot(matrix, lo, preferred_element_type=F32)


def call(kernel, name, out_shape, in_specs, out_specs, flops, moved, scratch=(), limit=8):
    return pl.pallas_call(
        kernel,
        out_shape=out_shape,
        in_specs=in_specs,
        out_specs=out_specs,
        scratch_shapes=list(scratch),
        compiler_params=pltpu.CompilerParams(vmem_limit_bytes=limit * 2**20),
        cost_estimate=pl.CostEstimate(flops=flops, bytes_accessed=moved, transcendentals=0),
        name=name,
    )


def encode(value, out):
    rows = value.shape[0]
    top = jnp.maximum(jnp.max(jnp.abs(value), axis=0, keepdims=True), 1e-30)
    power = jnp.clip(jnp.ceil(jnp.log2(top)), -100.0, 126.0)
    steps = jnp.floor(value * (STEPS * jnp.exp2(-power)) + 0.5)
    out[0:rows, :] = steps.astype(jnp.int32).astype(jnp.int16)
    tail = jnp.broadcast_to(power, (PAD, value.shape[1]))
    out[rows : rows + PAD, :] = tail.astype(jnp.int32).astype(jnp.int16)


def decode(coded):
    rows = coded.shape[0] - PAD
    power = coded[rows : rows + PAD, :].astype(jnp.int32).astype(F32)[0:1]
    return coded[0:rows, :].astype(jnp.int32).astype(F32) * (jnp.exp2(power) * (1.0 / STEPS))


def edge_kernel(head, tail, head_out, tail_out):
    encode(head[...], head_out)
    encode(tail[...], tail_out)


def stiff_kernel(with_prev, with_wet, *refs):
    refs = list(refs)
    cols, k_hbm, low, here_hbm, high, scale, shift = refs[:7]
    del refs[:7]
    prev_hbm = refs.pop(0) if with_prev else None
    pick = refs.pop(0) if with_wet else None
    out_hbm = refs.pop(0)
    wet = refs.pop(0) if with_wet else None
    k, here, prev, out, p_hi, p_lo, k_sem, here_sem, prev_sem, out_sem = refs
    rows = here.shape[0]
    size = k.shape[2]
    halo = low.shape[0] - PAD
    count = rows // size
    here_copy = pltpu.make_async_copy(here_hbm, here, here_sem)
    here_copy.start()
    row_copies = []
    for i in range(count):
        mine = pl.ds(i * size, size)
        row_copies.append([pltpu.make_async_copy(k_hbm.at[i], k.at[i], k_sem.at[i])])
        if with_prev:
            row_copies[i].append(
                pltpu.make_async_copy(prev_hbm.at[mine], prev.at[mine], prev_sem.at[i])
            )
        for copy in row_copies[i]:
            copy.start()

    def put(value, start):
        hi, lo = two_parts(value)
        p_hi[start : start + value.shape[0], :] = hi
        p_lo[start : start + value.shape[0], :] = lo

    put(decode(low), 0)
    put(decode(high), halo + rows)
    here_copy.wait()
    put(here[...], halo)
    out_copies = []
    for i in range(count):
        for copy in row_copies[i]:
            copy.wait()
        at = [pl.ds(pl.multiple_of(cols[i, j] * size, size), size) for j in range(k.shape[1])]
        k_parts = [two_parts(k[i, j]) for j in range(k.shape[1])]
        k_hi = jnp.concatenate([part[0] for part in k_parts], axis=1)
        k_lo = jnp.concatenate([part[1] for part in k_parts], axis=1)
        v_hi = jnp.concatenate([p_hi[rows_at, :] for rows_at in at], axis=0)
        v_lo = jnp.concatenate([p_lo[rows_at, :] for rows_at in at], axis=0)
        pair = jnp.dot(jnp.concatenate([k_hi, k_lo], axis=0), v_hi, preferred_element_type=F32)
        acc = pair[:size] + pair[size:] + jnp.dot(k_hi, v_lo, preferred_element_type=F32)
        mine = pl.ds(i * size, size)
        value = scale[...] * acc + shift[...] * here[mine, :]
        if with_prev:
            value = value - prev[mine, :]
        out[mine, :] = value
        copy = pltpu.make_async_copy(out.at[mine], out_hbm.at[mine], out_sem.at[i])
        copy.start()
        out_copies.append(copy)
    if with_wet:
        wet[...] = choose(pick[...], out[...])
    for copy in out_copies:
        copy.wait()


def pack_kernel(last, *refs):
    refs = list(refs)
    parts, gain, spread, wet = refs[:4]
    del refs[:4]
    load = None if last else refs.pop(0)
    message = refs.pop(0)
    total = decode(parts.at[0])
    for i in range(1, parts.shape[0]):
        total = total + decode(parts.at[i])
    total = total * gain[...]
    if not last:
        encode(total, load)
    sent = choose(spread[...], total)
    devices = sent.shape[0] // 2
    rows = message.shape[0] // devices
    for h in range(2):
        piece = slice(h * LANES, (h + 1) * LANES)
        for s in range(2):
            mine = slice(s * devices, (s + 1) * devices)
            message[pl.ds((2 if last else 4) * h + s, devices, stride=rows), :] = sent[mine, piece]
            if not last:
                message[pl.ds(4 * h + 2 + s, devices, stride=rows), :] = wet[mine, piece]


def slot_rows(got, devices, first):
    rows = got.shape[0] // devices
    half = min(rows // 2, 4)

    def one(s):
        halves = [got[pl.ds(half * h + first + s, devices, stride=rows), :] for h in range(2)]
        return jnp.concatenate(halves, axis=1)

    return jnp.concatenate([one(0), one(1)], axis=0)


def wet_kernel(got, load, gather, sent):
    devices = gather.shape[1] // 2
    value = choose(gather[...], slot_rows(got, devices, 2)) + decode(load)
    value = value.astype(BF16)
    for i in range(sent.shape[0]):
        sent[i] = value


def shell_kernel(last, with_square, small, *refs):
    refs = list(refs)
    got, dry_hbm, place = refs[:3]
    del refs[:3]
    out_hbm = refs.pop(0)
    head, tail = (None, None) if last else (refs.pop(0), refs.pop(0))
    square = refs.pop(0) if with_square else None
    dry, out, in_sem, out_sem = refs
    count = in_sem.shape[0]
    chunk = dry.shape[0] // count
    order = [0, count - 1, *range(1, count - 1)]
    ins, outs = {}, {}
    for i in order:
        mine = pl.ds(i * chunk, chunk)
        ins[i] = pltpu.make_async_copy(dry_hbm.at[mine], dry.at[mine], in_sem.at[i])
        ins[i].start()
        outs[i] = pltpu.make_async_copy(out.at[mine], out_hbm.at[mine], out_sem.at[i])
    devices = place.shape[1] // 2
    hi, lo = two_parts(slot_rows(got, devices, 0))
    squares = None
    for i in order:
        mine = pl.ds(i * chunk, chunk)
        matrix = place[mine, :]
        value = jnp.dot(matrix, hi, preferred_element_type=F32)
        value = value + jnp.dot(matrix, lo, preferred_element_type=F32)
        ins[i].wait()
        value = dry[mine, :] + value
        out[mine, :] = value
        outs[i].start()
        if not last and i == 0:
            encode(value, head)
        if not last and i == count - 1:
            encode(value, tail)
        if with_square:
            scaled = value * small
            more = jnp.sum(scaled * scaled, axis=0, keepdims=True)
            squares = more if squares is None else squares + more
    if with_square:
        square[...] = jnp.broadcast_to(squares, square.shape)
    for i in order:
        outs[i].wait()


def tie_kernel(value, other, out):
    pass


def fetch_kernel(earlier, mass_hbm, out, sems):
    chunk = mass_hbm.shape[0] // sems.shape[0]
    copies = []
    for i in range(sems.shape[0]):
        rows = pl.ds(i * chunk, chunk)
        copies.append(pltpu.make_async_copy(mass_hbm.at[rows], out.at[rows], sems.at[i]))
        copies[i].start()
    for copy in copies:
        copy.wait()


def dot_kernel(core, mass, same, other, out, panels):
    count, depth, _ = same.shape
    block = out.shape[1] - PAD
    chunk = 2 * block
    for j in range(count):
        at = pl.multiple_of((2 * j + core[0]) * depth, depth)
        panels[pl.ds(at, depth), :] = same[j]
        at = pl.multiple_of((2 * j + 1 - core[0]) * depth, depth)
        panels[pl.ds(at, depth), :] = other[j]
    for i in range(out.shape[0] // 2):
        value = jnp.dot(
            mass[i * chunk : (i + 1) * chunk, :], panels[...], preferred_element_type=F32
        )
        for j in range(2):
            encode(value[j * block : (j + 1) * block], out.at[2 * i + j])


def body(mode_block, k_blocks, block_cols, panel_node, added_mass, low_edge, high_edge):
    n_row = lax.axis_size("row")
    n_col = lax.axis_size("col")
    devices = n_row * n_col
    my_row = lax.axis_index("row")
    my_col = lax.axis_index("col")
    linear = my_row * n_col + my_col
    core = (my_row % 2).astype(jnp.int32).reshape(1)
    rows_dev, width = mode_block.shape
    size = k_blocks.shape[2]
    blocks_dev = rows_dev // size
    per_block = panel_node.shape[0] // devices
    slots = 2 * devices
    both = ("row", "col")

    panel_rows = panel_node.reshape(devices, per_block)
    source = panel_rows // rows_dev
    before = jnp.concatenate([jnp.full((devices, 1), -1, source.dtype), source[:, :-1]], axis=1)
    rank = (source == before).astype(jnp.int32)
    owned = source == linear
    local = panel_rows - linear * rows_dev
    first = jnp.max(jnp.where(owned & (rank == 0), local, -1), axis=1)
    second = jnp.max(jnp.where(owned & (rank == 1), local, -1), axis=1)
    by_block = jnp.stack([first, second], axis=0)
    by_target = by_block.reshape(2, n_col, n_row).transpose(0, 2, 1)
    shell_rows = jnp.arange(rows_dev, dtype=jnp.int32)
    pick = (by_target.reshape(slots, 1) == shell_rows[None, :]).astype(BF16)
    place = (shell_rows[:, None] == by_block.reshape(1, slots)).astype(BF16)
    flat = rank * devices + source
    slot_ids = jnp.arange(slots, dtype=jnp.int32)
    in_flat = lax.dynamic_index_in_dim(flat, my_col * n_row + my_row, 0, keepdims=False)
    out_flat = lax.dynamic_index_in_dim(flat, linear, 0, keepdims=False)
    gather_in = (in_flat[:, None] == slot_ids[None, :]).astype(BF16)
    spread_out = (slot_ids[:, None] == out_flat[None, :]).astype(BF16)

    cols = block_cols - (linear * blocks_dev - 2)
    halo = 2 * size
    n_same = n_row // 2
    same_core = [[i for i in range(n_row) if i % 2 == c] for c in range(2)]
    swap_core = [(i, i ^ 1) for i in range(n_row)]
    forward = [(i, i + 1) for i in range(devices - 1)]
    backward = [(i + 1, i) for i in range(devices - 1)]
    to_in = [(b, (b % n_row) * n_col + b // n_row) for b in range(devices)]

    block_f32 = jax.ShapeDtypeStruct((rows_dev, width), F32)
    wet_f32 = jax.ShapeDtypeStruct((slots, width), F32)
    eight_f32 = jax.ShapeDtypeStruct((8, width), F32)
    load_i16 = jax.ShapeDtypeStruct((per_block + PAD, width), jnp.int16)
    parts_i16 = jax.ShapeDtypeStruct((n_col, per_block + PAD, width), jnp.int16)
    edge_i16 = jax.ShapeDtypeStruct((halo + PAD, width), jnp.int16)
    sent_bf16 = jax.ShapeDtypeStruct((n_same, per_block, width), BF16)
    block_vmem = pltpu.VMEM((rows_dev, width), F32)
    padded = pltpu.VMEM((rows_dev + 2 * halo, width), BF16)
    dma = pltpu.SemaphoreType.DMA

    def stiff(low, current, high, previous, scale, shift, with_wet):
        with_prev = previous is not None
        args = [cols, k_blocks, low, current, high, scale, shift]
        specs = [SMEM, HBM, VMEM, HBM, VMEM, VMEM, VMEM]
        if with_prev:
            args, specs = args + [previous], specs + [HBM]
        if with_wet:
            args, specs = args + [pick], specs + [VMEM]
        made = call(
            functools.partial(stiff_kernel, with_prev, with_wet), "stiff",
            [block_f32] + [wet_f32] * with_wet, specs, [HBM] + [VMEM] * with_wet,
            80 * 10**9, 8 * 2**20,
            [
                pltpu.VMEM(k_blocks.shape, F32), block_vmem, block_vmem, block_vmem, padded, padded,
                dma((blocks_dev,)), dma, dma((blocks_dev,)), dma((blocks_dev,)),
            ],
            52,
        )(*args)
        return (made[0], made[1] if with_wet else None)

    def fetch(earlier):
        return call(
            fetch_kernel, "fetch", pltpu.VMEM(added_mass.shape, BF16), [ANY, HBM], VMEM,
            10 * 10**9, 4 * 2**20, [dma((4,))], 48,
        )(earlier, added_mass)

    def mass_dot(mass, same, other):
        return call(
            dot_kernel, "mass_dot", parts_i16, [SMEM, VMEM, VMEM, VMEM], VMEM,
            2 * added_mass.size * width, 6 * 2**20,
            [pltpu.VMEM((added_mass.shape[1], width), BF16)], 48,
        )(core, mass, same, other)

    def pack(parts, gain, wet, last):
        rows = 4 if last else 8
        message = jax.ShapeDtypeStruct((rows * devices, LANES), F32)
        shapes = [message] if last else [load_i16, message]
        args = [parts, gain, spread_out, wet]
        specs = [VMEM] * 3 + [ANY if last else VMEM]
        made = call(
            functools.partial(pack_kernel, last), "pack",
            shapes, specs, [VMEM] * len(shapes), 10**8, 3 * 2**20, (), 52 if last else 8,
        )(*args)
        return (None, made[0]) if last else made

    def wet_rows(got, load):
        return call(wet_kernel, "wet_rows", sent_bf16, [VMEM] * 3, VMEM, 10**8, 10**6)(
            got, load, gather_in
        )

    def shell(got, dry, last, with_square, small):
        shapes = [block_f32] if last else [block_f32, edge_i16, edge_i16]
        shapes = shapes + [eight_f32] * with_square
        made = list(call(
            functools.partial(shell_kernel, last, with_square, small), "shell",
            shapes, [VMEM, HBM, VMEM], [HBM] + [VMEM] * (len(shapes) - 1), 20 * 10**9, 4 * 2**20,
            [block_vmem, block_vmem, dma((rows_dev // halo,)), dma((rows_dev // halo,))], 52,
        )(got, dry, place))
        current = made.pop(0)
        head, tail = (None, None) if last else (made.pop(0), made.pop(0))
        return current, head, tail, made.pop(0) if with_square else None

    def tie(value, other):
        return pl.pallas_call(
            tie_kernel,
            out_shape=jax.ShapeDtypeStruct(value.shape, value.dtype),
            in_specs=[ANY, ANY],
            out_specs=ANY,
            input_output_aliases={0: 0},
            compiler_params=pltpu.CompilerParams(vmem_limit_bytes=4 * 2**20),
            cost_estimate=pl.CostEstimate(flops=0, bytes_accessed=0, transcendentals=0),
            name="tie",
        )(value, other)

    def exchange(message):
        return lax.all_to_all(message, both, split_axis=0, concat_axis=0, tiled=True)

    def gathered(sent, low):
        same = lax.all_to_all(
            sent, "row", split_axis=0, concat_axis=0, tiled=True, axis_index_groups=same_core
        )
        same = tie(same, low)
        return same, lax.ppermute(same, "row", swap_core)

    lower = low_edge.astype(F32) * 0.25
    upper = high_edge.astype(F32) * 0.25
    centre = (0.5 * (upper + lower))[None, :]
    radius = (0.5 * (upper - lower))[None, :]
    total_rows = rows_dev * devices

    current = mode_block
    start_rows = jnp.dot(pick, current.astype(BF16), preferred_element_type=F32)
    start_rows = start_rows.astype(BF16).reshape(2, devices, width).transpose(1, 0, 2)
    start_rows = exchange(start_rows).transpose(1, 0, 2).reshape(slots, width)
    wetted = jnp.dot(gather_in, start_rows, preferred_element_type=F32).astype(BF16)
    sent = jnp.broadcast_to(wetted[None], (n_same,) + wetted.shape)
    head, tail = call(
        edge_kernel, "edges", [edge_i16, edge_i16], [VMEM] * 2, [VMEM] * 2, 10**6, 2**20
    )(current[:halo], current[rows_dev - halo :])
    previous, squares = None, []
    got = start_rows
    for outer_no in range(OUTER):
        for degree_no in range(DEGREE):
            last = outer_no == OUTER - 1 and degree_no == DEGREE - 1
            gain = (1.0 if degree_no == 0 else 2.0) / radius
            before = None if degree_no == 0 else previous
            low = lax.ppermute(tail, both, forward)
            high = lax.ppermute(head, both, backward)
            mass = fetch(got)
            same, other = gathered(sent, low)
            partial = mass_dot(mass, same, other)
            dry, wet = stiff(low, current, high, before, gain, -centre * gain, not last)
            parts = lax.all_to_all(partial, "col", split_axis=0, concat_axis=0, tiled=True)
            load, message = pack(parts, gain, dry if last else wet, last)
            got = exchange(message.reshape(devices, -1, LANES)).reshape(-1, LANES)
            previous = current
            if not last:
                sent = wet_rows(got, lax.ppermute(load, both, to_in))
            current, head, tail, square = shell(got, dry, last, degree_no == DEGREE - 1, SMALL if last else 1.0)
            if square is not None:
                squares.append(square[:1])
    both_sums = jnp.stack(squares, axis=1)
    both_sums = exchange(jnp.broadcast_to(both_sums, (devices, OUTER, width)))
    both_sums = jnp.sum(both_sums, axis=0)
    first = both_sums[0:1] / total_rows + 1e-06
    second = both_sums[1:2] / total_rows / first * (1.0 / (SMALL * SMALL)) + 1e-06
    return current / (jnp.sqrt(first) * jnp.sqrt(second))


def solution(mesh):
    placed = (
        P(("row", "col"), None),
        P(("row", "col"), None, None, None),
        P(("row", "col"), None),
        P(),
        P("row", "col"),
        P(),
        P(),
    )
    return jax.shard_map(
        body, mesh=mesh, in_specs=placed, out_specs=P(("row", "col"), None), check_vma=False
    )
```

```python
import functools

import jax
import jax.numpy as jnp
from jax import lax
from jax.experimental import pallas as pl
from jax.experimental.pallas import tpu as pltpu
from jax.sharding import PartitionSpec as P

DEGREE = 3
OUTER = 2
F32 = jnp.float32
BF16 = jnp.bfloat16
LANES = 128
PAD = 16
STEPS = 32000.0
SMALL = 2.0**-20
VMEM = pl.BlockSpec(memory_space=pltpu.VMEM)
HBM = pl.BlockSpec(memory_space=pltpu.HBM)
ANY = pl.BlockSpec(memory_space=pl.ANY)
SMEM = pl.BlockSpec(memory_space=pltpu.SMEM)


def two_parts(value):
    hi = value.astype(BF16)
    return hi, (value - hi.astype(F32)).astype(BF16)


def choose(matrix, value):
    hi, lo = two_parts(value)
    picked = jnp.dot(matrix, hi, preferred_element_type=F32)
    return picked + jnp.dot(matrix, lo, preferred_element_type=F32)


def call(kernel, name, out_shape, in_specs, out_specs, flops, moved, scratch=(), limit=8):
    return pl.pallas_call(
        kernel,
        out_shape=out_shape,
        in_specs=in_specs,
        out_specs=out_specs,
        scratch_shapes=list(scratch),
        compiler_params=pltpu.CompilerParams(vmem_limit_bytes=limit * 2**20),
        cost_estimate=pl.CostEstimate(flops=flops, bytes_accessed=moved, transcendentals=0),
        name=name,
    )


def encode(value, out):
    rows = value.shape[0]
    top = jnp.maximum(jnp.max(jnp.abs(value), axis=0, keepdims=True), 1e-30)
    power = jnp.clip(jnp.ceil(jnp.log2(top)), -100.0, 126.0)
    steps = jnp.floor(value * (STEPS * jnp.exp2(-power)) + 0.5)
    out[0:rows, :] = steps.astype(jnp.int32).astype(jnp.int16)
    tail = jnp.broadcast_to(power, (PAD, value.shape[1]))
    out[rows : rows + PAD, :] = tail.astype(jnp.int32).astype(jnp.int16)


def decode(coded):
    rows = coded.shape[0] - PAD
    power = coded[rows : rows + PAD, :].astype(jnp.int32).astype(F32)[0:1]
    return coded[0:rows, :].astype(jnp.int32).astype(F32) * (jnp.exp2(power) * (1.0 / STEPS))


def placed(matrix, hi, lo):
    value = jnp.dot(matrix, hi, preferred_element_type=F32)
    return value + jnp.dot(matrix, lo, preferred_element_type=F32)


def border_kernel(got, dry_hbm, place, head, tail, dry, sems):
    halo = dry.shape[1]
    starts = [0, place.shape[0] - halo]
    copies = [
        pltpu.make_async_copy(dry_hbm.at[pl.ds(at, halo)], dry.at[i], sems.at[i])
        for i, at in enumerate(starts)
    ]
    for copy in copies:
        copy.start()
    loads = two_parts(slot_rows(got, place.shape[1] // 2, 0))
    for i, (at, out) in enumerate(zip(starts, (head, tail))):
        more = placed(place[at : at + halo, :], *loads)
        copies[i].wait()
        encode(dry[i] + more, out)


def edge_kernel(head, tail, head_out, tail_out):
    encode(head[...], head_out)
    encode(tail[...], tail_out)


def stiff_kernel(fresh, with_prev, with_wet, with_square, *refs):
    refs = list(refs)
    cols, k_hbm, low, here_hbm, high, scale, shift = refs[:7]
    del refs[:7]
    got, place = (None, None) if fresh else (refs.pop(0), refs.pop(0))
    prev_hbm = refs.pop(0) if with_prev else None
    pick = refs.pop(0) if with_wet else None
    out_hbm = refs.pop(0)
    wet = refs.pop(0) if with_wet else None
    made_hbm = None if fresh else refs.pop(0)
    square = refs.pop(0) if with_square else None
    k, here, prev, out, p_hi, p_lo, k_sem, here_sem, prev_sem, out_sem, made_sem = refs
    rows = here.shape[0]
    size = k.shape[2]
    halo = low.shape[0] - PAD
    count = rows // size
    chunks = [pl.ds(i * halo, halo) for i in range(rows // halo)]
    here_copies = [
        pltpu.make_async_copy(here_hbm.at[mine], here.at[mine], here_sem.at[i])
        for i, mine in enumerate(chunks)
    ]
    for copy in here_copies:
        copy.start()
    row_copies = []
    for i in range(count):
        mine = pl.ds(i * size, size)
        row_copies.append([pltpu.make_async_copy(k_hbm.at[i], k.at[i], k_sem.at[i])])
        if with_prev:
            row_copies[i].append(
                pltpu.make_async_copy(prev_hbm.at[mine], prev.at[mine], prev_sem.at[i])
            )
        for copy in row_copies[i]:
            copy.start()

    def put(value, start):
        hi, lo = two_parts(value)
        p_hi[start : start + value.shape[0], :] = hi
        p_lo[start : start + value.shape[0], :] = lo

    put(decode(low), 0)
    put(decode(high), halo + rows)
    out_copies = []
    if not fresh:
        loads = two_parts(slot_rows(got, place.shape[1] // 2, 0))
    squares = None
    for i, mine in enumerate(chunks):
        here_copies[i].wait()
        value = here[mine, :]
        if not fresh:
            value = value + placed(place[mine, :], *loads)
            here[mine, :] = value
            copy = pltpu.make_async_copy(here.at[mine], made_hbm.at[mine], made_sem.at[i])
            copy.start()
            out_copies.append(copy)
        put(value, (i + 1) * halo)
        if with_square:
            more = jnp.sum(value * value, axis=0, keepdims=True)
            squares = more if squares is None else squares + more
    if with_square:
        square[...] = jnp.broadcast_to(squares, square.shape)
    for i in range(count):
        for copy in row_copies[i]:
            copy.wait()
        at = [pl.ds(pl.multiple_of(cols[i, j] * size, size), size) for j in range(k.shape[1])]
        k_parts = [two_parts(k[i, j]) for j in range(k.shape[1])]
        k_hi = jnp.concatenate([part[0] for part in k_parts], axis=1)
        k_lo = jnp.concatenate([part[1] for part in k_parts], axis=1)
        v_hi = jnp.concatenate([p_hi[rows_at, :] for rows_at in at], axis=0)
        v_lo = jnp.concatenate([p_lo[rows_at, :] for rows_at in at], axis=0)
        pair = jnp.dot(jnp.concatenate([k_hi, k_lo], axis=0), v_hi, preferred_element_type=F32)
        acc = pair[:size] + pair[size:] + jnp.dot(k_hi, v_lo, preferred_element_type=F32)
        mine = pl.ds(i * size, size)
        value = scale[...] * acc + shift[...] * here[mine, :]
        if with_prev:
            value = value - prev[mine, :]
        out[mine, :] = value
        copy = pltpu.make_async_copy(out.at[mine], out_hbm.at[mine], out_sem.at[i])
        copy.start()
        out_copies.append(copy)
    if with_wet:
        wet[...] = choose(pick[...], out[...])
    for copy in out_copies:
        copy.wait()


def pack_kernel(last, *refs):
    refs = list(refs)
    parts, gain, spread, wet = refs[:4]
    del refs[:4]
    load = None if last else refs.pop(0)
    message = refs.pop(0)
    total = decode(parts.at[0])
    for i in range(1, parts.shape[0]):
        total = total + decode(parts.at[i])
    total = total * gain[...]
    if not last:
        encode(total, load)
    sent = choose(spread[...], total)
    devices = sent.shape[0] // 2
    rows = message.shape[0] // devices
    for h in range(2):
        piece = slice(h * LANES, (h + 1) * LANES)
        for s in range(2):
            mine = slice(s * devices, (s + 1) * devices)
            message[pl.ds((2 if last else 4) * h + s, devices, stride=rows), :] = sent[mine, piece]
            if not last:
                message[pl.ds(4 * h + 2 + s, devices, stride=rows), :] = wet[mine, piece]


def slot_rows(got, devices, first):
    rows = got.shape[0] // devices
    half = min(rows // 2, 4)

    def one(s):
        halves = [got[pl.ds(half * h + first + s, devices, stride=rows), :] for h in range(2)]
        return jnp.concatenate(halves, axis=1)

    return jnp.concatenate([one(0), one(1)], axis=0)


def wet_kernel(got, load, gather, sent):
    devices = gather.shape[1] // 2
    value = choose(gather[...], slot_rows(got, devices, 2)) + decode(load)
    value = value.astype(BF16)
    for i in range(sent.shape[0]):
        sent[i] = value


def shell_kernel(got, dry_hbm, place, out, square, dry, sem):
    copy = pltpu.make_async_copy(dry_hbm, dry, sem)
    copy.start()
    more = placed(place[...], *two_parts(slot_rows(got, place.shape[1] // 2, 0)))
    copy.wait()
    value = dry[...] + more
    out[...] = value
    scaled = value * SMALL
    square[...] = jnp.broadcast_to(jnp.sum(scaled * scaled, axis=0, keepdims=True), square.shape)


def tie_kernel(value, other, out):
    pass


def fetch_kernel(earlier, mass_hbm, out, sems):
    chunk = mass_hbm.shape[0] // sems.shape[0]
    copies = []
    for i in range(sems.shape[0]):
        rows = pl.ds(i * chunk, chunk)
        copies.append(pltpu.make_async_copy(mass_hbm.at[rows], out.at[rows], sems.at[i]))
        copies[i].start()
    for copy in copies:
        copy.wait()


def dot_kernel(core, mass, same, other, out, panels):
    count, depth, _ = same.shape
    block = out.shape[1] - PAD
    chunk = 2 * block
    for j in range(count):
        at = pl.multiple_of((2 * j + core[0]) * depth, depth)
        panels[pl.ds(at, depth), :] = same[j]
        at = pl.multiple_of((2 * j + 1 - core[0]) * depth, depth)
        panels[pl.ds(at, depth), :] = other[j]
    for i in range(out.shape[0] // 2):
        value = jnp.dot(
            mass[i * chunk : (i + 1) * chunk, :], panels[...], preferred_element_type=F32
        )
        for j in range(2):
            encode(value[j * block : (j + 1) * block], out.at[2 * i + j])


def body(mode_block, k_blocks, block_cols, panel_node, added_mass, low_edge, high_edge):
    n_row = lax.axis_size("row")
    n_col = lax.axis_size("col")
    devices = n_row * n_col
    my_row = lax.axis_index("row")
    my_col = lax.axis_index("col")
    linear = my_row * n_col + my_col
    core = (my_row % 2).astype(jnp.int32).reshape(1)
    rows_dev, width = mode_block.shape
    size = k_blocks.shape[2]
    blocks_dev = rows_dev // size
    per_block = panel_node.shape[0] // devices
    slots = 2 * devices
    both = ("row", "col")

    panel_rows = panel_node.reshape(devices, per_block)
    source = panel_rows // rows_dev
    before = jnp.concatenate([jnp.full((devices, 1), -1, source.dtype), source[:, :-1]], axis=1)
    rank = (source == before).astype(jnp.int32)
    owned = source == linear
    local = panel_rows - linear * rows_dev
    first = jnp.max(jnp.where(owned & (rank == 0), local, -1), axis=1)
    second = jnp.max(jnp.where(owned & (rank == 1), local, -1), axis=1)
    by_block = jnp.stack([first, second], axis=0)
    by_target = by_block.reshape(2, n_col, n_row).transpose(0, 2, 1)
    shell_rows = jnp.arange(rows_dev, dtype=jnp.int32)
    pick = (by_target.reshape(slots, 1) == shell_rows[None, :]).astype(BF16)
    place = (shell_rows[:, None] == by_block.reshape(1, slots)).astype(BF16)
    flat = rank * devices + source
    slot_ids = jnp.arange(slots, dtype=jnp.int32)
    in_flat = lax.dynamic_index_in_dim(flat, my_col * n_row + my_row, 0, keepdims=False)
    out_flat = lax.dynamic_index_in_dim(flat, linear, 0, keepdims=False)
    gather_in = (in_flat[:, None] == slot_ids[None, :]).astype(BF16)
    spread_out = (slot_ids[:, None] == out_flat[None, :]).astype(BF16)

    cols = block_cols - (linear * blocks_dev - 2)
    halo = 2 * size
    n_same = n_row // 2
    same_core = [[i for i in range(n_row) if i % 2 == c] for c in range(2)]
    swap_core = [(i, i ^ 1) for i in range(n_row)]
    forward = [(i, i + 1) for i in range(devices - 1)]
    backward = [(i + 1, i) for i in range(devices - 1)]
    to_in = [(b, (b % n_row) * n_col + b // n_row) for b in range(devices)]

    block_f32 = jax.ShapeDtypeStruct((rows_dev, width), F32)
    wet_f32 = jax.ShapeDtypeStruct((slots, width), F32)
    eight_f32 = jax.ShapeDtypeStruct((8, width), F32)
    load_i16 = jax.ShapeDtypeStruct((per_block + PAD, width), jnp.int16)
    parts_i16 = jax.ShapeDtypeStruct((n_col, per_block + PAD, width), jnp.int16)
    edge_i16 = jax.ShapeDtypeStruct((halo + PAD, width), jnp.int16)
    sent_bf16 = jax.ShapeDtypeStruct((n_same, per_block, width), BF16)
    block_vmem = pltpu.VMEM((rows_dev, width), F32)
    padded = pltpu.VMEM((rows_dev + 2 * halo, width), BF16)
    dma = pltpu.SemaphoreType.DMA

    def stiff(low, here, high, got, previous, scale, shift, with_wet, with_square):
        fresh, with_prev = got is None, previous is not None
        args = [cols, k_blocks, low, here, high, scale, shift]
        specs = [SMEM, HBM, VMEM, HBM, VMEM, VMEM, VMEM]
        if not fresh:
            args, specs = args + [got, place], specs + [VMEM, VMEM]
        if with_prev:
            args, specs = args + [previous], specs + [HBM]
        if with_wet:
            args, specs = args + [pick], specs + [VMEM]
        shapes = [block_f32] + [wet_f32] * with_wet + [block_f32] * (not fresh) + [eight_f32] * with_square
        outs = [HBM] + [VMEM] * with_wet + [HBM] * (not fresh) + [VMEM] * with_square
        made = list(call(
            functools.partial(stiff_kernel, fresh, with_prev, with_wet, with_square), "stiff",
            shapes, specs, outs, 80 * 10**9, 8 * 2**20,
            [
                pltpu.VMEM(k_blocks.shape, F32), block_vmem, block_vmem, block_vmem, padded, padded,
                dma((blocks_dev,)), dma((rows_dev // halo,)), dma((blocks_dev,)), dma((blocks_dev,)),
                dma((rows_dev // halo,)),
            ],
            52,
        )(*args))
        dry = made.pop(0)
        wet = made.pop(0) if with_wet else None
        current = here if fresh else made.pop(0)
        return dry, wet, current, made.pop(0) if with_square else None

    def fetch(earlier):
        return call(
            fetch_kernel, "fetch", pltpu.VMEM(added_mass.shape, BF16), [ANY, HBM], VMEM,
            10 * 10**9, 4 * 2**20, [dma((4,))], 48,
        )(earlier, added_mass)

    def mass_dot(mass, same, other):
        return call(
            dot_kernel, "mass_dot", parts_i16, [SMEM, VMEM, VMEM, VMEM], VMEM,
            2 * added_mass.size * width, 6 * 2**20,
            [pltpu.VMEM((added_mass.shape[1], width), BF16)], 48,
        )(core, mass, same, other)

    def pack(parts, gain, wet, last):
        rows = 4 if last else 8
        message = jax.ShapeDtypeStruct((rows * devices, LANES), F32)
        shapes = [message] if last else [load_i16, message]
        args = [parts, gain, spread_out, wet]
        specs = [VMEM] * 4
        made = call(
            functools.partial(pack_kernel, last), "pack",
            shapes, specs, [VMEM] * len(shapes), 10**8, 3 * 2**20,
        )(*args)
        return (None, made[0]) if last else made

    def wet_rows(got, load):
        return call(wet_kernel, "wet_rows", sent_bf16, [VMEM] * 3, VMEM, 10**8, 10**6)(
            got, load, gather_in
        )

    def border(got, dry):
        return call(
            border_kernel, "border", [edge_i16, edge_i16], [VMEM, HBM, VMEM], [VMEM, VMEM],
            20 * 10**9, 2 * 2**20, [pltpu.VMEM((2, halo, width), F32), dma((2,))], 52,
        )(got, dry, place)

    def shell(got, dry):
        return call(
            shell_kernel, "shell", [block_f32, eight_f32], [VMEM, HBM, VMEM], [VMEM, VMEM],
            2 * 10**9, 4 * 2**20, [block_vmem, dma], 52,
        )(got, dry, place)

    def tie(value, other):
        return pl.pallas_call(
            tie_kernel,
            out_shape=jax.ShapeDtypeStruct(value.shape, value.dtype),
            in_specs=[ANY, ANY],
            out_specs=ANY,
            input_output_aliases={0: 0},
            compiler_params=pltpu.CompilerParams(vmem_limit_bytes=4 * 2**20),
            cost_estimate=pl.CostEstimate(flops=0, bytes_accessed=0, transcendentals=0),
            name="tie",
        )(value, other)

    def exchange(message):
        return lax.all_to_all(message, both, split_axis=0, concat_axis=0, tiled=True)

    def gathered(sent, low):
        same = lax.all_to_all(
            sent, "row", split_axis=0, concat_axis=0, tiled=True, axis_index_groups=same_core
        )
        same = tie(same, low)
        return same, lax.ppermute(same, "row", swap_core)

    lower = low_edge.astype(F32) * 0.25
    upper = high_edge.astype(F32) * 0.25
    centre = (0.5 * (upper + lower))[None, :]
    radius = (0.5 * (upper - lower))[None, :]
    total_rows = rows_dev * devices

    here = mode_block
    start_rows = jnp.dot(pick, here.astype(BF16), preferred_element_type=F32)
    start_rows = start_rows.astype(BF16).reshape(2, devices, width).transpose(1, 0, 2)
    start_rows = exchange(start_rows).transpose(1, 0, 2).reshape(slots, width)
    wetted = jnp.dot(gather_in, start_rows, preferred_element_type=F32).astype(BF16)
    sent = jnp.broadcast_to(wetted[None], (n_same,) + wetted.shape)
    head, tail = call(
        edge_kernel, "edges", [edge_i16, edge_i16], [VMEM] * 2, [VMEM] * 2, 10**6, 2**20
    )(here[:halo], here[rows_dev - halo :])
    current, got, squares = None, None, []
    for outer_no in range(OUTER):
        for degree_no in range(DEGREE):
            last = outer_no == OUTER - 1 and degree_no == DEGREE - 1
            gain = (1.0 if degree_no == 0 else 2.0) / radius
            before = None if degree_no == 0 else current
            low = lax.ppermute(tail, both, forward)
            high = lax.ppermute(head, both, backward)
            mass = fetch(start_rows if got is None else got)
            same, other = gathered(sent, low)
            partial = mass_dot(mass, same, other)
            end = outer_no > 0 and degree_no == 0
            dry, wet, current, square = stiff(
                low, here, high, got, before, gain, -centre * gain, True, end
            )
            if end:
                squares.append(square[:1])
            here = dry
            parts = lax.all_to_all(partial, "col", split_axis=0, concat_axis=0, tiled=True)
            load, message = pack(parts, gain, wet, last)
            got = exchange(message.reshape(devices, -1, LANES)).reshape(-1, LANES)
            if not last:
                sent = wet_rows(got, lax.ppermute(load, both, to_in))
                head, tail = border(got, dry)
    current, square = shell(got, dry)
    squares.append(square[:1])
    both_sums = jnp.stack(squares, axis=1)
    both_sums = exchange(jnp.broadcast_to(both_sums, (devices, OUTER, width)))
    both_sums = jnp.sum(both_sums, axis=0)
    first = both_sums[0:1] / total_rows + 1e-06
    second = both_sums[1:2] / total_rows / first * (1.0 / (SMALL * SMALL)) + 1e-06
    return current / (jnp.sqrt(first) * jnp.sqrt(second))


def solution(mesh):
    placed = (
        P(("row", "col"), None),
        P(("row", "col"), None, None, None),
        P(("row", "col"), None),
        P(),
        P("row", "col"),
        P(),
        P(),
    )
    return jax.shard_map(
        body, mesh=mesh, in_specs=placed, out_specs=P(("row", "col"), None), check_vma=False
    )
```

```python
import functools

import jax
import jax.numpy as jnp
from jax import lax
from jax.experimental import pallas as pl
from jax.experimental.pallas import tpu as pltpu
from jax.sharding import PartitionSpec as P

DEGREE = 3
OUTER = 2
F32 = jnp.float32
BF16 = jnp.bfloat16
LANES = 128
PAD = 16
STEPS = 32000.0
SMALL = 2.0**-20
VMEM = pl.BlockSpec(memory_space=pltpu.VMEM)
HBM = pl.BlockSpec(memory_space=pltpu.HBM)
ANY = pl.BlockSpec(memory_space=pl.ANY)
SMEM = pl.BlockSpec(memory_space=pltpu.SMEM)


def two_parts(value):
    hi = value.astype(BF16)
    return hi, (value - hi.astype(F32)).astype(BF16)


def choose(matrix, value):
    hi, lo = two_parts(value)
    picked = jnp.dot(matrix, hi, preferred_element_type=F32)
    return picked + jnp.dot(matrix, lo, preferred_element_type=F32)


def call(kernel, name, out_shape, in_specs, out_specs, flops, moved, scratch=(), limit=8):
    return pl.pallas_call(
        kernel,
        out_shape=out_shape,
        in_specs=in_specs,
        out_specs=out_specs,
        scratch_shapes=list(scratch),
        compiler_params=pltpu.CompilerParams(vmem_limit_bytes=limit * 2**20),
        cost_estimate=pl.CostEstimate(flops=flops, bytes_accessed=moved, transcendentals=0),
        name=name,
    )


def encode(value, out):
    rows = value.shape[0]
    top = jnp.maximum(jnp.max(jnp.abs(value), axis=0, keepdims=True), 1e-30)
    power = jnp.clip(jnp.ceil(jnp.log2(top)), -100.0, 126.0)
    steps = jnp.floor(value * (STEPS * jnp.exp2(-power)) + 0.5)
    out[0:rows, :] = steps.astype(jnp.int32).astype(jnp.int16)
    tail = jnp.broadcast_to(power, (PAD, value.shape[1]))
    out[rows : rows + PAD, :] = tail.astype(jnp.int32).astype(jnp.int16)


def decode(coded):
    rows = coded.shape[0] - PAD
    power = coded[rows : rows + PAD, :].astype(jnp.int32).astype(F32)[0:1]
    return coded[0:rows, :].astype(jnp.int32).astype(F32) * (jnp.exp2(power) * (1.0 / STEPS))


def placed(matrix, hi, lo):
    value = jnp.dot(matrix, hi, preferred_element_type=F32)
    return value + jnp.dot(matrix, lo, preferred_element_type=F32)


def border_kernel(got, dry_hbm, place, head, tail, dry, sems):
    halo = dry.shape[1]
    starts = [0, place.shape[0] - halo]
    copies = [
        pltpu.make_async_copy(dry_hbm.at[pl.ds(at, halo)], dry.at[i], sems.at[i])
        for i, at in enumerate(starts)
    ]
    for copy in copies:
        copy.start()
    loads = two_parts(slot_rows(got, place.shape[1] // 2, 0))
    for i, (at, out) in enumerate(zip(starts, (head, tail))):
        more = placed(place[at : at + halo, :], *loads)
        copies[i].wait()
        encode(dry[i] + more, out)


def edge_kernel(head, tail, head_out, tail_out):
    encode(head[...], head_out)
    encode(tail[...], tail_out)


def stiff_kernel(fresh, with_prev, with_wet, with_square, *refs):
    refs = list(refs)
    cols, k_hbm, low, here_hbm, high, scale, shift = refs[:7]
    del refs[:7]
    got, place = (None, None) if fresh else (refs.pop(0), refs.pop(0))
    prev_hbm = refs.pop(0) if with_prev else None
    pick = refs.pop(0) if with_wet else None
    out_hbm = refs.pop(0)
    wet = refs.pop(0) if with_wet else None
    made_hbm = None if fresh else refs.pop(0)
    square = refs.pop(0) if with_square else None
    k, here, prev, out, p_hi, p_lo, k_sem, here_sem, prev_sem, out_sem, made_sem = refs
    rows = here.shape[0]
    size = k.shape[2]
    halo = low.shape[0] - PAD
    count = rows // size
    chunks = [pl.ds(i * halo, halo) for i in range(rows // halo)]
    here_copies = [
        pltpu.make_async_copy(here_hbm.at[mine], here.at[mine], here_sem.at[i])
        for i, mine in enumerate(chunks)
    ]
    for copy in here_copies:
        copy.start()
    row_copies = []
    for i in range(count):
        mine = pl.ds(i * size, size)
        row_copies.append([pltpu.make_async_copy(k_hbm.at[i], k.at[i], k_sem.at[i])])
        if with_prev:
            row_copies[i].append(
                pltpu.make_async_copy(prev_hbm.at[mine], prev.at[mine], prev_sem.at[i])
            )
        for copy in row_copies[i]:
            copy.start()

    def put(value, start):
        hi, lo = two_parts(value)
        p_hi[start : start + value.shape[0], :] = hi
        p_lo[start : start + value.shape[0], :] = lo

    put(decode(low), 0)
    put(decode(high), halo + rows)
    out_copies = []
    if not fresh:
        loads = two_parts(slot_rows(got, place.shape[1] // 2, 0))
    squares = None
    for i, mine in enumerate(chunks):
        here_copies[i].wait()
        value = here[mine, :]
        if not fresh:
            value = value + placed(place[mine, :], *loads)
            here[mine, :] = value
            copy = pltpu.make_async_copy(here.at[mine], made_hbm.at[mine], made_sem.at[i])
            copy.start()
            out_copies.append(copy)
        put(value, (i + 1) * halo)
        if with_square:
            more = jnp.sum(value * value, axis=0, keepdims=True)
            squares = more if squares is None else squares + more
    if with_square:
        square[...] = jnp.broadcast_to(squares, square.shape)
    for i in range(count):
        for copy in row_copies[i]:
            copy.wait()
        at = [pl.ds(pl.multiple_of(cols[i, j] * size, size), size) for j in range(k.shape[1])]
        k_parts = [two_parts(k[i, j]) for j in range(k.shape[1])]
        k_hi = jnp.concatenate([part[0] for part in k_parts], axis=1)
        k_lo = jnp.concatenate([part[1] for part in k_parts], axis=1)
        v_hi = jnp.concatenate([p_hi[rows_at, :] for rows_at in at], axis=0)
        v_lo = jnp.concatenate([p_lo[rows_at, :] for rows_at in at], axis=0)
        pair = jnp.dot(jnp.concatenate([k_hi, k_lo], axis=0), v_hi, preferred_element_type=F32)
        acc = pair[:size] + pair[size:] + jnp.dot(k_hi, v_lo, preferred_element_type=F32)
        mine = pl.ds(i * size, size)
        value = scale[...] * acc + shift[...] * here[mine, :]
        if with_prev:
            value = value - prev[mine, :]
        out[mine, :] = value
        copy = pltpu.make_async_copy(out.at[mine], out_hbm.at[mine], out_sem.at[i])
        copy.start()
        out_copies.append(copy)
    if with_wet:
        wet[...] = choose(pick[...], out[...])
    for copy in out_copies:
        copy.wait()


def pack_kernel(last, *refs):
    refs = list(refs)
    parts, gain, spread, wet = refs[:4]
    del refs[:4]
    load = None if last else refs.pop(0)
    message = refs.pop(0)
    total = decode(parts.at[0])
    for i in range(1, parts.shape[0]):
        total = total + decode(parts.at[i])
    total = total * gain[...]
    if not last:
        encode(total, load)
    sent = choose(spread[...], total)
    devices = sent.shape[0] // 2
    rows = message.shape[0] // devices
    for h in range(2):
        piece = slice(h * LANES, (h + 1) * LANES)
        for s in range(2):
            mine = slice(s * devices, (s + 1) * devices)
            message[pl.ds((2 if last else 4) * h + s, devices, stride=rows), :] = sent[mine, piece]
            if not last:
                message[pl.ds(4 * h + 2 + s, devices, stride=rows), :] = wet[mine, piece]


def slot_rows(got, devices, first):
    rows = got.shape[0] // devices
    half = min(rows // 2, 4)

    def one(s):
        halves = [got[pl.ds(half * h + first + s, devices, stride=rows), :] for h in range(2)]
        return jnp.concatenate(halves, axis=1)

    return jnp.concatenate([one(0), one(1)], axis=0)


def wet_kernel(got, load, gather, sent):
    devices = gather.shape[1] // 2
    value = choose(gather[...], slot_rows(got, devices, 2)) + decode(load)
    value = value.astype(BF16)
    for i in range(sent.shape[0]):
        sent[i] = value


def shell_kernel(got, dry_hbm, place, out, square, dry, sem):
    copy = pltpu.make_async_copy(dry_hbm, dry, sem)
    copy.start()
    more = placed(place[...], *two_parts(slot_rows(got, place.shape[1] // 2, 0)))
    copy.wait()
    value = dry[...] + more
    out[...] = value
    scaled = value * SMALL
    square[...] = jnp.broadcast_to(jnp.sum(scaled * scaled, axis=0, keepdims=True), square.shape)


def tie_kernel(*refs):
    pass


def fetch_kernel(earlier, mass_hbm, out, sems):
    chunk = mass_hbm.shape[0] // sems.shape[0]
    copies = []
    for i in range(sems.shape[0]):
        rows = pl.ds(i * chunk, chunk)
        copies.append(pltpu.make_async_copy(mass_hbm.at[rows], out.at[rows], sems.at[i]))
        copies[i].start()
    for copy in copies:
        copy.wait()


def dot_kernel(core, mass, same, other, out, panels):
    count, depth, _ = same.shape
    block = out.shape[1] - PAD
    chunk = 2 * block
    for j in range(count):
        at = pl.multiple_of((2 * j + core[0]) * depth, depth)
        panels[pl.ds(at, depth), :] = same[j]
        at = pl.multiple_of((2 * j + 1 - core[0]) * depth, depth)
        panels[pl.ds(at, depth), :] = other[j]
    for i in range(out.shape[0] // 2):
        value = jnp.dot(
            mass[i * chunk : (i + 1) * chunk, :], panels[...], preferred_element_type=F32
        )
        for j in range(2):
            encode(value[j * block : (j + 1) * block], out.at[2 * i + j])


def body(mode_block, k_blocks, block_cols, panel_node, added_mass, low_edge, high_edge):
    n_row = lax.axis_size("row")
    n_col = lax.axis_size("col")
    devices = n_row * n_col
    my_row = lax.axis_index("row")
    my_col = lax.axis_index("col")
    linear = my_row * n_col + my_col
    core = (my_row % 2).astype(jnp.int32).reshape(1)
    rows_dev, width = mode_block.shape
    size = k_blocks.shape[2]
    blocks_dev = rows_dev // size
    per_block = panel_node.shape[0] // devices
    slots = 2 * devices
    both = ("row", "col")

    panel_rows = panel_node.reshape(devices, per_block)
    source = panel_rows // rows_dev
    before = jnp.concatenate([jnp.full((devices, 1), -1, source.dtype), source[:, :-1]], axis=1)
    rank = (source == before).astype(jnp.int32)
    owned = source == linear
    local = panel_rows - linear * rows_dev
    first = jnp.max(jnp.where(owned & (rank == 0), local, -1), axis=1)
    second = jnp.max(jnp.where(owned & (rank == 1), local, -1), axis=1)
    by_block = jnp.stack([first, second], axis=0)
    by_target = by_block.reshape(2, n_col, n_row).transpose(0, 2, 1)
    shell_rows = jnp.arange(rows_dev, dtype=jnp.int32)
    pick = (by_target.reshape(slots, 1) == shell_rows[None, :]).astype(BF16)
    place = (shell_rows[:, None] == by_block.reshape(1, slots)).astype(BF16)
    flat = rank * devices + source
    slot_ids = jnp.arange(slots, dtype=jnp.int32)
    in_flat = lax.dynamic_index_in_dim(flat, my_col * n_row + my_row, 0, keepdims=False)
    out_flat = lax.dynamic_index_in_dim(flat, linear, 0, keepdims=False)
    gather_in = (in_flat[:, None] == slot_ids[None, :]).astype(BF16)
    spread_out = (slot_ids[:, None] == out_flat[None, :]).astype(BF16)

    cols = block_cols - (linear * blocks_dev - 2)
    halo = 2 * size
    n_same = n_row // 2
    same_core = [[i for i in range(n_row) if i % 2 == c] for c in range(2)]
    swap_core = [(i, i ^ 1) for i in range(n_row)]
    forward = [(i, i + 1) for i in range(devices - 1)]
    backward = [(i + 1, i) for i in range(devices - 1)]
    to_in = [(b, (b % n_row) * n_col + b // n_row) for b in range(devices)]

    block_f32 = jax.ShapeDtypeStruct((rows_dev, width), F32)
    wet_f32 = jax.ShapeDtypeStruct((slots, width), F32)
    eight_f32 = jax.ShapeDtypeStruct((8, width), F32)
    load_i16 = jax.ShapeDtypeStruct((per_block + PAD, width), jnp.int16)
    parts_i16 = jax.ShapeDtypeStruct((n_col, per_block + PAD, width), jnp.int16)
    edge_i16 = jax.ShapeDtypeStruct((halo + PAD, width), jnp.int16)
    sent_bf16 = jax.ShapeDtypeStruct((n_same, per_block, width), BF16)
    block_vmem = pltpu.VMEM((rows_dev, width), F32)
    padded = pltpu.VMEM((rows_dev + 2 * halo, width), BF16)
    dma = pltpu.SemaphoreType.DMA

    def stiff(low, here, high, got, previous, scale, shift, with_wet, with_square):
        fresh, with_prev = got is None, previous is not None
        args = [cols, k_blocks, low, here, high, scale, shift]
        specs = [SMEM, HBM, VMEM, HBM, VMEM, VMEM, VMEM]
        if not fresh:
            args, specs = args + [got, place], specs + [VMEM, VMEM]
        if with_prev:
            args, specs = args + [previous], specs + [HBM]
        if with_wet:
            args, specs = args + [pick], specs + [VMEM]
        shapes = [block_f32] + [wet_f32] * with_wet + [block_f32] * (not fresh) + [eight_f32] * with_square
        outs = [HBM] + [VMEM] * with_wet + [HBM] * (not fresh) + [VMEM] * with_square
        made = list(call(
            functools.partial(stiff_kernel, fresh, with_prev, with_wet, with_square), "stiff",
            shapes, specs, outs, 80 * 10**9, 8 * 2**20,
            [
                pltpu.VMEM(k_blocks.shape, F32), block_vmem, block_vmem, block_vmem, padded, padded,
                dma((blocks_dev,)), dma((rows_dev // halo,)), dma((blocks_dev,)), dma((blocks_dev,)),
                dma((rows_dev // halo,)),
            ],
            52,
        )(*args))
        dry = made.pop(0)
        wet = made.pop(0) if with_wet else None
        current = here if fresh else made.pop(0)
        return dry, wet, current, made.pop(0) if with_square else None

    def fetch(earlier):
        return call(
            fetch_kernel, "fetch", pltpu.VMEM(added_mass.shape, BF16), [ANY, HBM], VMEM,
            10 * 10**9, 4 * 2**20, [dma((4,))], 48,
        )(earlier, added_mass)

    def mass_dot(mass, same, other):
        return call(
            dot_kernel, "mass_dot", parts_i16, [SMEM, VMEM, VMEM, VMEM], VMEM,
            2 * added_mass.size * width, 6 * 2**20,
            [pltpu.VMEM((added_mass.shape[1], width), BF16)], 48,
        )(core, mass, same, other)

    def pack(parts, gain, wet, last):
        rows = 4 if last else 8
        message = jax.ShapeDtypeStruct((rows * devices, LANES), F32)
        shapes = [message] if last else [load_i16, message]
        args = [parts, gain, spread_out, wet]
        specs = [VMEM] * 4
        made = call(
            functools.partial(pack_kernel, last), "pack",
            shapes, specs, [VMEM] * len(shapes), 10**8, 3 * 2**20,
        )(*args)
        return (None, made[0]) if last else made

    def wet_rows(got, load):
        return call(wet_kernel, "wet_rows", sent_bf16, [VMEM] * 3, VMEM, 10**8, 10**6)(
            got, load, gather_in
        )

    def border(got, dry):
        return call(
            border_kernel, "border", [edge_i16, edge_i16], [VMEM, HBM, VMEM], [VMEM, VMEM],
            20 * 10**9, 2 * 2**20, [pltpu.VMEM((2, halo, width), F32), dma((2,))], 52,
        )(got, dry, place)

    def shell(got, dry):
        return call(
            shell_kernel, "shell", [block_f32, eight_f32], [VMEM, HBM, VMEM], [VMEM, VMEM],
            2 * 10**9, 4 * 2**20, [block_vmem, dma], 52,
        )(got, dry, place)

    def tie(value, other=None, flops=0):
        args = (value,) if other is None else (value, other)
        return pl.pallas_call(
            tie_kernel,
            out_shape=jax.ShapeDtypeStruct(value.shape, value.dtype),
            in_specs=[ANY] * len(args),
            out_specs=ANY,
            input_output_aliases={0: 0},
            compiler_params=pltpu.CompilerParams(vmem_limit_bytes=4 * 2**20),
            cost_estimate=pl.CostEstimate(flops=flops, bytes_accessed=0, transcendentals=0),
            name="tie",
        )(*args)

    def exchange(message):
        return lax.all_to_all(message, both, split_axis=0, concat_axis=0, tiled=True)

    def gathered(sent, low):
        same = lax.all_to_all(
            sent, "row", split_axis=0, concat_axis=0, tiled=True, axis_index_groups=same_core
        )
        same = tie(same, low)
        return same, lax.ppermute(same, "row", swap_core)

    lower = low_edge.astype(F32) * 0.25
    upper = high_edge.astype(F32) * 0.25
    centre = (0.5 * (upper + lower))[None, :]
    radius = (0.5 * (upper - lower))[None, :]
    total_rows = rows_dev * devices

    here = mode_block
    start_rows = jnp.dot(pick, here.astype(BF16), preferred_element_type=F32)
    start_rows = start_rows.astype(BF16).reshape(2, devices, width).transpose(1, 0, 2)
    start_rows = exchange(start_rows).transpose(1, 0, 2).reshape(slots, width)
    wetted = jnp.dot(gather_in, start_rows, preferred_element_type=F32).astype(BF16)
    sent = jnp.broadcast_to(wetted[None], (n_same,) + wetted.shape)
    head, tail = call(
        edge_kernel, "edges", [edge_i16, edge_i16], [VMEM] * 2, [VMEM] * 2, 10**6, 2**20
    )(here[:halo], here[rows_dev - halo :])
    current, got, squares = None, None, []
    for outer_no in range(OUTER):
        for degree_no in range(DEGREE):
            last = outer_no == OUTER - 1 and degree_no == DEGREE - 1
            gain = (1.0 if degree_no == 0 else 2.0) / radius
            before = None if degree_no == 0 else current
            low = lax.ppermute(tail, both, forward)
            high = lax.ppermute(head, both, backward)
            mass = fetch(start_rows if got is None else got)
            same, other = gathered(sent, low)
            partial = mass_dot(mass, same, other)
            end = outer_no > 0 and degree_no == 0
            dry, wet, current, square = stiff(
                low, here, high, got, before, gain, -centre * gain, True, end
            )
            if end:
                squares.append(square[:1])
            here = dry
            parts = lax.all_to_all(partial, "col", split_axis=0, concat_axis=0, tiled=True)
            load, message = pack(parts, gain, wet, last)
            got = exchange(message.reshape(devices, -1, LANES)).reshape(-1, LANES)
            if not last:
                load_in = tie(lax.ppermute(load, both, to_in), flops=80 * 10**9)
                sent = wet_rows(got, load_in)
                head, tail = border(got, dry)
    current, square = shell(got, dry)
    squares.append(square[:1])
    both_sums = jnp.stack(squares, axis=1)
    both_sums = exchange(jnp.broadcast_to(both_sums, (devices, OUTER, width)))
    both_sums = jnp.sum(both_sums, axis=0)
    first = both_sums[0:1] / total_rows + 1e-06
    second = both_sums[1:2] / total_rows / first * (1.0 / (SMALL * SMALL)) + 1e-06
    return current / (jnp.sqrt(first) * jnp.sqrt(second))


def solution(mesh):
    placed = (
        P(("row", "col"), None),
        P(("row", "col"), None, None, None),
        P(("row", "col"), None),
        P(),
        P("row", "col"),
        P(),
        P(),
    )
    return jax.shard_map(
        body, mesh=mesh, in_specs=placed, out_specs=P(("row", "col"), None), check_vma=False
    )
```

```python
import functools

import jax
import jax.numpy as jnp
from jax import lax
from jax.experimental import pallas as pl
from jax.experimental.pallas import tpu as pltpu
from jax.sharding import PartitionSpec as P

DEGREE = 3
OUTER = 2
F32 = jnp.float32
BF16 = jnp.bfloat16
LANES = 128
PAD = 16
STEPS = 32000.0
SMALL = 2.0**-20
VMEM = pl.BlockSpec(memory_space=pltpu.VMEM)
HBM = pl.BlockSpec(memory_space=pltpu.HBM)
ANY = pl.BlockSpec(memory_space=pl.ANY)
SMEM = pl.BlockSpec(memory_space=pltpu.SMEM)


def two_parts(value):
    hi = value.astype(BF16)
    return hi, (value - hi.astype(F32)).astype(BF16)


def choose(matrix, value):
    hi, lo = two_parts(value)
    picked = jnp.dot(matrix, hi, preferred_element_type=F32)
    return picked + jnp.dot(matrix, lo, preferred_element_type=F32)


def call(kernel, name, out_shape, in_specs, out_specs, flops, moved, scratch=(), limit=8):
    return pl.pallas_call(
        kernel,
        out_shape=out_shape,
        in_specs=in_specs,
        out_specs=out_specs,
        scratch_shapes=list(scratch),
        compiler_params=pltpu.CompilerParams(vmem_limit_bytes=limit * 2**20),
        cost_estimate=pl.CostEstimate(flops=flops, bytes_accessed=moved, transcendentals=0),
        name=name,
    )


def encode(value, out):
    rows = value.shape[0]
    top = jnp.maximum(jnp.max(jnp.abs(value), axis=0, keepdims=True), 1e-30)
    power = jnp.clip(jnp.ceil(jnp.log2(top)), -100.0, 126.0)
    steps = jnp.floor(value * (STEPS * jnp.exp2(-power)) + 0.5)
    out[0:rows, :] = steps.astype(jnp.int32).astype(jnp.int16)
    tail = jnp.broadcast_to(power, (PAD, value.shape[1]))
    out[rows : rows + PAD, :] = tail.astype(jnp.int32).astype(jnp.int16)


def decode(coded):
    rows = coded.shape[0] - PAD
    power = coded[rows : rows + PAD, :].astype(jnp.int32).astype(F32)[0:1]
    return coded[0:rows, :].astype(jnp.int32).astype(F32) * (jnp.exp2(power) * (1.0 / STEPS))


def placed(matrix, hi, lo):
    value = jnp.dot(matrix, hi, preferred_element_type=F32)
    return value + jnp.dot(matrix, lo, preferred_element_type=F32)


def border_kernel(got, dry_hbm, place, head, tail, dry, sems):
    halo = dry.shape[1]
    starts = [0, place.shape[0] - halo]
    copies = [
        pltpu.make_async_copy(dry_hbm.at[pl.ds(at, halo)], dry.at[i], sems.at[i])
        for i, at in enumerate(starts)
    ]
    for copy in copies:
        copy.start()
    loads = two_parts(slot_rows(got, place.shape[1] // 2, 0))
    for i, (at, out) in enumerate(zip(starts, (head, tail))):
        more = placed(place[at : at + halo, :], *loads)
        copies[i].wait()
        encode(dry[i] + more, out)


def edge_kernel(head, tail, head_out, tail_out):
    encode(head[...], head_out)
    encode(tail[...], tail_out)


def stiff_kernel(fresh, with_prev, with_wet, with_square, *refs):
    refs = list(refs)
    cols, k_hbm, low, here_hbm, high, scale, shift = refs[:7]
    del refs[:7]
    got, place = (None, None) if fresh else (refs.pop(0), refs.pop(0))
    prev_hbm = refs.pop(0) if with_prev else None
    pick = refs.pop(0) if with_wet else None
    out_hbm = refs.pop(0)
    wet = refs.pop(0) if with_wet else None
    made_hbm = None if fresh else refs.pop(0)
    square = refs.pop(0) if with_square else None
    k, here, prev, out, p_hi, p_lo, k_sem, here_sem, prev_sem, out_sem, made_sem = refs
    rows = here.shape[0]
    size = k.shape[2]
    halo = low.shape[0] - PAD
    count = rows // size
    chunks = [pl.ds(i * halo, halo) for i in range(rows // halo)]
    here_copies = [
        pltpu.make_async_copy(here_hbm.at[mine], here.at[mine], here_sem.at[i])
        for i, mine in enumerate(chunks)
    ]
    for copy in here_copies:
        copy.start()
    row_copies = []
    for i in range(count):
        mine = pl.ds(i * size, size)
        row_copies.append([pltpu.make_async_copy(k_hbm.at[i], k.at[i], k_sem.at[i])])
        if with_prev:
            row_copies[i].append(
                pltpu.make_async_copy(prev_hbm.at[mine], prev.at[mine], prev_sem.at[i])
            )
        for copy in row_copies[i]:
            copy.start()

    def put(value, start):
        hi, lo = two_parts(value)
        p_hi[start : start + value.shape[0], :] = hi
        p_lo[start : start + value.shape[0], :] = lo

    put(decode(low), 0)
    put(decode(high), halo + rows)
    out_copies = []
    if not fresh:
        loads = two_parts(slot_rows(got, place.shape[1] // 2, 0))
    squares = None
    for i, mine in enumerate(chunks):
        here_copies[i].wait()
        value = here[mine, :]
        if not fresh:
            value = value + placed(place[mine, :], *loads)
            here[mine, :] = value
            copy = pltpu.make_async_copy(here.at[mine], made_hbm.at[mine], made_sem.at[i])
            copy.start()
            out_copies.append(copy)
        put(value, (i + 1) * halo)
        if with_square:
            more = jnp.sum(value * value, axis=0, keepdims=True)
            squares = more if squares is None else squares + more
    if with_square:
        square[...] = jnp.broadcast_to(squares, square.shape)
    for i in range(count):
        for copy in row_copies[i]:
            copy.wait()
        at = [pl.ds(pl.multiple_of(cols[i, j] * size, size), size) for j in range(k.shape[1])]
        k_parts = [two_parts(k[i, j]) for j in range(k.shape[1])]
        k_hi = jnp.concatenate([part[0] for part in k_parts], axis=1)
        k_lo = jnp.concatenate([part[1] for part in k_parts], axis=1)
        v_hi = jnp.concatenate([p_hi[rows_at, :] for rows_at in at], axis=0)
        v_lo = jnp.concatenate([p_lo[rows_at, :] for rows_at in at], axis=0)
        pair = jnp.dot(jnp.concatenate([k_hi, k_lo], axis=0), v_hi, preferred_element_type=F32)
        acc = pair[:size] + pair[size:] + jnp.dot(k_hi, v_lo, preferred_element_type=F32)
        mine = pl.ds(i * size, size)
        value = scale[...] * acc + shift[...] * here[mine, :]
        if with_prev:
            value = value - prev[mine, :]
        out[mine, :] = value
        copy = pltpu.make_async_copy(out.at[mine], out_hbm.at[mine], out_sem.at[i])
        copy.start()
        out_copies.append(copy)
    if with_wet:
        wet[...] = choose(pick[...], out[...])
    for copy in out_copies:
        copy.wait()


def pack_kernel(last, *refs):
    refs = list(refs)
    parts, gain, spread, wet = refs[:4]
    del refs[:4]
    load = None if last else refs.pop(0)
    message = refs.pop(0)
    total = decode(parts.at[0])
    for i in range(1, parts.shape[0]):
        total = total + decode(parts.at[i])
    total = total * gain[...]
    if not last:
        encode(total, load)
    sent = choose(spread[...], total)
    devices = sent.shape[0] // 2
    rows = message.shape[0] // devices
    for h in range(2):
        piece = slice(h * LANES, (h + 1) * LANES)
        for s in range(2):
            mine = slice(s * devices, (s + 1) * devices)
            message[pl.ds((2 if last else 4) * h + s, devices, stride=rows), :] = sent[mine, piece]
            if not last:
                message[pl.ds(4 * h + 2 + s, devices, stride=rows), :] = wet[mine, piece]


def slot_rows(got, devices, first):
    rows = got.shape[0] // devices
    half = min(rows // 2, 4)

    def one(s):
        halves = [got[pl.ds(half * h + first + s, devices, stride=rows), :] for h in range(2)]
        return jnp.concatenate(halves, axis=1)

    return jnp.concatenate([one(0), one(1)], axis=0)


def wet_kernel(got, load, gather, sent):
    devices = gather.shape[1] // 2
    value = choose(gather[...], slot_rows(got, devices, 2)) + decode(load)
    value = value.astype(BF16)
    for i in range(sent.shape[0]):
        sent[i] = value


def shell_kernel(got, dry_hbm, place, out, square, dry, sem):
    copy = pltpu.make_async_copy(dry_hbm, dry, sem)
    copy.start()
    more = placed(place[...], *two_parts(slot_rows(got, place.shape[1] // 2, 0)))
    copy.wait()
    value = dry[...] + more
    out[...] = value
    scaled = value * SMALL
    square[...] = jnp.broadcast_to(jnp.sum(scaled * scaled, axis=0, keepdims=True), square.shape)


def tie_kernel(value, other, out):
    pass


def fetch_kernel(earlier, mass_hbm, out, sems):
    chunk = mass_hbm.shape[0] // sems.shape[0]
    copies = []
    for i in range(sems.shape[0]):
        rows = pl.ds(i * chunk, chunk)
        copies.append(pltpu.make_async_copy(mass_hbm.at[rows], out.at[rows], sems.at[i]))
        copies[i].start()
    for copy in copies:
        copy.wait()


def dot_kernel(core, mass, same, other, out, panels):
    count, depth, _ = same.shape
    block = out.shape[1] - PAD
    chunk = 2 * block
    for j in range(count):
        at = pl.multiple_of((count * core[0] + j) * depth, depth)
        panels[pl.ds(at, depth), :] = same[j]
        at = pl.multiple_of((count * (1 - core[0]) + j) * depth, depth)
        panels[pl.ds(at, depth), :] = other[j]
    for i in range(out.shape[0] // 2):
        value = jnp.dot(
            mass[i * chunk : (i + 1) * chunk, :], panels[...], preferred_element_type=F32
        )
        for j in range(2):
            encode(value[j * block : (j + 1) * block], out.at[2 * i + j])


def body(mode_block, k_blocks, block_cols, panel_node, added_mass, low_edge, high_edge):
    n_row = lax.axis_size("row")
    n_col = lax.axis_size("col")
    devices = n_row * n_col
    my_row = lax.axis_index("row")
    my_col = lax.axis_index("col")
    linear = my_row * n_col + my_col
    core = (my_row % 2).astype(jnp.int32).reshape(1)
    rows_dev, width = mode_block.shape
    size = k_blocks.shape[2]
    blocks_dev = rows_dev // size
    per_block = panel_node.shape[0] // devices
    slots = 2 * devices
    both = ("row", "col")

    panel_rows = panel_node.reshape(devices, per_block)
    source = panel_rows // rows_dev
    before = jnp.concatenate([jnp.full((devices, 1), -1, source.dtype), source[:, :-1]], axis=1)
    rank = (source == before).astype(jnp.int32)
    owned = source == linear
    local = panel_rows - linear * rows_dev
    first = jnp.max(jnp.where(owned & (rank == 0), local, -1), axis=1)
    second = jnp.max(jnp.where(owned & (rank == 1), local, -1), axis=1)
    by_block = jnp.stack([first, second], axis=0)
    by_target = by_block.reshape(2, n_col, 2, n_row // 2).transpose(0, 3, 2, 1)
    shell_rows = jnp.arange(rows_dev, dtype=jnp.int32)
    pick = (by_target.reshape(slots, 1) == shell_rows[None, :]).astype(BF16)
    place = (shell_rows[:, None] == by_block.reshape(1, slots)).astype(BF16)
    flat = rank * devices + source
    slot_ids = jnp.arange(slots, dtype=jnp.int32)
    in_place = my_row % 2 * (n_row // 2) + my_row // 2
    in_flat = lax.dynamic_index_in_dim(flat, my_col * n_row + in_place, 0, keepdims=False)
    out_flat = lax.dynamic_index_in_dim(flat, linear, 0, keepdims=False)
    gather_in = (in_flat[:, None] == slot_ids[None, :]).astype(BF16)
    spread_out = (slot_ids[:, None] == out_flat[None, :]).astype(BF16)

    cols = block_cols - (linear * blocks_dev - 2)
    halo = 2 * size
    n_same = n_row // 2
    same_core = [[i for i in range(n_row) if i % 2 == c] for c in range(2)]
    swap_core = [(i, i ^ 1) for i in range(n_row)]
    forward = [(i, i + 1) for i in range(devices - 1)]
    backward = [(i + 1, i) for i in range(devices - 1)]
    to_in = []
    for b in range(devices):
        core_at, chip_at = divmod(b % n_row, n_row // 2)
        to_in.append((b, (2 * chip_at + core_at) * n_col + b // n_row))

    block_f32 = jax.ShapeDtypeStruct((rows_dev, width), F32)
    wet_f32 = jax.ShapeDtypeStruct((slots, width), F32)
    eight_f32 = jax.ShapeDtypeStruct((8, width), F32)
    load_i16 = jax.ShapeDtypeStruct((per_block + PAD, width), jnp.int16)
    parts_i16 = jax.ShapeDtypeStruct((n_col, per_block + PAD, width), jnp.int16)
    edge_i16 = jax.ShapeDtypeStruct((halo + PAD, width), jnp.int16)
    sent_bf16 = jax.ShapeDtypeStruct((n_same, per_block, width), BF16)
    block_vmem = pltpu.VMEM((rows_dev, width), F32)
    padded = pltpu.VMEM((rows_dev + 2 * halo, width), BF16)
    dma = pltpu.SemaphoreType.DMA

    def stiff(low, here, high, got, previous, scale, shift, with_wet, with_square):
        fresh, with_prev = got is None, previous is not None
        args = [cols, k_blocks, low, here, high, scale, shift]
        specs = [SMEM, HBM, VMEM, HBM, VMEM, VMEM, VMEM]
        if not fresh:
            args, specs = args + [got, place], specs + [VMEM, VMEM]
        if with_prev:
            args, specs = args + [previous], specs + [HBM]
        if with_wet:
            args, specs = args + [pick], specs + [VMEM]
        shapes = [block_f32] + [wet_f32] * with_wet + [block_f32] * (not fresh) + [eight_f32] * with_square
        outs = [HBM] + [VMEM] * with_wet + [HBM] * (not fresh) + [VMEM] * with_square
        made = list(call(
            functools.partial(stiff_kernel, fresh, with_prev, with_wet, with_square), "stiff",
            shapes, specs, outs, 80 * 10**9, 8 * 2**20,
            [
                pltpu.VMEM(k_blocks.shape, F32), block_vmem, block_vmem, block_vmem, padded, padded,
                dma((blocks_dev,)), dma((rows_dev // halo,)), dma((blocks_dev,)), dma((blocks_dev,)),
                dma((rows_dev // halo,)),
            ],
            52,
        )(*args))
        dry = made.pop(0)
        wet = made.pop(0) if with_wet else None
        current = here if fresh else made.pop(0)
        return dry, wet, current, made.pop(0) if with_square else None

    def fetch(earlier):
        return call(
            fetch_kernel, "fetch", pltpu.VMEM(added_mass.shape, BF16), [ANY, HBM], VMEM,
            10 * 10**9, 4 * 2**20, [dma((4,))], 48,
        )(earlier, added_mass)

    def mass_dot(mass, same, other):
        return call(
            dot_kernel, "mass_dot", parts_i16, [SMEM, VMEM, VMEM, VMEM], VMEM,
            2 * added_mass.size * width, 6 * 2**20,
            [pltpu.VMEM((added_mass.shape[1], width), BF16)], 48,
        )(core, mass, same, other)

    def pack(parts, gain, wet, last):
        rows = 4 if last else 8
        message = jax.ShapeDtypeStruct((rows * devices, LANES), F32)
        shapes = [message] if last else [load_i16, message]
        args = [parts, gain, spread_out, wet]
        specs = [VMEM] * 4
        made = call(
            functools.partial(pack_kernel, last), "pack",
            shapes, specs, [VMEM] * len(shapes), 10**8, 3 * 2**20,
        )(*args)
        return (None, made[0]) if last else made

    def wet_rows(got, load):
        return call(wet_kernel, "wet_rows", sent_bf16, [VMEM] * 3, VMEM, 10**8, 10**6)(
            got, load, gather_in
        )

    def border(got, dry):
        return call(
            border_kernel, "border", [edge_i16, edge_i16], [VMEM, HBM, VMEM], [VMEM, VMEM],
            20 * 10**9, 2 * 2**20, [pltpu.VMEM((2, halo, width), F32), dma((2,))], 52,
        )(got, dry, place)

    def shell(got, dry):
        return call(
            shell_kernel, "shell", [block_f32, eight_f32], [VMEM, HBM, VMEM], [VMEM, VMEM],
            2 * 10**9, 4 * 2**20, [block_vmem, dma], 52,
        )(got, dry, place)

    def tie(value, other):
        return pl.pallas_call(
            tie_kernel,
            out_shape=jax.ShapeDtypeStruct(value.shape, value.dtype),
            in_specs=[ANY, ANY],
            out_specs=ANY,
            input_output_aliases={0: 0},
            compiler_params=pltpu.CompilerParams(vmem_limit_bytes=4 * 2**20),
            cost_estimate=pl.CostEstimate(flops=0, bytes_accessed=0, transcendentals=0),
            name="tie",
        )(value, other)

    def exchange(message):
        return lax.all_to_all(message, both, split_axis=0, concat_axis=0, tiled=True)

    def gathered(sent, low):
        same = lax.all_to_all(
            sent, "row", split_axis=0, concat_axis=0, tiled=True, axis_index_groups=same_core
        )
        same = tie(same, low)
        return same, lax.ppermute(same, "row", swap_core)

    lower = low_edge.astype(F32) * 0.25
    upper = high_edge.astype(F32) * 0.25
    centre = (0.5 * (upper + lower))[None, :]
    radius = (0.5 * (upper - lower))[None, :]
    total_rows = rows_dev * devices

    here = mode_block
    start_rows = jnp.dot(pick, here.astype(BF16), preferred_element_type=F32)
    start_rows = start_rows.astype(BF16).reshape(2, devices, width).transpose(1, 0, 2)
    start_rows = exchange(start_rows).transpose(1, 0, 2).reshape(slots, width)
    wetted = jnp.dot(gather_in, start_rows, preferred_element_type=F32).astype(BF16)
    sent = jnp.broadcast_to(wetted[None], (n_same,) + wetted.shape)
    head, tail = call(
        edge_kernel, "edges", [edge_i16, edge_i16], [VMEM] * 2, [VMEM] * 2, 10**6, 2**20
    )(here[:halo], here[rows_dev - halo :])
    current, got, squares = None, None, []
    for outer_no in range(OUTER):
        for degree_no in range(DEGREE):
            last = outer_no == OUTER - 1 and degree_no == DEGREE - 1
            gain = (1.0 if degree_no == 0 else 2.0) / radius
            before = None if degree_no == 0 else current
            low = lax.ppermute(tail, both, forward)
            high = lax.ppermute(head, both, backward)
            mass = fetch(start_rows if got is None else got)
            same, other = gathered(sent, low)
            partial = mass_dot(mass, same, other)
            end = outer_no > 0 and degree_no == 0
            dry, wet, current, square = stiff(
                low, here, high, got, before, gain, -centre * gain, True, end
            )
            if end:
                squares.append(square[:1])
            here = dry
            parts = lax.all_to_all(partial, "col", split_axis=0, concat_axis=0, tiled=True)
            load, message = pack(parts, gain, wet, last)
            got = exchange(message.reshape(devices, -1, LANES)).reshape(-1, LANES)
            if not last:
                sent = wet_rows(got, lax.ppermute(load, both, to_in))
                head, tail = border(got, dry)
    current, square = shell(got, dry)
    squares.append(square[:1])
    both_sums = jnp.stack(squares, axis=1)
    both_sums = exchange(jnp.broadcast_to(both_sums, (devices, OUTER, width)))
    both_sums = jnp.sum(both_sums, axis=0)
    first = both_sums[0:1] / total_rows + 1e-06
    second = both_sums[1:2] / total_rows / first * (1.0 / (SMALL * SMALL)) + 1e-06
    return current / (jnp.sqrt(first) * jnp.sqrt(second))


def solution(mesh):
    placed = (
        P(("row", "col"), None),
        P(("row", "col"), None, None, None),
        P(("row", "col"), None),
        P(),
        P("row", "col"),
        P(),
        P(),
    )
    return jax.shard_map(
        body, mesh=mesh, in_specs=placed, out_specs=P(("row", "col"), None), check_vma=False
    )
```

```python
import functools

import jax
import jax.numpy as jnp
from jax import lax
from jax.experimental import pallas as pl
from jax.experimental.pallas import tpu as pltpu
from jax.sharding import PartitionSpec as P

DEGREE = 3
OUTER = 2
F32 = jnp.float32
BF16 = jnp.bfloat16
LANES = 128
PAD = 16
STEPS = 32000.0
SMALL = 2.0**-20
VMEM = pl.BlockSpec(memory_space=pltpu.VMEM)
HBM = pl.BlockSpec(memory_space=pltpu.HBM)
ANY = pl.BlockSpec(memory_space=pl.ANY)
SMEM = pl.BlockSpec(memory_space=pltpu.SMEM)


def two_parts(value):
    hi = value.astype(BF16)
    return hi, (value - hi.astype(F32)).astype(BF16)


def choose(matrix, value):
    hi, lo = two_parts(value)
    picked = jnp.dot(matrix, hi, preferred_element_type=F32)
    return picked + jnp.dot(matrix, lo, preferred_element_type=F32)


def call(kernel, name, out_shape, in_specs, out_specs, flops, moved, scratch=(), limit=8):
    return pl.pallas_call(
        kernel,
        out_shape=out_shape,
        in_specs=in_specs,
        out_specs=out_specs,
        scratch_shapes=list(scratch),
        compiler_params=pltpu.CompilerParams(vmem_limit_bytes=limit * 2**20),
        cost_estimate=pl.CostEstimate(flops=flops, bytes_accessed=moved, transcendentals=0),
        name=name,
    )


def encode(value, out):
    rows = value.shape[0]
    top = jnp.maximum(jnp.max(jnp.abs(value), axis=0, keepdims=True), 1e-30)
    power = jnp.clip(jnp.ceil(jnp.log2(top)), -100.0, 126.0)
    steps = jnp.floor(value * (STEPS * jnp.exp2(-power)) + 0.5)
    out[0:rows, :] = steps.astype(jnp.int32).astype(jnp.int16)
    tail = jnp.broadcast_to(power, (PAD, value.shape[1]))
    out[rows : rows + PAD, :] = tail.astype(jnp.int32).astype(jnp.int16)


def decode(coded):
    rows = coded.shape[0] - PAD
    power = coded[rows : rows + PAD, :].astype(jnp.int32).astype(F32)[0:1]
    return coded[0:rows, :].astype(jnp.int32).astype(F32) * (jnp.exp2(power) * (1.0 / STEPS))


def placed(matrix, hi, lo):
    value = jnp.dot(matrix, hi, preferred_element_type=F32)
    return value + jnp.dot(matrix, lo, preferred_element_type=F32)


def border_kernel(got, dry_hbm, place, head, tail, dry, sems):
    halo = dry.shape[1]
    starts = [0, place.shape[0] - halo]
    copies = [
        pltpu.make_async_copy(dry_hbm.at[pl.ds(at, halo)], dry.at[i], sems.at[i])
        for i, at in enumerate(starts)
    ]
    for copy in copies:
        copy.start()
    loads = two_parts(slot_rows(got, place.shape[1] // 2, 0))
    for i, (at, out) in enumerate(zip(starts, (head, tail))):
        more = placed(place[at : at + halo, :], *loads)
        copies[i].wait()
        encode(dry[i] + more, out)


def edge_kernel(head, tail, head_out, tail_out):
    encode(head[...], head_out)
    encode(tail[...], tail_out)


def stiff_kernel(fresh, with_prev, with_wet, with_square, *refs):
    refs = list(refs)
    cols, k_hbm, low, here_hbm, high, scale, shift = refs[:7]
    del refs[:7]
    got, place = (None, None) if fresh else (refs.pop(0), refs.pop(0))
    prev_hbm = refs.pop(0) if with_prev else None
    pick = refs.pop(0) if with_wet else None
    out_hbm = refs.pop(0)
    wet = refs.pop(0) if with_wet else None
    made_hbm = None if fresh else refs.pop(0)
    square = refs.pop(0) if with_square else None
    k, here, prev, out, p_hi, p_lo, k_sem, here_sem, prev_sem, out_sem, made_sem = refs
    rows = here.shape[0]
    size = k.shape[2]
    halo = low.shape[0] - PAD
    count = rows // size
    chunks = [pl.ds(i * halo, halo) for i in range(rows // halo)]
    here_copies = [
        pltpu.make_async_copy(here_hbm.at[mine], here.at[mine], here_sem.at[i])
        for i, mine in enumerate(chunks)
    ]
    for copy in here_copies:
        copy.start()
    row_copies = []
    for i in range(count):
        mine = pl.ds(i * size, size)
        row_copies.append([pltpu.make_async_copy(k_hbm.at[i], k.at[i], k_sem.at[i])])
        if with_prev:
            row_copies[i].append(
                pltpu.make_async_copy(prev_hbm.at[mine], prev.at[mine], prev_sem.at[i])
            )
        for copy in row_copies[i]:
            copy.start()

    def put(value, start):
        hi, lo = two_parts(value)
        p_hi[start : start + value.shape[0], :] = hi
        p_lo[start : start + value.shape[0], :] = lo

    put(decode(low), 0)
    put(decode(high), halo + rows)
    out_copies = []
    if not fresh:
        loads = two_parts(slot_rows(got, place.shape[1] // 2, 0))
    squares = None
    for i, mine in enumerate(chunks):
        here_copies[i].wait()
        value = here[mine, :]
        if not fresh:
            value = value + placed(place[mine, :], *loads)
            here[mine, :] = value
            copy = pltpu.make_async_copy(here.at[mine], made_hbm.at[mine], made_sem.at[i])
            copy.start()
            out_copies.append(copy)
        put(value, (i + 1) * halo)
        if with_square:
            more = jnp.sum(value * value, axis=0, keepdims=True)
            squares = more if squares is None else squares + more
    if with_square:
        square[...] = jnp.broadcast_to(squares, square.shape)
    for i in range(count):
        for copy in row_copies[i]:
            copy.wait()
        at = [pl.ds(pl.multiple_of(cols[i, j] * size, size), size) for j in range(k.shape[1])]
        k_parts = [two_parts(k[i, j]) for j in range(k.shape[1])]
        k_hi = jnp.concatenate([part[0] for part in k_parts], axis=1)
        k_lo = jnp.concatenate([part[1] for part in k_parts], axis=1)
        v_hi = jnp.concatenate([p_hi[rows_at, :] for rows_at in at], axis=0)
        v_lo = jnp.concatenate([p_lo[rows_at, :] for rows_at in at], axis=0)
        pair = jnp.dot(jnp.concatenate([k_hi, k_lo], axis=0), v_hi, preferred_element_type=F32)
        acc = pair[:size] + pair[size:] + jnp.dot(k_hi, v_lo, preferred_element_type=F32)
        mine = pl.ds(i * size, size)
        value = scale[...] * acc + shift[...] * here[mine, :]
        if with_prev:
            value = value - prev[mine, :]
        out[mine, :] = value
        copy = pltpu.make_async_copy(out.at[mine], out_hbm.at[mine], out_sem.at[i])
        copy.start()
        out_copies.append(copy)
    if with_wet:
        wet[...] = choose(pick[...], out[...])
    for copy in out_copies:
        copy.wait()


def pack_kernel(last, *refs):
    refs = list(refs)
    parts, gain, spread, wet = refs[:4]
    del refs[:4]
    load = None if last else refs.pop(0)
    message = refs.pop(0)
    total = decode(parts.at[0])
    for i in range(1, parts.shape[0]):
        total = total + decode(parts.at[i])
    total = total * gain[...]
    if not last:
        encode(total, load)
    sent = choose(spread[...], total)
    devices = sent.shape[0] // 2
    rows = message.shape[0] // devices
    for h in range(2):
        piece = slice(h * LANES, (h + 1) * LANES)
        for s in range(2):
            mine = slice(s * devices, (s + 1) * devices)
            message[pl.ds((2 if last else 4) * h + s, devices, stride=rows), :] = sent[mine, piece]
            if not last:
                message[pl.ds(4 * h + 2 + s, devices, stride=rows), :] = wet[mine, piece]


def slot_rows(got, devices, first):
    rows = got.shape[0] // devices
    half = min(rows // 2, 4)

    def one(s):
        halves = [got[pl.ds(half * h + first + s, devices, stride=rows), :] for h in range(2)]
        return jnp.concatenate(halves, axis=1)

    return jnp.concatenate([one(0), one(1)], axis=0)


def wet_kernel(got, load, gather, sent):
    devices = gather.shape[1] // 2
    value = choose(gather[...], slot_rows(got, devices, 2)) + decode(load)
    value = value.astype(BF16)
    for i in range(sent.shape[0]):
        sent[i] = value


def shell_kernel(got, dry_hbm, place, out, square, dry, sem):
    copy = pltpu.make_async_copy(dry_hbm, dry, sem)
    copy.start()
    more = placed(place[...], *two_parts(slot_rows(got, place.shape[1] // 2, 0)))
    copy.wait()
    value = dry[...] + more
    out[...] = value
    scaled = value * SMALL
    square[...] = jnp.broadcast_to(jnp.sum(scaled * scaled, axis=0, keepdims=True), square.shape)


def first_kernel(gather, rows, sent):
    value = jnp.dot(gather[...], rows[...], preferred_element_type=F32).astype(BF16)
    for i in range(sent.shape[0]):
        sent[i] = value


def tie_kernel(value, other, out):
    pass


def fetch_kernel(earlier, mass_hbm, out, sems):
    chunk = mass_hbm.shape[0] // sems.shape[0]
    copies = []
    for i in range(sems.shape[0]):
        rows = pl.ds(i * chunk, chunk)
        copies.append(pltpu.make_async_copy(mass_hbm.at[rows], out.at[rows], sems.at[i]))
        copies[i].start()
    for copy in copies:
        copy.wait()


def dot_kernel(core, mass, same, other, out, panels):
    count, depth, _ = same.shape
    block = out.shape[1] - PAD
    chunk = mass.shape[0]
    for j in range(count):
        at = pl.multiple_of((2 * j + core[0]) * depth, depth)
        panels[pl.ds(at, depth), :] = same[j]
        at = pl.multiple_of((2 * j + 1 - core[0]) * depth, depth)
        panels[pl.ds(at, depth), :] = other[j]
    for i in range(1):
        value = jnp.dot(
            mass[i * chunk : (i + 1) * chunk, :], panels[...], preferred_element_type=F32
        )
        for j in range(out.shape[0]):
            encode(value[j * block : (j + 1) * block], out.at[j])


def body(mode_block, k_blocks, block_cols, panel_node, added_mass, low_edge, high_edge):
    n_row = lax.axis_size("row")
    n_col = lax.axis_size("col")
    devices = n_row * n_col
    my_row = lax.axis_index("row")
    my_col = lax.axis_index("col")
    linear = my_row * n_col + my_col
    core = (my_row % 2).astype(jnp.int32).reshape(1)
    rows_dev, width = mode_block.shape
    size = k_blocks.shape[2]
    blocks_dev = rows_dev // size
    per_block = panel_node.shape[0] // devices
    slots = 2 * devices
    both = ("row", "col")

    panel_rows = panel_node.reshape(devices, per_block)
    source = panel_rows // rows_dev
    before = jnp.concatenate([jnp.full((devices, 1), -1, source.dtype), source[:, :-1]], axis=1)
    rank = (source == before).astype(jnp.int32)
    owned = source == linear
    local = panel_rows - linear * rows_dev
    first = jnp.max(jnp.where(owned & (rank == 0), local, -1), axis=1)
    second = jnp.max(jnp.where(owned & (rank == 1), local, -1), axis=1)
    by_block = jnp.stack([first, second], axis=0)
    by_target = by_block.reshape(2, n_col, n_row).transpose(0, 2, 1)
    shell_rows = jnp.arange(rows_dev, dtype=jnp.int32)
    pick = (by_target.reshape(slots, 1) == shell_rows[None, :]).astype(BF16)
    place = (shell_rows[:, None] == by_block.reshape(1, slots)).astype(BF16)
    flat = rank * devices + source
    slot_ids = jnp.arange(slots, dtype=jnp.int32)
    in_flat = lax.dynamic_index_in_dim(flat, my_col * n_row + my_row, 0, keepdims=False)
    out_flat = lax.dynamic_index_in_dim(flat, linear, 0, keepdims=False)
    gather_in = (in_flat[:, None] == slot_ids[None, :]).astype(BF16)
    spread_out = (slot_ids[:, None] == out_flat[None, :]).astype(BF16)

    cols = block_cols - (linear * blocks_dev - 2)
    halo = 2 * size
    n_same = n_row // 2
    same_core = [[i for i in range(n_row) if i % 2 == c] for c in range(2)]
    swap_core = [(i, i ^ 1) for i in range(n_row)]
    forward = [(i, i + 1) for i in range(devices - 1)]
    backward = [(i + 1, i) for i in range(devices - 1)]
    to_in = [(b, (b % n_row) * n_col + b // n_row) for b in range(devices)]

    block_f32 = jax.ShapeDtypeStruct((rows_dev, width), F32)
    wet_f32 = jax.ShapeDtypeStruct((slots, width), F32)
    eight_f32 = jax.ShapeDtypeStruct((8, width), F32)
    load_i16 = jax.ShapeDtypeStruct((per_block + PAD, width), jnp.int16)
    parts_i16 = jax.ShapeDtypeStruct((n_col, per_block + PAD, width), jnp.int16)
    edge_i16 = jax.ShapeDtypeStruct((halo + PAD, width), jnp.int16)
    sent_bf16 = jax.ShapeDtypeStruct((n_same, per_block, width), BF16)
    block_vmem = pltpu.VMEM((rows_dev, width), F32)
    padded = pltpu.VMEM((rows_dev + 2 * halo, width), BF16)
    dma = pltpu.SemaphoreType.DMA

    def stiff(low, here, high, got, previous, scale, shift, with_wet, with_square):
        fresh, with_prev = got is None, previous is not None
        args = [cols, k_blocks, low, here, high, scale, shift]
        specs = [SMEM, HBM, VMEM, HBM, VMEM, VMEM, VMEM]
        if not fresh:
            args, specs = args + [got, place], specs + [VMEM, VMEM]
        if with_prev:
            args, specs = args + [previous], specs + [HBM]
        if with_wet:
            args, specs = args + [pick], specs + [VMEM]
        shapes = [block_f32] + [wet_f32] * with_wet + [block_f32] * (not fresh) + [eight_f32] * with_square
        outs = [HBM] + [VMEM] * with_wet + [HBM] * (not fresh) + [VMEM] * with_square
        made = list(call(
            functools.partial(stiff_kernel, fresh, with_prev, with_wet, with_square), "stiff",
            shapes, specs, outs, 80 * 10**9, 8 * 2**20,
            [
                pltpu.VMEM(k_blocks.shape, F32), block_vmem, block_vmem, block_vmem, padded, padded,
                dma((blocks_dev,)), dma((rows_dev // halo,)), dma((blocks_dev,)), dma((blocks_dev,)),
                dma((rows_dev // halo,)),
            ],
            52,
        )(*args))
        dry = made.pop(0)
        wet = made.pop(0) if with_wet else None
        current = here if fresh else made.pop(0)
        return dry, wet, current, made.pop(0) if with_square else None

    def fetch(earlier):
        return call(
            fetch_kernel, "fetch", pltpu.VMEM(added_mass.shape, BF16), [ANY, HBM], VMEM,
            10 * 10**9, 4 * 2**20, [dma((4,))], 48,
        )(earlier, added_mass)

    def mass_dot(mass, same, other):
        return call(
            dot_kernel, "mass_dot", parts_i16, [SMEM, VMEM, VMEM, VMEM], VMEM,
            2 * added_mass.size * width, 6 * 2**20,
            [pltpu.VMEM((added_mass.shape[1], width), BF16)], 48,
        )(core, mass, same, other)

    def pack(parts, gain, wet, last):
        rows = 4 if last else 8
        message = jax.ShapeDtypeStruct((rows * devices, LANES), F32)
        shapes = [message] if last else [load_i16, message]
        args = [parts, gain, spread_out, wet]
        specs = [VMEM] * 4
        made = call(
            functools.partial(pack_kernel, last), "pack",
            shapes, specs, [VMEM] * len(shapes), 10**8, 3 * 2**20,
        )(*args)
        return (None, made[0]) if last else made

    def wet_rows(got, load):
        return call(wet_kernel, "wet_rows", sent_bf16, [VMEM] * 3, VMEM, 10**8, 10**6)(
            got, load, gather_in
        )

    def border(got, dry):
        return call(
            border_kernel, "border", [edge_i16, edge_i16], [VMEM, HBM, VMEM], [VMEM, VMEM],
            20 * 10**9, 2 * 2**20, [pltpu.VMEM((2, halo, width), F32), dma((2,))], 52,
        )(got, dry, place)

    def shell(got, dry):
        return call(
            shell_kernel, "shell", [block_f32, eight_f32], [VMEM, HBM, VMEM], [VMEM, VMEM],
            2 * 10**9, 4 * 2**20, [block_vmem, dma], 52,
        )(got, dry, place)

    def tie(value, other):
        return pl.pallas_call(
            tie_kernel,
            out_shape=jax.ShapeDtypeStruct(value.shape, value.dtype),
            in_specs=[ANY, ANY],
            out_specs=ANY,
            input_output_aliases={0: 0},
            compiler_params=pltpu.CompilerParams(vmem_limit_bytes=4 * 2**20),
            cost_estimate=pl.CostEstimate(flops=0, bytes_accessed=0, transcendentals=0),
            name="tie",
        )(value, other)

    def exchange(message):
        return lax.all_to_all(message, both, split_axis=0, concat_axis=0, tiled=True)

    def gathered(sent, low):
        same = lax.all_to_all(
            sent, "row", split_axis=0, concat_axis=0, tiled=True, axis_index_groups=same_core
        )
        same = tie(same, low)
        return same, lax.ppermute(same, "row", swap_core)

    lower = low_edge.astype(F32) * 0.25
    upper = high_edge.astype(F32) * 0.25
    centre = (0.5 * (upper + lower))[None, :]
    radius = (0.5 * (upper - lower))[None, :]
    total_rows = rows_dev * devices

    here = mode_block
    start_rows = jnp.dot(pick, here.astype(BF16), preferred_element_type=F32)
    start_rows = start_rows.astype(BF16).reshape(2, devices, width).transpose(1, 0, 2)
    start_rows = exchange(start_rows).transpose(1, 0, 2).reshape(slots, width)
    sent = call(first_kernel, "first", sent_bf16, [VMEM] * 2, VMEM, 10**8, 10**6)(gather_in, start_rows)
    head, tail = call(
        edge_kernel, "edges", [edge_i16, edge_i16], [VMEM] * 2, [VMEM] * 2, 10**6, 2**20
    )(here[:halo], here[rows_dev - halo :])
    current, got, squares = None, None, []
    for outer_no in range(OUTER):
        for degree_no in range(DEGREE):
            last = outer_no == OUTER - 1 and degree_no == DEGREE - 1
            gain = (1.0 if degree_no == 0 else 2.0) / radius
            before = None if degree_no == 0 else current
            low = lax.ppermute(tail, both, forward)
            high = lax.ppermute(head, both, backward)
            mass = fetch(start_rows if got is None else got)
            same, other = gathered(sent, low)
            partial = mass_dot(mass, same, other)
            end = outer_no > 0 and degree_no == 0
            dry, wet, current, square = stiff(
                low, here, high, got, before, gain, -centre * gain, True, end
            )
            if end:
                squares.append(square[:1])
            here = dry
            parts = lax.all_to_all(partial, "col", split_axis=0, concat_axis=0, tiled=True)
            load, message = pack(parts, gain, wet, last)
            got = exchange(message.reshape(devices, -1, LANES)).reshape(-1, LANES)
            if not last:
                sent = wet_rows(got, lax.ppermute(load, both, to_in))
                head, tail = border(got, dry)
    current, square = shell(got, dry)
    squares.append(square[:1])
    both_sums = jnp.stack(squares, axis=1)
    both_sums = exchange(jnp.broadcast_to(both_sums, (devices, OUTER, width)))
    both_sums = jnp.sum(both_sums, axis=0)
    first = both_sums[0:1] / total_rows + 1e-06
    second = both_sums[1:2] / total_rows / first * (1.0 / (SMALL * SMALL)) + 1e-06
    return current / (jnp.sqrt(first) * jnp.sqrt(second))


def solution(mesh):
    placed = (
        P(("row", "col"), None),
        P(("row", "col"), None, None, None),
        P(("row", "col"), None),
        P(),
        P("row", "col"),
        P(),
        P(),
    )
    return jax.shard_map(
        body, mesh=mesh, in_specs=placed, out_specs=P(("row", "col"), None), check_vma=False
    )
```
